128 devices in a mesh: lon: 8 (over z, x_lo), lat: 16 (over x_hi, y, core).
Axes of the slice: x: 4 (x_hi: 2, x_lo: 2; x = x_hi * 2 + x_lo), y: 4, z: 4, core: 2. Of those that a mesh axis runs over, the one named last changes fastest.
Arguments:
- flux_probes: float32 [192, 288, 64], P('lat', 'lon'), may hold values from -6 to 6
- conc_start: float32 [192, 288, 47, 64], P('lat', 'lon'), may hold values from -6 to 6
- u_courant: float32 [192, 288, 47], P('lat', 'lon'), may hold values from -0.45 to 0.45
- v_courant: float32 [192, 288, 47], P('lat', 'lon'), may hold values from -0.45 to 0.45
- vert_mix: float32 [192, 288, 47], P('lat', 'lon'), may hold values from 0.02 to 0.24
- obs_cell: int32 [131072], P(('lon', 'lat')), may hold values from 0 to 20303
- obs_weight: float32 [131072], P(('lon', 'lat')), may hold values from 0.3 to 3
- obs_count: int32 [128], P(('lon', 'lat')), may hold values from 341 to 1024, as said below
Outputs:
- basis: float32 [131072, 64], P(('lon', 'lat'))
- factor: float32 [64, 64], replicated
The draws below stay inside these ranges and needn't reach their ends.
Inputs may be any that keep to these rules, and one draw needn't show every extreme that they name: `obs_count`: each device's number of live slots; some device has exactly 1024.
All inputs are finite; a program needn't handle non-finite values.
Results may differ from the reference program's by a relative error of at most 0.0003.
Values sent between devices are 32-bit elements; how exact they have to be, the bound alone decides.
No kernel may reach another device: no remote copies, remote signals or barrier semaphores. Data moves between devices by JAX's collectives and lax.ppermute only.
A program may use at most 192 MiB of HBM per device.

```python
import math
import jax
import jax.numpy as jnp
from jax import lax

LEV = 47
PROBES = 64
STEPS = 4
LAT_DEV = 12
LON_DEV = 36
OBS_DEV = 1024
NLAT = 192
NLON = 288
OBS_ROWS = 131072
N_LAT = 16
DEVICES = 128


def draw_obs_count(key, part):
    key = jax.random.fold_in(key, 5)
    key_counts, key_full = jax.random.split(key)
    counts = jax.random.randint(key_counts, (DEVICES,), OBS_DEV // 3, OBS_DEV + 1)
    chosen = jax.random.randint(key_full, (), 0, DEVICES)
    places = jnp.arange(DEVICES, dtype=jnp.int32)
    return jnp.where(places == chosen, OBS_DEV, counts).astype(jnp.int32)


def courant_field(key, sign_shape, smallest):
    sign_key, magnitude_key = jax.random.split(key)
    sign_bits = jax.random.randint(sign_key, sign_shape, 0, 2)
    sign_field = (2 * sign_bits - 1).astype(jnp.float32)
    magnitude = jax.random.uniform(magnitude_key, (NLAT, NLON, LEV), jnp.float32, smallest, 0.45)
    return (sign_field * magnitude).astype(jnp.float32)


def draw_u_courant(key, part):
    key = jax.random.fold_in(key, 7)
    smallest = 0.2
    return courant_field(key, (NLAT, 1, LEV), smallest)


def draw_v_courant(key, part):
    key = jax.random.fold_in(key, 11)
    smallest = 0.2
    return courant_field(key, (1, NLON, LEV), smallest)


def place_ends(entries, stream_key, low, top_value):
    index_at = [jax.random.randint(jax.random.fold_in(stream_key, axis), (), 0, length) for axis, length in enumerate(entries.shape)]
    main_axis = entries.shape.index(max(entries.shape))
    next_to = index_at[:main_axis] + [(index_at[main_axis] + 1) % entries.shape[main_axis]] + index_at[main_axis + 1:]
    return entries.at[tuple(index_at)].set(low).at[tuple(next_to)].set(top_value)


def block_scale(key, dims, cuts, low, high):
    def one(axis_at, blocks):
        heights = jax.random.uniform(jax.random.fold_in(jax.random.fold_in(key, 6), axis_at), (blocks,), jnp.float32, low / len(cuts), high / len(cuts))
        return jnp.repeat(jnp.exp(heights), dims[axis_at] // blocks).reshape((-1,) + (1,) * (len(dims) - axis_at - 1))

    factor_of = one(*cuts[0])
    for cut in cuts[1:]:
        factor_of = factor_of * one(*cut)
    return factor_of


def normal_values(own_key, extent, width, bound, pieces=(), kind=jnp.bfloat16):
    drawn = jax.random.normal(own_key, extent, jnp.float32) * width
    if len(pieces) > 0:
        drawn = block_scale(own_key, extent, pieces, -0.22, 0.18) * drawn
    return jnp.clip(drawn, min=-bound, max=bound).astype(kind)


def setup_inputs(seed: int = 0) -> dict:
    splits = jax.random.split(jax.random.key(seed), 9)
    flux_probes = normal_values(splits[0], (NLAT, NLON, PROBES), 1.0, 6.0, ((0, 16), (1, 8)), jnp.float32)
    conc_start = normal_values(splits[1], (NLAT, NLON, LEV, PROBES), 1.0, 6.0, ((0, 16), (1, 8)), jnp.float32)
    u_courant = draw_u_courant(jax.random.fold_in(splits[8], 71), 0)
    v_courant = draw_v_courant(jax.random.fold_in(splits[8], 71), 0)
    vert_mix = jnp.clip(jnp.exp(math.log(0.24) - 2.4849066 * jax.random.uniform(splits[4], (NLAT, NLON, LEV), jnp.float32) ** block_scale(splits[4], (NLAT, NLON, LEV), ((0, 16), (1, 8)), -0.2, 0.2)), 0.02, 0.24)
    obs_cell = place_ends(jax.random.randint(splits[5], (OBS_ROWS,), 0, LAT_DEV * LON_DEV * LEV), jax.random.fold_in(splits[5], 1), 0, (LAT_DEV * LON_DEV * LEV) - 1).astype(jnp.int32)
    obs_weight = jnp.clip(jnp.exp(math.log(3.0) - 2.3025851 * jax.random.uniform(splits[6], (OBS_ROWS,), jnp.float32) ** block_scale(splits[6], (OBS_ROWS,), ((0, 128),), -0.2, 0.2)), 0.3, 3.0)
    obs_count = draw_obs_count(jax.random.fold_in(splits[8], 71), 0)
    return {"flux_probes": flux_probes, "conc_start": conc_start, "u_courant": u_courant, "v_courant": v_courant, "vert_mix": vert_mix, "obs_cell": obs_cell, "obs_weight": obs_weight, "obs_count": obs_count}


def advance(conc, u_face, v_face, mixing):
    west = jnp.roll(conc, 1, axis=1)
    east = jnp.roll(conc, -1, axis=1)
    u_east = jnp.roll(u_face, -1, axis=1)
    zero_row = jnp.zeros_like(conc[:1])
    south = jnp.concatenate([zero_row, conc[:-1]], axis=0)
    north = jnp.concatenate([conc[1:], zero_row], axis=0)
    v_north = jnp.concatenate([v_face[1:], jnp.zeros_like(v_face[:1])], axis=0)
    flux_w = jnp.maximum(u_face, 0.0) * west + jnp.minimum(u_face, 0.0) * conc
    flux_e = jnp.maximum(u_east, 0.0) * conc + jnp.minimum(u_east, 0.0) * east
    flux_s = jnp.maximum(v_face, 0.0) * south + jnp.minimum(v_face, 0.0) * conc
    flux_n = jnp.maximum(v_north, 0.0) * conc + jnp.minimum(v_north, 0.0) * north
    advected = conc + flux_w - flux_e + flux_s - flux_n
    mixed = mixing[:, :, :-1] * (advected[:, :, 1:] - advected[:, :, :-1])
    zero_lev = jnp.zeros_like(mixed[:, :, :1])
    return advected + jnp.concatenate([mixed, zero_lev], axis=2) - jnp.concatenate([zero_lev, mixed], axis=2)

def reference(flux_probes, conc_start, u_courant, v_courant, vert_mix, obs_cell, obs_weight, obs_count):
    block = min(16, PROBES)
    nblocks = PROBES // block
    u_face = u_courant[:, :, :, None]
    v_face = v_courant[:, :, :, None]
    mixing = vert_mix[:, :, :, None]
    rows = jnp.arange(OBS_ROWS, dtype=jnp.int32)
    device = rows // OBS_DEV
    lon_dev = device // N_LAT
    lat_dev = device % N_LAT
    level = obs_cell % LEV
    rest = obs_cell // LEV
    glon = lon_dev * LON_DEV + rest % LON_DEV
    glat = lat_dev * LAT_DEV + rest // LON_DEV
    flat_index = ((glat * NLON + glon) * LEV + level).astype(jnp.int32)
    live = rows % OBS_DEV < obs_count[device]
    scale = jnp.where(live, obs_weight, 0.0).astype(jnp.float32)

    def one_block(which):
        start = (which * block).astype(jnp.int32)
        fluxes = lax.dynamic_slice_in_dim(flux_probes, start, block, 2)
        conc = lax.dynamic_slice_in_dim(conc_start, start, block, 3)
        for step in range(STEPS):
            conc = conc.at[:, :, 0, :].add(fluxes)
            conc = advance(conc, u_face, v_face, mixing)
        flat = conc.reshape(NLAT * NLON * LEV, block)
        return jnp.take(flat, flat_index, axis=0) * scale[:, None]
    images = jnp.moveaxis(lax.map(one_block, jnp.arange(nblocks, dtype=jnp.int32)), 0, 1).reshape(OBS_ROWS, PROBES)
    gram = jnp.dot(images.T.astype(jnp.float32), images.astype(jnp.float32), precision=lax.Precision.HIGHEST, preferred_element_type=jnp.float32)
    upper = jnp.linalg.cholesky(gram).T
    basis_t = jax.scipy.linalg.solve_triangular(upper, images.T, trans='T', lower=False)
    root = jnp.sqrt(jnp.float32(OBS_ROWS))
    return (basis_t.T * root, upper / root)
```

```python
import jax
import jax.numpy as jnp
from jax import lax
from jax.experimental import pallas as pl
from jax.experimental.pallas import tpu as pltpu
from jax.sharding import PartitionSpec as P

STEPS = 4
BANDS, COLS, LEVS, PROBES = 12, 36, 47, 64
HALO = STEPS
TALL = BANDS + 2 * HALO
WIDE = COLS + 2 * HALO
LEVP = 48
HALF = COLS // 2
PAIRS = HALF + 2 * HALO
SLOTS = 1024
FIELD_ROWS = TALL * HALF * LEVP
ZERO_ROW = 2 * FIELD_ROWS
F32 = jnp.float32
HIGHEST = lax.Precision.HIGHEST
VMEM_BYTES = 62 * 1024 * 1024


def params():
    return pltpu.CompilerParams(vmem_limit_bytes=VMEM_BYTES)


def whole(space=pltpu.VMEM):
    return pl.BlockSpec(memory_space=space)


def along(x, axis, step, wrap):
    size = lax.axis_size(axis)
    pairs = [(i, (i + step) % size) for i in range(size) if wrap or 0 <= i + step < size]
    return lax.ppermute(x, axis, pairs)


def all_sum(x):
    for axis, bits in (("lat", (1,)), ("lat", (2, 4)), ("lon", (2, 4)), ("lon", (1,)), ("lat", (8,))):
        size = lax.axis_size(axis)
        masks = [bits[0]] if len(bits) == 1 else [bits[0], bits[1], bits[0] | bits[1]]
        terms = [lax.ppermute(x, axis, [(i, i ^ mask) for i in range(size)]) for mask in masks]
        for term in terms:
            x = x + term
    return x


def edges_kernel(west, east, flux_west, flux_east, to_west, to_east):
    half = BANDS // 2
    for band in range(half):
        for col in range(HALO):
            for src, flux, dst in ((west, flux_west, to_west), (east, flux_east, to_east)):
                dst[band, col, 0:LEVS, 0:PROBES] = src[band, col]
                dst[band, col, 0:LEVS, PROBES:] = src[band + half, col]
                dst[band, col, LEVS:LEVP, 0:PROBES] = flux[band, col : col + 1]
                dst[band, col, LEVS:LEVP, PROBES:] = flux[band + half, col : col + 1]


def pack_edges(conc, flux):
    last = COLS // HALO - 1
    field = lambda at: pl.BlockSpec((BANDS, HALO, LEVS, PROBES), lambda i: (0, at, 0, 0))
    out = jax.ShapeDtypeStruct((BANDS // 2, HALO, LEVP, 2 * PROBES), F32)
    spec = pl.BlockSpec(out.shape, lambda i: (0, 0, 0, 0))
    return pl.pallas_call(
        edges_kernel,
        grid=(1,),
        in_specs=[field(0), field(last), whole(), whole()],
        out_specs=[spec, spec],
        out_shape=[out, out],
        compiler_params=params(),
        name="pack_edges",
    )(conc, conc, flux[:, :HALO], flux[:, -HALO:])


def split_terms(x):
    doubled = x + pltpu.roll(x, 64, 1)
    high = doubled.astype(jnp.bfloat16).astype(F32)
    lane = lax.broadcasted_iota(jnp.int32, x.shape, 1)
    return jnp.where(lane < 64, high, doubled - high).astype(jnp.bfloat16)


def spread(split_ref, refs, tile, source, sign=None):
    shape = (128, 256)
    row = lax.broadcasted_iota(jnp.int32, shape, 0) & 63
    col = lax.broadcasted_iota(jnp.int32, shape, 1)
    pair = 2 * tile + (col >> 7)
    upper = ((col >> 6) & 1) == 1
    for which, ref in enumerate(refs):
        low, high, high_sign = source(which, pair)
        weight = jnp.where(upper, high_sign, 1.0)
        chosen = jnp.where(row == jnp.where(upper, high, low), weight, 0.0).astype(jnp.bfloat16)
        out = jnp.dot(split_ref[which], chosen, preferred_element_type=F32)
        out = out.reshape(TALL, 1, LEVP, 256)
        ref[:, pl.ds(2 * tile, 1)] = out[..., :128]
        ref[:, pl.ds(2 * tile + 1, 1)] = out[..., 128:]


def face_flux(speed, behind, ahead):
    return speed * jnp.where(speed > 0.0, behind, ahead)


def mix_levels(advected, mixing):
    moved = mixing * (pltpu.roll(advected, LEVP - 1, 0) - advected)
    return advected + moved - pltpu.roll(moved, 1, 0)


def transport_kernel(conc, flux, coef, out, c, u, v, m, fs, split, stage, in_sem, out_sem):
    def fetch(band, slot):
        return pltpu.make_async_copy(conc.at[band], stage.at[slot], in_sem.at[slot])

    fetch(0, 0).start()
    fetch(1, 1).start()
    for which in range(3):
        split[which] = split_terms(coef[which].reshape(TALL * LEVP, 128))

    def expand(tile, carry):
        spread(split, (u, v, m), tile, lambda which, pair: (pair, pair + HALF, 1.0))
        return carry

    lax.fori_loop(0, PAIRS // 2, expand, 0)

    def clear(band, carry):
        c[band] = jnp.zeros((PAIRS, LEVP, 128), F32)
        return carry

    lax.fori_loop(0, TALL, clear, 0)

    def load(band, carry):
        slot = lax.rem(band, 2)
        fetch(band, slot).wait()
        for pair in range(PAIRS):
            low, high = pair - HALO, pair - HALO + HALF
            if low >= 0:
                c[band + HALO, pair, 0:LEVS, 0:PROBES] = stage[slot, low]
            if high < COLS:
                c[band + HALO, pair, 0:LEVS, PROBES:] = stage[slot, high]

        @pl.when(band + 2 < BANDS)
        def _():
            fetch(band + 2, slot).start()

        return carry

    lax.fori_loop(0, BANDS, load, 0)

    def save(band):
        return pltpu.make_async_copy(c.at[band, pl.ds(HALO, HALF)], out.at[band], out_sem.at[band])

    for step in range(1, STEPS + 1):
        first, last = step, PAIRS - step
        chunk = {24: 6, 22: 11, 20: 5, 18: 6}[last - first]

        def gain(band, carry):
            for pair in range(PAIRS):
                c[band + HALO, pair, 0:1] = c[band + HALO, pair, 0:1] + flux[band, pair : pair + 1]
            return carry

        lax.fori_loop(0, BANDS, gain, 0)
        fs[first:last] = jnp.zeros((last - first, LEVP, 128), F32)

        def row(band, carry):
            north = jnp.minimum(band + 1, TALL - 1)
            here = c[band, first]
            west = face_flux(u[band, first], c[band, first - 1], here)

            def some(at, state):
                here, west = state
                for k in range(chunk):
                    pair = first + at * chunk + k
                    ahead = c[band, pair + 1]
                    east = face_flux(u[band, pair + 1], here, ahead)
                    top = face_flux(v[north, pair], here, c[north, pair])
                    advected = here + (west - east) + (fs[pair] - top)
                    fs[pair] = top
                    c[band, pair] = mix_levels(advected, m[band, pair])
                    here, west = ahead, east
                return here, west

            lax.fori_loop(0, (last - first) // chunk, some, (here, west))
            if step == STEPS:
                save(band).start()
            return carry

        lax.fori_loop(HALO - step, TALL - HALO + step, row, 0)

    def drain(band, carry):
        save(band).wait()
        return carry

    lax.fori_loop(0, TALL, drain, 0)


def transport(conc, flux, coef):
    field = pltpu.VMEM((TALL, PAIRS, LEVP, 128), F32)
    return pl.pallas_call(
        transport_kernel,
        in_specs=[whole(pl.ANY), whole(), whole()],
        out_specs=whole(pl.ANY),
        out_shape=jax.ShapeDtypeStruct((TALL, HALF, LEVP, 128), F32),
        scratch_shapes=[
            field,
            field,
            field,
            field,
            pltpu.VMEM((PAIRS, LEVP, 128), F32),
            pltpu.VMEM((3, TALL * LEVP, 128), jnp.bfloat16),
            pltpu.VMEM((2, COLS, LEVS, PROBES), F32),
            pltpu.SemaphoreType.DMA((2,)),
            pltpu.SemaphoreType.DMA((TALL,)),
        ],
        compiler_params=params(),
        name="transport",
    )(conc, flux, coef)


def strips_kernel(index, west, east, coef, field, out, c, u, v, m, fs, gain, split, full, sem):
    fetch = pltpu.make_async_copy(field, full.at[pl.ds(0, FIELD_ROWS)], sem)
    fetch.start()
    for which in range(3):
        split[which] = split_terms(coef[which].reshape(TALL * LEVP, 128))

    def source(which, pair):
        if which == 0:
            return pair, WIDE - pair, -1.0
        return pair, WIDE - 1 - pair, 1.0

    def expand(tile, carry):
        spread(split, (u, v, m), tile, source)
        return carry

    lax.fori_loop(0, HALO, expand, 0)

    def clear(band, carry):
        c[band] = jnp.zeros((2 * HALO, LEVP, 128), F32)
        return carry

    lax.fori_loop(0, TALL, clear, 0)
    lane = lax.broadcasted_iota(jnp.int32, (LEVP, 128), 1)
    lower = lane < PROBES
    inside = lax.broadcasted_iota(jnp.int32, (LEVP, 128), 0) < LEVS

    def place(band, carry):
        for k in range(HALO):
            left, right = west[band, k], east[band, HALO - 1 - k]
            for at, value in (
                (band, jnp.where(lower, left, pltpu.roll(right, PROBES, 1))),
                (band + BANDS // 2, jnp.where(lower, pltpu.roll(left, PROBES, 1), right)),
            ):
                c[at + HALO, k] = jnp.where(inside, value, 0.0)
                gain[at, k, 0:1] = value[LEVS:LEVP]
        return carry

    lax.fori_loop(0, BANDS // 2, place, 0)

    for step in range(1, STEPS + 1):
        region = range(step, step + HALO)

        def add(band, carry):
            for k in range(step - 1, HALO):
                c[band + HALO, k, 0:1] = c[band + HALO, k, 0:1] + gain[band, k, 0:1]
            return carry

        lax.fori_loop(0, BANDS, add, 0)
        for k in region:
            fs[k] = jnp.zeros((LEVP, 128), F32)

        def row(band, carry):
            north = jnp.minimum(band + 1, TALL - 1)
            here = c[band, step]
            behind = face_flux(u[band, step], c[band, step - 1], here)
            for k in region:
                if k < step + HALO - 1:
                    ahead = c[band, k + 1]
                    front = face_flux(u[band, k + 1], here, ahead)
                    net = behind - front
                else:
                    net = behind
                top = face_flux(v[north, k], here, c[north, k])
                advected = here + net + (fs[k] - top)
                fs[k] = top
                c[band, k] = mix_levels(advected, m[band, k])
                here, behind = ahead, front
            return carry

        lax.fori_loop(HALO - step, TALL - HALO + step, row, 0)

    fetch.wait()

    def merge(band, carry):
        base = band * (HALF * LEVP)
        for k in range(HALO):
            share = c[band, HALO + k]
            for pair, keep in ((k, lower), (HALF - 1 - k, ~lower)):
                rows = pl.ds(pl.multiple_of(base + pair * LEVP, LEVP), LEVP)
                full[rows] = full[rows] + jnp.where(keep, share, 0.0)
        for pair in range(HALF):
            at = pl.multiple_of(base + pair * LEVP, LEVP)
            full[pl.ds(FIELD_ROWS + at, LEVP)] = pltpu.roll(full[pl.ds(at, LEVP)], PROBES, 1)
        return carry

    lax.fori_loop(0, TALL, merge, 0)
    full[ZERO_ROW : ZERO_ROW + 8] = jnp.zeros((8, 128), F32)

    half = SLOTS // 2
    low_lanes = lax.broadcasted_iota(jnp.int32, (1, 128), 1) < PROBES
    unroll = 16
    for group in range(3):

        def pick(at, carry):
            for k in range(unroll):
                slot = at * unroll + k
                one = full[pl.ds(index[group, slot], 1)]
                two = full[pl.ds(index[group, slot + half], 1)]
                out[group, pl.ds(slot, 1)] = jnp.where(low_lanes, one, two)
            return carry

        lax.fori_loop(0, half // unroll, pick, 0)


def strips(index, west, east, coef, field):
    strip = pltpu.VMEM((TALL, 2 * HALO, LEVP, 128), F32)
    return pl.pallas_call(
        strips_kernel,
        in_specs=[whole(pltpu.SMEM), whole(), whole(), whole(), whole(pl.ANY)],
        out_specs=whole(),
        out_shape=jax.ShapeDtypeStruct((3, SLOTS // 2, 128), F32),
        scratch_shapes=[
            strip,
            strip,
            strip,
            strip,
            pltpu.VMEM((2 * HALO, LEVP, 128), F32),
            pltpu.VMEM((BANDS, HALO, 8, 128), F32),
            pltpu.VMEM((3, TALL * LEVP, 128), jnp.bfloat16),
            pltpu.VMEM((ZERO_ROW + 8, 128), F32),
            pltpu.SemaphoreType.DMA,
        ],
        compiler_params=params(),
        name="strips",
    )(index, west, east, coef, field)


def row_index(cells, shift, wanted):
    level = cells % LEVS
    rest = cells // LEVS
    col = rest % COLS
    band = rest // COLS + HALO + shift
    held = (band >= 0) & (band < TALL)
    upper = (col >= HALF).astype(jnp.int32)
    row = (band * HALF + col - HALF * upper) * LEVP + level + FIELD_ROWS * (upper ^ wanted)
    return jnp.where(held, row, ZERO_ROW)


def gram_kernel(own, from_south, from_north, weight, images, gram):
    rows = (own[...] + from_south[...] + from_north[...]) * weight[...]
    images[...] = rows
    both = lax.dot_general(
        rows, rows, (((0,), (0,)), ((), ())), precision=HIGHEST, preferred_element_type=F32
    )
    total = both[:PROBES, :PROBES] + both[PROBES:, PROBES:]
    gram[:, 0:PROBES] = total[: PROBES // 2]
    gram[:, PROBES:] = total[PROBES // 2 :]


def gram_of(own, from_south, from_north, weight):
    return pl.pallas_call(
        gram_kernel,
        in_specs=[whole()] * 4,
        out_specs=[whole()] * 2,
        out_shape=[
            jax.ShapeDtypeStruct((SLOTS // 2, 128), F32),
            jax.ShapeDtypeStruct((PROBES // 2, 128), F32),
        ],
        compiler_params=params(),
        name="gram",
    )(own, from_south, from_north, weight)


def factor_kernel(root, gram, images, basis_t, factor, work):
    half = PROBES // 2
    work[0:half, 0:PROBES] = gram[:, 0:PROBES]
    work[half:, 0:PROBES] = gram[:, PROBES:]
    diagonal = (
        lax.broadcasted_iota(jnp.int32, (PROBES, PROBES), 0)
        == lax.broadcasted_iota(jnp.int32, (PROBES, PROBES), 1)
    )
    work[:, PROBES:] = diagonal.astype(F32)
    state = work[...]
    below = lax.broadcasted_iota(jnp.int32, (PROBES, 128), 0)
    done = []
    for k in range(PROBES):
        column = jnp.broadcast_to(state[:, k : k + 1], (PROBES, 128))
        scale = 1.0 / jnp.sqrt(column[k : k + 1])
        pivot = state[k : k + 1] * scale
        work[k : k + 1] = pivot
        state = state - jnp.where(below > k, column * scale, 0.0) * pivot
    both = work[...]
    row = lax.broadcasted_iota(jnp.int32, (PROBES, PROBES), 0)
    col = lax.broadcasted_iota(jnp.int32, (PROBES, PROBES), 1)
    factor[...] = jnp.where(col >= row, both[:, :PROBES], 0.0) * (1.0 / root)
    inverse_t = jnp.where(col <= row, both[:, PROBES:], 0.0) * root
    zero = jnp.zeros((PROBES, PROBES), F32)
    twice = jnp.concatenate(
        [
            jnp.concatenate([inverse_t, zero], axis=1),
            jnp.concatenate([zero, inverse_t], axis=1),
        ],
        axis=0,
    )
    basis = lax.dot_general(
        twice, images[...], (((1,), (1,)), ((), ())), precision=HIGHEST, preferred_element_type=F32
    )
    basis_t[:, 0 : SLOTS // 2] = basis[:PROBES]
    basis_t[:, SLOTS // 2 :] = basis[PROBES:]


def factor_of(gram, images, root):
    return pl.pallas_call(
        lambda *refs: factor_kernel(root, *refs),
        in_specs=[whole()] * 2,
        out_specs=[whole()] * 2,
        out_shape=[
            jax.ShapeDtypeStruct((PROBES, SLOTS), F32),
            jax.ShapeDtypeStruct((PROBES, PROBES), F32),
        ],
        scratch_shapes=[pltpu.VMEM((PROBES, 128), F32)],
        compiler_params=params(),
        name="factor",
    )(gram, images)


def on_device(
    flux_probes, conc_start, u_courant, v_courant, vert_mix, obs_cell, obs_weight, obs_count
):
    coef = jnp.stack([u_courant, v_courant, vert_mix.at[:, :, LEVS - 1].set(0.0)])
    from_south = along(coef[:, -HALO:], "lat", 1, False)
    from_north = along(coef[:, :HALO], "lat", -1, False)
    to_west, to_east = pack_edges(conc_start, flux_probes)
    west_field = along(to_east, "lon", 1, True)
    east_field = along(to_west, "lon", -1, True)
    north_cells = along(obs_cell, "lat", -1, False)
    south_cells = along(obs_cell, "lat", 1, False)
    tall = jnp.concatenate([from_south, coef, from_north], axis=1)
    from_west = along(tall[:, :, -HALO:], "lon", 1, True)
    from_east = along(tall[:, :, :HALO], "lon", -1, True)
    wide = jnp.concatenate([from_west, tall, from_east], axis=2)
    wide = jnp.pad(wide.transpose(0, 1, 3, 2), ((0, 0), (0, 0), (0, LEVP - LEVS), (0, 128 - WIDE)))
    flux_wide = jnp.pad(flux_probes, ((0, 0), (HALO, HALO), (0, 0)))
    flux_pairs = jnp.concatenate([flux_wide[:, :PAIRS], flux_wide[:, HALF:]], axis=2)
    field = transport(conc_start, flux_pairs, wide)

    wanted = (jnp.arange(SLOTS, dtype=jnp.int32) >= SLOTS // 2).astype(jnp.int32)
    index = jnp.stack(
        [
            row_index(obs_cell, 0, wanted),
            row_index(north_cells, BANDS, wanted),
            row_index(south_cells, -BANDS, wanted),
        ]
    )
    rows = strips(index, west_field, east_field, wide, field.reshape(FIELD_ROWS, 128))
    south_rows = along(rows[1], "lat", 1, False)
    north_rows = along(rows[2], "lat", -1, False)
    live = jnp.arange(SLOTS, dtype=jnp.int32) < obs_count[0]
    scale = jnp.where(live, obs_weight, 0.0)
    lanes = (SLOTS // 2, PROBES)
    weight = jnp.concatenate(
        [
            jnp.broadcast_to(scale[: SLOTS // 2, None], lanes),
            jnp.broadcast_to(scale[SLOTS // 2 :, None], lanes),
        ],
        axis=1,
    )
    images, gram = gram_of(rows[0], south_rows, north_rows, weight)
    gram = all_sum(gram)
    total_rows = SLOTS * lax.axis_size("lon") * lax.axis_size("lat")
    basis_t, factor = factor_of(gram, images, float(total_rows) ** 0.5)
    return basis_t.T, factor


def solution(mesh):
    in_specs = (
        P("lat", "lon", None),
        P("lat", "lon", None, None),
        P("lat", "lon", None),
        P("lat", "lon", None),
        P("lat", "lon", None),
        P(("lon", "lat")),
        P(("lon", "lat")),
        P(("lon", "lat")),
    )
    out_specs = (P(("lon", "lat"), None), P())
    return jax.shard_map(
        on_device, mesh=mesh, in_specs=in_specs, out_specs=out_specs, check_vma=False
    )
```

```python
import jax
import jax.numpy as jnp
from jax import lax
from jax.experimental import pallas as pl
from jax.experimental.pallas import tpu as pltpu
from jax.sharding import PartitionSpec as P

STEPS = 4
BANDS, COLS, LEVS, PROBES = 12, 36, 47, 64
HALO = STEPS
TALL = BANDS + 2 * HALO
WIDE = COLS + 2 * HALO
LEVP = 48
TILES = LEVP // 8
COLP = 40
RING = 4
BLOCK = 4
LAT_ROWS = 3 * HALO * COLP
HALF = COLS // 2
PAIRS = HALF + 2 * HALO
SLOTS = 1024
FIELD_ROWS = TALL * HALF * LEVP
ZERO_ROW = FIELD_ROWS
F32 = jnp.float32
HIGHEST = lax.Precision.HIGHEST
MIB = 1024 * 1024


def params(mib=12):
    return pltpu.CompilerParams(vmem_limit_bytes=mib * MIB)


def whole(space=pltpu.VMEM):
    return pl.BlockSpec(memory_space=space)


def along(x, axis, step, wrap):
    size = lax.axis_size(axis)
    pairs = [(i, (i + step) % size) for i in range(size) if wrap or 0 <= i + step < size]
    return lax.ppermute(x, axis, pairs)


def all_sum(x):
    lats = lax.axis_size("lat")
    size = lats * lax.axis_size("lon")
    for bits in ((1,), (2, 4), (2 * lats, 4 * lats), (lats, 8)):
        masks = [bits[0]] if len(bits) == 1 else [bits[0], bits[1], bits[0] | bits[1]]
        terms = [lax.ppermute(x, ("lon", "lat"), [(i, i ^ m) for i in range(size)]) for m in masks]
        for term in terms:
            x = x + term
    return x


def pack_lat_kernel(u, v, mix, cells, to_south, to_north):
    for which, ref in enumerate((u, v, mix)):
        for band in range(HALO):
            at = (which * HALO + band) * COLP
            to_south[at : at + COLS, 0:LEVS] = ref[band]
            to_north[at : at + COLS, 0:LEVS] = ref[BANDS - HALO + band]
    for dst in (to_south, to_north):
        dst[LAT_ROWS:] = cells[...].astype(F32)


def pack_lat(u, v, mix, cells):
    out = jax.ShapeDtypeStruct((LAT_ROWS + 8, 128), F32)
    return pl.pallas_call(
        pack_lat_kernel,
        in_specs=[whole()] * 4,
        out_specs=[whole()] * 2,
        out_shape=[out, out],
        compiler_params=params(62),
        name="pack_lat",
    )(u, v, mix, cells.reshape(8, 128))


def pack_lon_kernel(west, east, south, north, to_west, to_east):
    for src, dst, col in ((west, to_west, 0), (east, to_east, COLS - HALO)):
        dst[:, HALO // 2 : (HALO + BANDS) // 2] = src[...]
        for which in range(3):
            for edge in range(HALO):
                row = (which * HALO + edge) * COLP + col
                at = HALO * (edge % 2)
                dst[which, edge // 2, at : at + HALO] = south[row : row + HALO]
                dst[which, (HALO + BANDS + edge) // 2, at : at + HALO] = north[row : row + HALO]


def pack_lon(west, east, south, north):
    out = jax.ShapeDtypeStruct((3, TALL // 2, 8, 128), F32)
    return pl.pallas_call(
        pack_lon_kernel,
        in_specs=[whole()] * 4,
        out_specs=[whole()] * 2,
        out_shape=[out, out],
        compiler_params=params(),
        name="pack_lon",
    )(west, east, south, north)


def order_levels(dst, at, src):
    for tile in range(TILES):
        dst[at + (slice(8 * tile, 8 * tile + 8),)] = src[pl.ds(tile, 8, stride=TILES)]


def flip(dst, at, rows, flat, first, last_level):
    flat[0:LEVS, first : first + rows.shape[0]] = rows.T
    if last_level:
        flat[LEVS - 1 : LEVS] = jnp.zeros((1, 128), F32)
    order_levels(dst, at, flat)


def level_tile(ref, at, tile):
    if tile < TILES - 1:
        return ref[at + (pl.ds(tile, 8, stride=TILES),)]
    part = ref[at + (pl.ds(tile, 7, stride=TILES),)]
    return jnp.concatenate([part, jnp.zeros((1, PROBES), F32)], axis=0)


def prepare_kernel(
    west, east, flux, u, v, mix, gains, coef, to_west, to_east, coef_west, coef_east, flat
):
    high = HALF - HALO
    none = jnp.zeros((BANDS, HALO, PROBES), F32)
    gains[:, 0:HALO, 0:PROBES] = none
    gains[:, HALO:, 0:PROBES] = flux[:, 0 : HALF + HALO]
    gains[:, 0 : HALF + HALO, PROBES:] = flux[:, high:]
    gains[:, HALF + HALO :, PROBES:] = none
    for dst, src, first in ((to_west, west, 0), (to_east, east, COLS - HALO)):

        def pack(band, carry):
            for k in range(2):
                for tile in range(TILES):
                    low, up = level_tile(src, (band, k), tile), level_tile(src, (band, k + 2), tile)
                    dst[band, k, 8 * tile : 8 * tile + 8] = jnp.concatenate([low, up], axis=1)
                at = first + k
                pair = jnp.concatenate([flux[band, at : at + 1], flux[band, at + 2 : at + 3]], axis=1)
                dst[band, k, LEVS:LEVP] = pair
            return carry

        lax.fori_loop(0, BANDS, pack, 0)
    flat[...] = jnp.zeros((LEVP, 128), F32)
    for which, ref in enumerate((u, v, mix)):
        for band in range(BANDS):
            flip(coef, (which, band), ref[band], flat, HALO, which == 2)
            at = HALO * (band % 2)
            coef_west[which, band // 2, at : at + HALO, 0:LEVS] = ref[band, 0:HALO]
            coef_east[which, band // 2, at : at + HALO, 0:LEVS] = ref[band, COLS - HALO :]


def prepare(conc, flux, u, v, mix):
    sds = lambda *shape: jax.ShapeDtypeStruct(shape, F32)
    edge = lambda at: pl.BlockSpec((BANDS, HALO, LEVS, PROBES), lambda i: (0, at, 0, 0))
    return pl.pallas_call(
        prepare_kernel,
        grid=(1,),
        in_specs=[edge(0), edge(COLS // HALO - 1)] + [whole()] * 4,
        out_specs=[whole()] * 6,
        out_shape=[
            sds(BANDS, PAIRS, 128),
            sds(3, BANDS, LEVP, 128),
            sds(BANDS, 2, LEVP, 128),
            sds(BANDS, 2, LEVP, 128),
            sds(3, BANDS // 2, 8, 128),
            sds(3, BANDS // 2, 8, 128),
        ],
        scratch_shapes=[pltpu.VMEM((LEVP, 128), F32)],
        compiler_params=params(62),
        name="prepare",
    )(conc, conc, flux, u, v, mix)


def row_code(cells, shift):
    rest = ((cells.astype(F32) + 0.5) * (1.0 / LEVS)).astype(jnp.int32)
    level = cells - rest * LEVS
    line = ((rest.astype(F32) + 0.5) * (1.0 / COLS)).astype(jnp.int32)
    col = rest - line * COLS
    group = ((level.astype(F32) + 0.5) * (1.0 / TILES)).astype(jnp.int32)
    band = line + HALO + shift
    held = (band >= 0) & (band < TALL)
    upper = (col >= HALF).astype(jnp.int32)
    row = (band * HALF + col - HALF * upper) * LEVP + (level - group * TILES) * 8 + group
    later = lax.broadcasted_iota(jnp.int32, cells.shape, 0) * 128 >= SLOTS // 2
    cross = (upper == 1) != later
    return jnp.where(held, row, ZERO_ROW), cross.astype(F32)


def margins_kernel(south, north, cells, coef, codes, turned, flat):
    places = (
        (cells[...], 0),
        (north[LAT_ROWS:].astype(jnp.int32), BANDS),
        (south[LAT_ROWS:].astype(jnp.int32), -BANDS),
    )
    lower = lax.broadcasted_iota(jnp.int32, (128, 128), 1) < PROBES
    for group, (at, shift) in enumerate(places):
        row, cross = row_code(at, shift)
        codes[8 * group : 8 * group + 8] = row
        column = jnp.concatenate([cross, jnp.zeros((120, 128), F32)], axis=0).T
        for k in range(4):
            low = jnp.broadcast_to(column[:, k : k + 1], (128, 128))
            high = jnp.broadcast_to(column[:, k + 4 : k + 5], (128, 128))
            turned[group, 128 * k : 128 * k + 128] = jnp.where(lower, low, high)
    flat[...] = jnp.zeros((LEVP, 128), F32)
    for which in range(3):
        for side, src in enumerate((south, north)):
            for band in range(HALO):
                at = (which * HALO + band) * COLP
                rows = src[at : at + COLS, 0:LEVS]
                flip(coef, (which, side * HALO + band), rows, flat, HALO, which == 2)


def margins(south, north, cells):
    return pl.pallas_call(
        margins_kernel,
        in_specs=[whole()] * 3,
        out_specs=[whole()] * 3,
        out_shape=[
            jax.ShapeDtypeStruct((3, 2 * HALO, LEVP, 128), F32),
            jax.ShapeDtypeStruct((24, 128), jnp.int32),
            jax.ShapeDtypeStruct((3, SLOTS // 2, 128), F32),
        ],
        scratch_shapes=[pltpu.VMEM((LEVP, 128), F32)],
        compiler_params=params(),
        name="margins",
    )(south, north, cells.reshape(8, 128))


def split_terms(x):
    doubled = x + pltpu.roll(x, 64, 1)
    high = doubled.astype(jnp.bfloat16).astype(F32)
    lane = lax.broadcasted_iota(jnp.int32, x.shape, 1)
    return jnp.where(lane < 64, high, doubled - high).astype(jnp.bfloat16)


def selector(tile, low, high, high_sign=1.0):
    shape = (128, 256)
    row = lax.broadcasted_iota(jnp.int32, shape, 0) & 63
    col = lax.broadcasted_iota(jnp.int32, shape, 1)
    pair = 2 * tile + (col >> 7)
    upper = ((col >> 6) & 1) == 1
    weight = jnp.where(upper, high_sign, 1.0)
    return jnp.where(row == jnp.where(upper, high(pair), low(pair)), weight, 0.0).astype(jnp.bfloat16)


def spread(ref, split, chosen, tile, first=0, count=TALL):
    out = jnp.dot(
        split[first * LEVP : (first + count) * LEVP], chosen, preferred_element_type=F32
    )
    out = out.reshape(count, 1, LEVP, 256)
    ref[first : first + count, pl.ds(2 * tile, 1)] = out[..., :128]
    ref[first : first + count, pl.ds(2 * tile + 1, 1)] = out[..., 128:]


def face_flux(speed, behind, ahead):
    return speed * jnp.where(speed > 0.0, behind, ahead)


def mix_levels(dst, line, mixing, at, pair):
    here = [line[pair, 8 * t : 8 * t + 8] for t in range(TILES)]
    above = here[1:] + [pltpu.roll(here[0], 7, 0)]
    moved = [
        mixing[at, pair, 8 * t : 8 * t + 8] * (above[t] - here[t]) for t in range(TILES)
    ]
    below = [pltpu.roll(moved[-1], 1, 0)] + moved[:-1]
    for t in range(TILES):
        dst[at, pair, 8 * t : 8 * t + 8] = here[t] + (moved[t] - below[t])


def join_coef(split, own, margin, west, east, sides, flat):
    for which in range(3):
        for side, src in enumerate((west, east)):
            flat[...] = jnp.zeros((LEVP, 128), F32)
            rows = src[which].reshape(TALL * HALO, 128)
            flat[0:LEVS, 0 : TALL * HALO] = rows.T[0:LEVS]
            if which == 2:
                flat[LEVS - 1 : LEVS] = jnp.zeros((1, 128), F32)
            order_levels(sides, (which, side), flat)
    lane = lax.broadcasted_iota(jnp.int32, (LEVP, 128), 1)

    def join(band, ref, at):
        for which in range(3):
            left = pltpu.roll(sides[which, 0], lax.rem(128 - HALO * band, 128), 1)
            right = pltpu.roll(sides[which, 1], lax.rem(128 + HALO + COLS - HALO * band, 128), 1)
            x = jnp.where(lane < HALO, left, ref[which, at])
            x = jnp.where(lane >= HALO + COLS, right, x)
            x = jnp.where(lane < WIDE, x, 0.0)
            split[which, pl.ds(pl.multiple_of(band * LEVP, LEVP), LEVP)] = split_terms(x)

    def inner(at, carry):
        join(at + HALO, own, at)
        return carry

    lax.fori_loop(0, BANDS, inner, 0)

    def outer(at, carry):
        join(at, margin, at)
        join(at + HALO + BANDS, margin, at + HALO)
        return carry

    lax.fori_loop(0, HALO, outer, 0)


def transport_kernel(
    conc, flux, own, margin, from_west, from_east, out, split,
    c, u, v, m, fs0, fs1, line, sides, flat, stage, in_sem, out_sem,
):
    def fetch(band):
        slot = lax.rem(band, RING)
        return pltpu.make_async_copy(conc.at[band], stage.at[slot], in_sem.at[slot])

    for band in range(RING):
        fetch(band).start()
    join_coef(split, own, margin, from_west, from_east, sides, flat)

    def expand(tile):
        chosen = selector(tile, lambda pair: pair, lambda pair: pair + HALF)
        half = TALL // 2
        for which, ref in enumerate((u, v, m)):
            for first in (0, half):
                yield lambda: spread(ref, split.at[which], chosen, tile, first, half)

    zero = jnp.zeros((8, PROBES), F32)

    def load(band, carry):
        slot = lax.rem(band, RING)
        fetch(band).wait()
        pieces = expand(band)
        for pair in range(PAIRS):
            low, high = pair - HALO, pair - HALO + HALF
            for t in range(TILES):
                left = level_tile(stage, (slot, low), t) if low >= 0 else zero
                right = level_tile(stage, (slot, high), t) if high < COLS else zero
                both = jnp.concatenate([left, right], axis=1)
                c[band + HALO, pair, 8 * t : 8 * t + 8] = both
            if pair % 4 == 3:
                next(pieces)()

        @pl.when(band + RING < BANDS)
        def _():
            fetch(band + RING).start()

        return carry

    lax.fori_loop(0, BANDS, load, 0)
    for piece in expand(BANDS):
        piece()

    def clear(band, carry):
        c[band] = jnp.zeros((PAIRS, LEVP, 128), F32)
        c[band + HALO + BANDS] = jnp.zeros((PAIRS, LEVP, 128), F32)
        return carry

    lax.fori_loop(0, HALO, clear, 0)

    def save(band):
        return pltpu.make_async_copy(c.at[band, pl.ds(HALO, HALF)], out.at[band], out_sem.at[band])

    for step in range(1, STEPS + 1):
        first, last = step, PAIRS - step
        count = last - first
        chunk = count

        def gain(band, carry):
            for pair in range(PAIRS):
                c[band + HALO, pair, 0:1] = c[band + HALO, pair, 0:1] + flux[band, pair : pair + 1]
            return carry

        lax.fori_loop(0, BANDS, gain, 0)
        fs0[first:last] = jnp.zeros((count, LEVP, 128), F32)

        def row(band, below, above):
            north = jnp.minimum(band + 1, TALL - 1)
            here = c[band, first]
            west = face_flux(u[band, first], c[band, first - 1], here)

            def some(at, state):
                here, west = state
                for k in range(chunk):
                    pair = first + at * chunk + k
                    ahead = c[band, pair + 1]
                    east = face_flux(u[band, pair + 1], here, ahead)
                    top = face_flux(v[north, pair], here, c[north, pair])
                    line[pair] = here + (west - east) + (below[pair] - top)
                    above[pair] = top
                    here, west = ahead, east
                return here, west

            lax.fori_loop(0, count // chunk, some, (here, west))

            def level(at, carry):
                for k in range(chunk):
                    pair = first + at * chunk + k
                    mix_levels(c, line, m, band, pair)
                return carry

            lax.fori_loop(0, count // chunk, level, 0)
            if step == STEPS:
                save(band).start()

        def rows(at, carry):
            band = HALO - step + 2 * at
            row(band, fs0, fs1)
            row(band + 1, fs1, fs0)
            return carry

        lax.fori_loop(0, (BANDS + 2 * step) // 2, rows, 0)

    def drain(band, carry):
        save(band).wait()
        return carry

    lax.fori_loop(0, TALL, drain, 0)


def transport(conc, flux, own, margin, from_west, from_east):
    field = pltpu.VMEM((TALL, PAIRS, LEVP, 128), F32)
    line = pltpu.VMEM((PAIRS, LEVP, 128), F32)
    return pl.pallas_call(
        transport_kernel,
        in_specs=[whole(pl.ANY)] + [whole()] * 5,
        out_specs=[whole(pl.ANY), whole()],
        out_shape=[
            jax.ShapeDtypeStruct((TALL, HALF, LEVP, 128), F32),
            jax.ShapeDtypeStruct((3, TALL * LEVP, 128), jnp.bfloat16),
        ],
        scratch_shapes=[
            field,
            field,
            field,
            field,
            line,
            line,
            line,
            pltpu.VMEM((3, 2, LEVP, 128), F32),
            pltpu.VMEM((LEVP, 128), F32),
            pltpu.VMEM((RING, COLS, LEVS, PROBES), F32),
            pltpu.SemaphoreType.DMA((RING,)),
            pltpu.SemaphoreType.DMA((TALL,)),
        ],
        compiler_params=params(62),
        name="transport",
    )(conc, flux, own, margin, from_west, from_east)


def strips_kernel(
    codes, turned, west, east, split, field, own, north, south,
    c, u, v, m, fs0, fs1, line, gain, full, got0, got1, got2, sem,
):
    fetch = pltpu.make_async_copy(field, full.at[pl.ds(0, FIELD_ROWS)], sem)
    fetch.start()

    def expand(tile, carry):
        faces = selector(tile, lambda k: k, lambda k: WIDE - k, -1.0)
        cells = selector(tile, lambda k: k, lambda k: WIDE - 1 - k)
        for which, ref in enumerate((u, v, m)):
            spread(ref, split.at[which], cells if which else faces, tile)
        return carry

    lax.fori_loop(0, HALO, expand, 0)

    def clear(band, carry):
        c[band] = jnp.zeros((2 * HALO, LEVP, 128), F32)
        return carry

    lax.fori_loop(0, TALL, clear, 0)
    lower = lax.broadcasted_iota(jnp.int32, (LEVP, 128), 1) < PROBES
    inside = lax.broadcasted_iota(jnp.int32, (LEVP, 128), 0) < LEVS

    def place(band, carry):
        for k in range(2):
            left, right = west[band, k], east[band, 1 - k]
            outer = jnp.where(lower, left, right)
            inner = pltpu.roll(jnp.where(lower, right, left), PROBES, 1)
            for at, value in ((k, outer), (k + 2, inner)):
                c[band + HALO, at] = jnp.where(inside, value, 0.0)
                gain[band, at, 0:1] = value[LEVS:LEVP]
        return carry

    lax.fori_loop(0, BANDS, place, 0)

    full[ZERO_ROW : ZERO_ROW + 8] = jnp.zeros((8, 128), F32)

    for step in range(1, STEPS + 1):
        region = range(step, step + HALO)

        def add(band, carry):
            for k in range(step - 1, HALO):
                c[band + HALO, k, 0:1] = c[band + HALO, k, 0:1] + gain[band, k, 0:1]
            return carry

        lax.fori_loop(0, BANDS, add, 0)
        for k in region:
            fs0[k] = jnp.zeros((LEVP, 128), F32)

        def row(band, below, above):
            north = jnp.minimum(band + 1, TALL - 1)
            here = c[band, step]
            behind = face_flux(u[band, step], c[band, step - 1], here)
            for k in region:
                if k < step + HALO - 1:
                    ahead = c[band, k + 1]
                    front = face_flux(u[band, k + 1], here, ahead)
                    net = behind - front
                else:
                    net = behind
                top = face_flux(v[north, k], here, c[north, k])
                line[k] = here + net + (below[k] - top)
                above[k] = top
                here, behind = ahead, front
            for k in region:
                mix_levels(c, line, m, band, k)

        def rows(at, carry):
            band = HALO - step + 2 * at
            row(band, fs0, fs1)
            row(band + 1, fs1, fs0)
            return carry

        lax.fori_loop(0, (BANDS + 2 * step) // 2, rows, 0)

    fetch.wait()

    def merge(band, carry):
        base = band * (HALF * LEVP)
        spots, sums = [], []
        for k in range(HALO):
            share = c[band, HALO + k]
            for pair, keep in ((k, lower), (HALF - 1 - k, ~lower)):
                rows = pl.ds(pl.multiple_of(base + pair * LEVP, LEVP), LEVP)
                spots.append(rows)
                sums.append(full[rows] + jnp.where(keep, share, 0.0))
        for rows, value in zip(spots, sums):
            full[rows] = value
        return carry

    lax.fori_loop(0, TALL, merge, 0)

    left_lanes = lax.broadcasted_iota(jnp.int32, (8, 128), 1) < PROBES
    for group, (out, buffer) in enumerate(((own, got0), (north, got1), (south, got2))):

        def pick(at, carry):
            rows = buffer.at[pl.ds(pl.multiple_of(at * 128, 128), 128)]
            for k in range(128):
                rows[k : k + 1] = full[pl.ds(codes[group * 8 + at, k], 1)]
            return carry

        lax.fori_loop(0, SLOTS // 128, pick, 0)

        def join(at, carry):
            for k in range(16):
                at8 = pl.multiple_of(at * 128 + k * 8, 8)
                one, two = buffer[pl.ds(at8, 8)], buffer[pl.ds(at8 + SLOTS // 2, 8)]
                straight = jnp.where(left_lanes, one, two)
                crossed = pltpu.roll(jnp.where(left_lanes, two, one), PROBES, 1)
                out[pl.ds(at8, 8)] = jnp.where(turned[group, pl.ds(at8, 8)] > 0.5, crossed, straight)
            return carry

        lax.fori_loop(0, SLOTS // 256, join, 0)


def strips(codes, turned, west, east, split, field):
    strip = pltpu.VMEM((TALL, 2 * HALO, LEVP, 128), F32)
    line = pltpu.VMEM((2 * HALO, LEVP, 128), F32)
    buffer = pltpu.VMEM((SLOTS, 128), F32)
    return pl.pallas_call(
        strips_kernel,
        in_specs=[whole(pltpu.SMEM), whole(), whole(), whole(), whole(), whole(pl.ANY)],
        out_specs=[whole()] * 3,
        out_shape=[jax.ShapeDtypeStruct((SLOTS // 2, 128), F32)] * 3,
        scratch_shapes=[
            strip,
            strip,
            strip,
            strip,
            line,
            line,
            line,
            pltpu.VMEM((BANDS, HALO, 8, 128), F32),
            pltpu.VMEM((FIELD_ROWS + 8, 128), F32),
            buffer,
            buffer,
            buffer,
            pltpu.SemaphoreType.DMA,
        ],
        compiler_params=params(62),
        name="strips",
    )(codes, turned, west, east, split, field)


def gram_kernel(own, from_south, from_north, weight, images, gram):
    rows = (own[...] + from_south[...] + from_north[...]) * weight[...]
    images[...] = rows
    both = lax.dot_general(
        rows, rows, (((0,), (0,)), ((), ())), precision=HIGHEST, preferred_element_type=F32
    )
    total = both[:PROBES, :PROBES] + both[PROBES:, PROBES:]
    gram[:, 0:PROBES] = total[: PROBES // 2]
    gram[:, PROBES:] = total[PROBES // 2 :]


def gram_of(own, from_south, from_north, weight):
    return pl.pallas_call(
        gram_kernel,
        in_specs=[whole()] * 4,
        out_specs=[whole()] * 2,
        out_shape=[
            jax.ShapeDtypeStruct((SLOTS // 2, 128), F32),
            jax.ShapeDtypeStruct((PROBES // 2, 128), F32),
        ],
        compiler_params=params(),
        name="gram",
    )(own, from_south, from_north, weight)


def factor_kernel(root, gram, images, basis_t, factor, work, pivots):
    sublane = lax.broadcasted_iota(jnp.int32, (8, 128), 0)
    half = PROBES // 2
    work[0:half, 0:PROBES] = gram[:, 0:PROBES]
    work[half:, 0:PROBES] = gram[:, PROBES:]
    diagonal = (
        lax.broadcasted_iota(jnp.int32, (PROBES, PROBES), 0)
        == lax.broadcasted_iota(jnp.int32, (PROBES, PROBES), 1)
    )
    work[:, PROBES:] = diagonal.astype(F32)
    tiles = [work[8 * t : 8 * t + 8] for t in range(PROBES // 8)]
    for first in range(0, PROBES, BLOCK):
        top = first // 8
        live = range(top, PROBES // 8)
        column = {
            (j, t): jnp.broadcast_to(tiles[t][:, first + j : first + j + 1], (8, 128))
            for j in range(BLOCK)
            for t in live
        }
        for j in range(BLOCK):
            at = first + j
            pick = lambda tile, n: jnp.broadcast_to(tile[n % 8 : n % 8 + 1], (8, 128))
            inverse = 1.0 / pick(column[j, top], at)
            pivots[at : at + 1] = column[j, top][at % 8 : at % 8 + 1]
            pivot = pick(tiles[top], at) * inverse
            later = [pick(column[j, top], first + i) * inverse for i in range(j + 1, BLOCK)]
            for t in live:
                share = column[j, t]
                if t == top:
                    share = jnp.where(sublane > at % 8, share, 0.0)
                tiles[t] = tiles[t] - share * pivot
                for i in range(j + 1, BLOCK):
                    column[i, t] = column[i, t] - share * later[i - j - 1]
    for t in range(PROBES // 8):
        rows = slice(8 * t, 8 * t + 8)
        work[rows] = tiles[t] * (1.0 / jnp.sqrt(pivots[rows]))
    both = work[...]
    row = lax.broadcasted_iota(jnp.int32, (PROBES, PROBES), 0)
    col = lax.broadcasted_iota(jnp.int32, (PROBES, PROBES), 1)
    factor[...] = jnp.where(col >= row, both[:, :PROBES], 0.0) * (1.0 / root)
    inverse_t = jnp.where(col <= row, both[:, PROBES:], 0.0) * root
    zero = jnp.zeros((PROBES, PROBES), F32)
    twice = jnp.concatenate(
        [
            jnp.concatenate([inverse_t, zero], axis=1),
            jnp.concatenate([zero, inverse_t], axis=1),
        ],
        axis=0,
    )
    basis = lax.dot_general(
        twice, images[...], (((1,), (1,)), ((), ())), precision=HIGHEST, preferred_element_type=F32
    )
    basis_t[:, 0 : SLOTS // 2] = basis[:PROBES]
    basis_t[:, SLOTS // 2 :] = basis[PROBES:]


def factor_of(gram, images, root):
    return pl.pallas_call(
        lambda *refs: factor_kernel(root, *refs),
        in_specs=[whole()] * 2,
        out_specs=[whole()] * 2,
        out_shape=[
            jax.ShapeDtypeStruct((PROBES, SLOTS), F32),
            jax.ShapeDtypeStruct((PROBES, PROBES), F32),
        ],
        scratch_shapes=[pltpu.VMEM((PROBES, 128), F32)] * 2,
        compiler_params=params(),
        name="factor",
    )(gram, images)


def on_device(
    flux_probes, conc_start, u_courant, v_courant, vert_mix, obs_cell, obs_weight, obs_count
):
    to_south, to_north = pack_lat(u_courant, v_courant, vert_mix, obs_cell)
    from_south = along(to_north, "lat", 1, False)
    from_north = along(to_south, "lat", -1, False)
    flux, own, edge_west, edge_east, coef_west, coef_east = prepare(
        conc_start, flux_probes, u_courant, v_courant, vert_mix
    )
    to_west, to_east = pack_lon(coef_west, coef_east, from_south, from_north)
    from_west = along(to_east, "lon", 1, True)
    from_east = along(to_west, "lon", -1, True)
    margin, codes, turned = margins(from_south, from_north, obs_cell)
    edge_west, edge_east, from_west, from_east = lax.optimization_barrier(
        (edge_west, edge_east, from_west, from_east)
    )
    west_field = along(edge_east, "lon", 1, True)
    east_field = along(edge_west, "lon", -1, True)
    field, split = transport(conc_start, flux, own, margin, from_west, from_east)
    rows, for_north, for_south = strips(
        codes, turned, west_field, east_field, split, field.reshape(FIELD_ROWS, 128)
    )
    south_rows = along(for_north, "lat", 1, False)
    north_rows = along(for_south, "lat", -1, False)
    live = jnp.arange(SLOTS, dtype=jnp.int32) < obs_count[0]
    scale = jnp.where(live, obs_weight, 0.0)
    lanes = (SLOTS // 2, PROBES)
    weight = jnp.concatenate(
        [
            jnp.broadcast_to(scale[: SLOTS // 2, None], lanes),
            jnp.broadcast_to(scale[SLOTS // 2 :, None], lanes),
        ],
        axis=1,
    )
    images, gram = gram_of(rows, south_rows, north_rows, weight)
    gram = all_sum(gram)
    total_rows = SLOTS * lax.axis_size("lon") * lax.axis_size("lat")
    basis_t, factor = factor_of(gram, images, float(total_rows) ** 0.5)
    return basis_t.T, factor


def solution(mesh):
    in_specs = (
        P("lat", "lon", None),
        P("lat", "lon", None, None),
        P("lat", "lon", None),
        P("lat", "lon", None),
        P("lat", "lon", None),
        P(("lon", "lat")),
        P(("lon", "lat")),
        P(("lon", "lat")),
    )
    out_specs = (P(("lon", "lat"), None), P())
    return jax.shard_map(
        on_device, mesh=mesh, in_specs=in_specs, out_specs=out_specs, check_vma=False
    )
```

```python
import jax
import jax.numpy as jnp
from jax import lax
from jax.experimental import pallas as pl
from jax.experimental.pallas import tpu as pltpu
from jax.sharding import PartitionSpec as P

STEPS = 4
BANDS, COLS, LEVS, PROBES = 12, 36, 47, 64
HALO = STEPS
TALL = BANDS + 2 * HALO
WIDE = COLS + 2 * HALO
LEVP = 48
TILES = LEVP // 8
COLP = 40
RING = 6
BLOCK = 4
LAT_ROWS = 3 * (HALO // 2) * COLP
LON_BANDS = TALL // 2
HALF = COLS // 2
PAIRS = HALF + 2 * HALO
SLOTS = 1024
FIELD_ROWS = TALL * HALF * LEVP
ZERO_ROW = FIELD_ROWS
F32 = jnp.float32
HIGHEST = lax.Precision.HIGHEST
MIB = 1024 * 1024


def params(mib=12):
    return pltpu.CompilerParams(vmem_limit_bytes=mib * MIB)


def whole(space=pltpu.VMEM):
    return pl.BlockSpec(memory_space=space)


def swap(x, axis, apart, wrap=False):
    size = lax.axis_size(axis)
    partner = [((i + 1) ^ 1) - 1 if apart else i ^ 1 for i in range(size)]
    if wrap:
        partner = [j % size for j in partner]
    return lax.ppermute(x, axis, [(i, j) for i, j in enumerate(partner) if 0 <= j < size])


def all_sum(x):
    lats = lax.axis_size("lat")
    size = lats * lax.axis_size("lon")
    for bits in ((1,), (2, 4), (2 * lats, 4 * lats), (lats, 8)):
        masks = [bits[0]] if len(bits) == 1 else [bits[0], bits[1], bits[0] | bits[1]]
        terms = [lax.ppermute(x, ("lon", "lat"), [(i, i ^ m) for i in range(size)]) for m in masks]
        for term in terms:
            x = x + term
    return x


def north_far(odd):
    return odd[0] & 1


def near_west(odd):
    return odd[0] >> 1


def lat_at(which, band):
    return (which * (HALO // 2) + band % (HALO // 2)) * COLP, 64 * (band // (HALO // 2))


def lon_at(band):
    place = band % LON_BANDS
    return place // 2, HALO * (place % 2), 64 * (band // LON_BANDS)


def pack_lat_kernel(odd, u, v, mix, cells, to_far, to_near, to_west, to_east):
    far = north_far(odd) * (BANDS - HALO)
    near = BANDS - HALO - far
    for which, ref in enumerate((u, v, mix)):
        for band in range(HALO):
            row, lane = lat_at(which, band)
            to_far[row : row + COLS, lane : lane + LEVS] = ref[far + band]
            to_near[row : row + COLS, lane : lane + LEVS] = ref[near + band]
        for band in range(BANDS):
            tile, row, lane = lon_at(band + HALO)
            for dst, col in ((to_west, 0), (to_east, COLS - HALO)):
                dst[which, tile, row : row + HALO, lane : lane + LEVS] = ref[band, col : col + HALO]
    for dst in (to_far, to_near):
        dst[LAT_ROWS:] = cells[...].astype(F32)


def pack_lat(odd, u, v, mix, cells):
    lat = jax.ShapeDtypeStruct((LAT_ROWS + 8, 128), F32)
    lon = jax.ShapeDtypeStruct((3, LON_BANDS // 2, 8, 128), F32)
    return pl.pallas_call(
        pack_lat_kernel,
        in_specs=[whole(pltpu.SMEM)] + [whole()] * 4,
        out_specs=[whole()] * 4,
        out_shape=[lat, lat, lon, lon],
        compiler_params=params(62),
        name="pack_lat",
    )(odd, u, v, mix, cells.reshape(8, 128))


def pack_lon_kernel(odd, west, east, far, near, to_far, to_near, edge_west, edge_east):
    far_north, west_near = north_far(odd) == 1, near_west(odd) == 1
    for src, dst, col in ((west, edge_west, 0), (east, edge_east, COLS - HALO)):
        dst[...] = src[...]
        for which in range(3):
            for edge in range(HALO):
                row, lane = lat_at(which, edge)
                ours = (slice(row + col, row + col + HALO), slice(lane, lane + LEVS))
                one, two = far[ours], near[ours]
                for rows, band in (
                    (jnp.where(far_north, two, one), edge),
                    (jnp.where(far_north, one, two), HALO + BANDS + edge),
                ):
                    tile, at, first = lon_at(band)
                    dst[which, tile, at : at + HALO, first : first + LEVS] = rows
    one, two = edge_west[...], edge_east[...]
    to_near[...] = jnp.where(west_near, one, two)
    to_far[...] = jnp.where(west_near, two, one)


def pack_lon(odd, west, east, far, near):
    out = jax.ShapeDtypeStruct(west.shape, F32)
    return pl.pallas_call(
        pack_lon_kernel,
        in_specs=[whole(pltpu.SMEM)] + [whole()] * 4,
        out_specs=[whole()] * 2,
        out_shape=[out, out],
        scratch_shapes=[pltpu.VMEM(west.shape, F32)] * 2,
        compiler_params=params(),
        name="pack_lon",
    )(odd, west, east, far, near)


def turn(dst, at, rows, flat, last_level):
    flat[0:LEVS, HALO : HALO + COLS] = rows.T
    if last_level:
        flat[LEVS - 1 : LEVS] = jnp.zeros((1, 128), F32)
    for tile in range(TILES):
        dst[at + (slice(8 * tile, 8 * tile + 8),)] = flat[pl.ds(tile, 8, stride=TILES)]


def two_terms(x, lane):
    high = x.astype(jnp.bfloat16).astype(F32)
    return jnp.where(lane < 64, high, x - high)


def level_tile(ref, at, tile):
    if tile < TILES - 1:
        return ref[at + (pl.ds(tile, 8, stride=TILES),)]
    part = ref[at + (pl.ds(tile, 7, stride=TILES),)]
    return jnp.concatenate([part, jnp.zeros((1, PROBES), F32)], axis=0)


def edges_kernel(odd, far, near, flux, to_far, to_near):
    for dst, src, west in ((to_far, far, 1 - near_west(odd)), (to_near, near, near_west(odd))):
        first = (1 - west) * (COLS - HALO)

        def pack(band, carry):
            for k in range(2):
                for tile in range(TILES):
                    low, up = level_tile(src, (band, k), tile), level_tile(src, (band, k + 2), tile)
                    dst[band, k, 8 * tile : 8 * tile + 8] = jnp.concatenate([low, up], axis=1)
                at = first + k
                pair = [flux[band, pl.ds(at, 1)], flux[band, pl.ds(at + 2, 1)]]
                dst[band, k, LEVS:LEVP] = jnp.concatenate(pair, axis=1)
            return carry

        lax.fori_loop(0, BANDS, pack, 0)


def pack_edges(odd, conc, flux):
    out = jax.ShapeDtypeStruct((BANDS, 2, LEVP, 128), F32)
    last = COLS // HALO - 1
    shape = (BANDS, HALO, LEVS, PROBES)
    return pl.pallas_call(
        edges_kernel,
        grid_spec=pltpu.PrefetchScalarGridSpec(
            num_scalar_prefetch=1,
            grid=(1,),
            in_specs=[
                pl.BlockSpec(shape, lambda i, odd: (0, last * near_west(odd), 0, 0)),
                pl.BlockSpec(shape, lambda i, odd: (0, last * (1 - near_west(odd)), 0, 0)),
                whole(),
            ],
            out_specs=[whole()] * 2,
        ),
        out_shape=[out, out],
        compiler_params=params(62),
        name="pack_edges",
    )(odd, conc, conc, flux)


def row_code(cells, shift):
    rest = ((cells.astype(F32) + 0.5) * (1.0 / LEVS)).astype(jnp.int32)
    level = cells - rest * LEVS
    line = ((rest.astype(F32) + 0.5) * (1.0 / COLS)).astype(jnp.int32)
    col = rest - line * COLS
    group = ((level.astype(F32) + 0.5) * (1.0 / TILES)).astype(jnp.int32)
    band = line + HALO + shift
    held = (band >= 0) & (band < TALL)
    upper = (col >= HALF).astype(jnp.int32)
    row = (band * HALF + col - HALF * upper) * LEVP + (level - group * TILES) * 8 + group
    later = lax.broadcasted_iota(jnp.int32, cells.shape, 0) * 128 >= SLOTS // 2
    cross = (upper == 1) != later
    return jnp.where(held, row, ZERO_ROW), cross.astype(F32)


def prepare_kernel(odd, flux, u, v, mix, far, near, cells, gains, coef, codes, turned, *flats):
    high = HALF - HALO
    none = jnp.zeros((BANDS, HALO, PROBES), F32)
    gains[:, 0:HALO, 0:PROBES] = none
    gains[:, HALO:, 0:PROBES] = flux[:, 0 : HALF + HALO]
    gains[:, 0 : HALF + HALO, PROBES:] = flux[:, high:]
    gains[:, HALF + HALO :, PROBES:] = none
    north = north_far(odd) * 2 - 1
    places = (
        (cells[...], 0),
        (far[LAT_ROWS:].astype(jnp.int32), BANDS * north),
        (near[LAT_ROWS:].astype(jnp.int32), -BANDS * north),
    )
    lower = lax.broadcasted_iota(jnp.int32, (128, 128), 1) < PROBES
    for group, (at, shift) in enumerate(places):
        row, cross = row_code(at, shift)
        codes[8 * group : 8 * group + 8] = row
        column = jnp.concatenate([cross, jnp.zeros((120, 128), F32)], axis=0).T
        for k in range(4):
            low = jnp.broadcast_to(column[:, k : k + 1], (128, 128))
            up = jnp.broadcast_to(column[:, k + 4 : k + 5], (128, 128))
            turned[group, 128 * k : 128 * k + 128] = jnp.where(lower, low, up)
    for flat in flats:
        flat[...] = jnp.zeros((LEVP, 128), F32)
    far_at = north_far(odd) * (HALO + BANDS)
    near_at = HALO + BANDS - far_at
    for which, ref in enumerate((u, v, mix)):
        for band in range(BANDS):
            turn(coef, (which, band + HALO), ref[band], flats[band % 4], which == 2)
        for band in range(HALO):
            row, lane = lat_at(which, band)
            for k, (first, src) in enumerate(((far_at, far), (near_at, near))):
                rows = src[row : row + COLS, lane : lane + LEVS]
                turn(coef, (which, first + band), rows, flats[band % 2 * 2 + k], which == 2)
    lane = lax.broadcasted_iota(jnp.int32, (LEVP, 128), 1)

    def split(at, carry):
        for which in range(3):
            for k in range(4):
                x = coef[which, at * 4 + k]
                coef[which, at * 4 + k] = two_terms(x + pltpu.roll(x, 64, 1), lane)
        return carry

    lax.fori_loop(0, TALL // 4, split, 0)


def prepare(odd, flux, u, v, mix, far, near, cells):
    return pl.pallas_call(
        prepare_kernel,
        in_specs=[whole(pltpu.SMEM)] + [whole()] * 7,
        out_specs=[whole()] * 4,
        out_shape=[
            jax.ShapeDtypeStruct((BANDS, PAIRS, 128), F32),
            jax.ShapeDtypeStruct((3, TALL, LEVP, 128), F32),
            jax.ShapeDtypeStruct((24, 128), jnp.int32),
            jax.ShapeDtypeStruct((3, SLOTS // 2, 128), F32),
        ],
        scratch_shapes=[pltpu.VMEM((LEVP, 128), F32)] * 4,
        compiler_params=params(62),
        name="prepare",
    )(odd, flux, u, v, mix, far, near, cells.reshape(8, 128))


def join_coef(odd, split, coef, far, near, sides, flat):
    span = 5 * HALO
    lane = lax.broadcasted_iota(jnp.int32, (8, 128), 1)
    west_near = near_west(odd) == 1
    flat[...] = jnp.zeros((LEVP, 128), F32)
    for which in range(3):
        one, two = far[which].reshape(-1, 128), near[which].reshape(-1, 128)
        west = jnp.where(west_near, two, one).T
        east = jnp.where(west_near, one, two).T
        for group in range(4):
            levels = slice(64 * (group // 2), 64 * (group // 2) + LEVS)
            cols = slice(span * (group % 2), span * (group % 2) + span)
            for at, src in ((0, west), (HALO + COLS, east)):
                flat[0:LEVS, at : at + span] = src[levels, cols]
            if which == 2:
                flat[LEVS - 1 : LEVS] = jnp.zeros((1, 128), F32)
            for tile in range(TILES):
                x = flat[pl.ds(tile, 8, stride=TILES)]
                x = x + pltpu.roll(x, 64, 1)
                sides[which, group, 8 * tile : 8 * tile + 8] = two_terms(x, lane)
    column = lax.broadcasted_iota(jnp.int32, (LEVP, 128), 1) & 63
    margin = (column < HALO) | ((column >= HALO + COLS) & (column < WIDE))

    def join(group, carry):
        for k in range(5):
            band = group * 5 + k
            rows = pl.ds(pl.multiple_of(band * LEVP, LEVP), LEVP)
            for which in range(3):
                beside = sides[which, group]
                if k:
                    beside = pltpu.roll(beside, 128 - HALO * k, 1)
                x = jnp.where(margin, beside, coef[which, band])
                split[which, rows] = x.astype(jnp.bfloat16)
        return carry

    lax.fori_loop(0, 4, join, 0)


def selector(tile, low, high, high_sign=1.0):
    shape = (128, 256)
    row = lax.broadcasted_iota(jnp.int32, shape, 0) & 63
    col = lax.broadcasted_iota(jnp.int32, shape, 1)
    pair = 2 * tile + (col >> 7)
    upper = ((col >> 6) & 1) == 1
    weight = jnp.where(upper, high_sign, 1.0)
    return jnp.where(row == jnp.where(upper, high(pair), low(pair)), weight, 0.0).astype(jnp.bfloat16)


def spread(ref, split, chosen, tile, first=0, count=TALL):
    out = jnp.dot(
        split[first * LEVP : (first + count) * LEVP], chosen, preferred_element_type=F32
    )
    out = out.reshape(count, 1, LEVP, 256)
    ref[first : first + count, pl.ds(2 * tile, 1)] = out[..., :128]
    ref[first : first + count, pl.ds(2 * tile + 1, 1)] = out[..., 128:]


def face_flux(speed, behind, ahead):
    return speed * jnp.where(speed > 0.0, behind, ahead)


def mix_levels(dst, line, mixing, at, pair):
    here = [line[pair, 8 * t : 8 * t + 8] for t in range(TILES)]
    above = here[1:] + [pltpu.roll(here[0], 7, 0)]
    moved = [
        mixing[at, pair, 8 * t : 8 * t + 8] * (above[t] - here[t]) for t in range(TILES)
    ]
    below = [pltpu.roll(moved[-1], 1, 0)] + moved[:-1]
    for t in range(TILES):
        dst[at, pair, 8 * t : 8 * t + 8] = here[t] + (moved[t] - below[t])


def two_rows(band, pairs, c, u, v, m, fs, line0, line1, closed=False):
    first, north = pairs[0], jnp.minimum(band + 2, TALL - 1)
    here0, here1 = c[band, first], c[band + 1, first]
    west0 = face_flux(u[band, first], c[band, first - 1], here0)
    west1 = face_flux(u[band + 1, first], c[band + 1, first - 1], here1)
    for pair in pairs:
        middle = face_flux(v[band + 1, pair], here0, here1)
        top = face_flux(v[north, pair], here1, c[north, pair])
        net0, net1 = here0 + west0, here1 + west1
        if not (closed and pair == pairs[-1]):
            ahead0, ahead1 = c[band, pair + 1], c[band + 1, pair + 1]
            west0 = face_flux(u[band, pair + 1], here0, ahead0)
            west1 = face_flux(u[band + 1, pair + 1], here1, ahead1)
            net0, net1 = net0 - west0, net1 - west1
            here0, here1 = ahead0, ahead1
        line0[pair] = net0 + (fs[pair] - middle)
        line1[pair] = net1 + (middle - top)
        fs[pair] = top
    for pair in pairs:
        mix_levels(c, line0, m, band, pair)
        mix_levels(c, line1, m, band + 1, pair)


def transport_kernel(
    odd, conc, flux, coef, far, near, out, split,
    c, u, v, m, fs, line0, line1, sides, flat, stage, in_sem, out_sem,
):
    def fetch(band):
        slot = lax.rem(band, RING)
        return pltpu.make_async_copy(conc.at[band], stage.at[slot], in_sem.at[slot])

    for band in range(RING):
        fetch(band).start()
    join_coef(odd, split, coef, far, near, sides, flat)

    def expand(tile):
        chosen = selector(tile, lambda pair: pair, lambda pair: pair + HALF)
        half = TALL // 2
        for which, ref in enumerate((u, v, m)):
            for first in (0, half):
                yield lambda: spread(ref, split.at[which], chosen, tile, first, half)

    zero = jnp.zeros((8, PROBES), F32)

    def load(band, carry):
        slot = lax.rem(band, RING)
        fetch(band).wait()
        pieces = expand(band)
        for pair in range(PAIRS):
            low, high = pair - HALO, pair - HALO + HALF
            for t in range(TILES):
                left = level_tile(stage, (slot, low), t) if low >= 0 else zero
                right = level_tile(stage, (slot, high), t) if high < COLS else zero
                both = jnp.concatenate([left, right], axis=1)
                c[band + HALO, pair, 8 * t : 8 * t + 8] = both
            if pair % 4 == 3:
                next(pieces)()

        @pl.when(band + RING < BANDS)
        def _():
            fetch(band + RING).start()

        return carry

    lax.fori_loop(0, BANDS, load, 0)
    for piece in expand(BANDS):
        piece()

    def clear(band, carry):
        c[band] = jnp.zeros((PAIRS, LEVP, 128), F32)
        c[band + HALO + BANDS] = jnp.zeros((PAIRS, LEVP, 128), F32)
        return carry

    lax.fori_loop(0, HALO, clear, 0)

    def save(band):
        return pltpu.make_async_copy(c.at[band, pl.ds(HALO, HALF)], out.at[band], out_sem.at[band])

    for step in range(1, STEPS + 1):
        first, last = step, PAIRS - step
        count = last - first

        def gain(band, carry):
            for pair in range(PAIRS):
                c[band + HALO, pair, 0:1] = c[band + HALO, pair, 0:1] + flux[band, pair : pair + 1]
            return carry

        lax.fori_loop(0, BANDS, gain, 0)
        fs[first:last] = jnp.zeros((count, LEVP, 128), F32)

        def rows(at, carry):
            band = HALO - step + 2 * at
            two_rows(band, range(first, last), c, u, v, m, fs, line0, line1)
            if step == STEPS:
                save(band).start()
                save(band + 1).start()
            return carry

        lax.fori_loop(0, (BANDS + 2 * step) // 2, rows, 0)

    def drain(band, carry):
        save(band).wait()
        return carry

    lax.fori_loop(0, TALL, drain, 0)


def transport(odd, conc, flux, coef, far, near):
    field = pltpu.VMEM((TALL, PAIRS, LEVP, 128), F32)
    line = pltpu.VMEM((PAIRS, LEVP, 128), F32)
    return pl.pallas_call(
        transport_kernel,
        in_specs=[whole(pltpu.SMEM), whole(pl.ANY)] + [whole()] * 4,
        out_specs=[whole(pl.ANY), whole()],
        out_shape=[
            jax.ShapeDtypeStruct((TALL, HALF, LEVP, 128), F32),
            jax.ShapeDtypeStruct((3, TALL * LEVP, 128), jnp.bfloat16),
        ],
        scratch_shapes=[
            field,
            field,
            field,
            field,
            line,
            line,
            line,
            pltpu.VMEM((3, 4, LEVP, 128), F32),
            pltpu.VMEM((LEVP, 128), F32),
            pltpu.VMEM((RING, COLS, LEVS, PROBES), F32),
            pltpu.SemaphoreType.DMA((RING,)),
            pltpu.SemaphoreType.DMA((TALL,)),
        ],
        compiler_params=params(62),
        name="transport",
    )(odd, conc, flux, coef, far, near)


def strips_kernel(
    odd, codes, turned, edge_far, edge_near, split, field, own, far, near,
    c, u, v, m, fs, line0, line1, gain, full, got0, got1, got2, sem,
):
    fetch = pltpu.make_async_copy(field, full.at[pl.ds(0, FIELD_ROWS)], sem)
    fetch.start()

    def expand(tile, carry):
        faces = selector(tile, lambda k: k, lambda k: WIDE - k, -1.0)
        cells = selector(tile, lambda k: k, lambda k: WIDE - 1 - k)
        for which, ref in enumerate((u, v, m)):
            spread(ref, split.at[which], cells if which else faces, tile)
        return carry

    lax.fori_loop(0, HALO, expand, 0)

    def clear(band, carry):
        c[band] = jnp.zeros((2 * HALO, LEVP, 128), F32)
        return carry

    lax.fori_loop(0, TALL, clear, 0)
    lower = lax.broadcasted_iota(jnp.int32, (LEVP, 128), 1) < PROBES
    inside = lax.broadcasted_iota(jnp.int32, (LEVP, 128), 0) < LEVS

    west_near = near_west(odd) == 1

    def place(band, carry):
        for k in range(2):
            left = jnp.where(west_near, edge_near[band, k], edge_far[band, k])
            right = jnp.where(west_near, edge_far[band, 1 - k], edge_near[band, 1 - k])
            outer = jnp.where(lower, left, right)
            inner = pltpu.roll(jnp.where(lower, right, left), PROBES, 1)
            for at, value in ((k, outer), (k + 2, inner)):
                c[band + HALO, at] = jnp.where(inside, value, 0.0)
                gain[band, at, 0:1] = value[LEVS:LEVP]
        return carry

    lax.fori_loop(0, BANDS, place, 0)

    full[ZERO_ROW : ZERO_ROW + 8] = jnp.zeros((8, 128), F32)

    for step in range(1, STEPS + 1):
        region = range(step, step + HALO)

        def add(band, carry):
            for k in range(step - 1, HALO):
                c[band + HALO, k, 0:1] = c[band + HALO, k, 0:1] + gain[band, k, 0:1]
            return carry

        lax.fori_loop(0, BANDS, add, 0)
        for k in region:
            fs[k] = jnp.zeros((LEVP, 128), F32)

        def rows(at, carry):
            two_rows(HALO - step + 2 * at, region, c, u, v, m, fs, line0, line1, closed=True)
            return carry

        lax.fori_loop(0, (BANDS + 2 * step) // 2, rows, 0)

    fetch.wait()

    def merge(band, carry):
        base = band * (HALF * LEVP)
        spots, sums = [], []
        for k in range(HALO):
            share = c[band, HALO + k]
            for pair, keep in ((k, lower), (HALF - 1 - k, ~lower)):
                rows = pl.ds(pl.multiple_of(base + pair * LEVP, LEVP), LEVP)
                spots.append(rows)
                sums.append(full[rows] + jnp.where(keep, share, 0.0))
        for rows, value in zip(spots, sums):
            full[rows] = value
        return carry

    lax.fori_loop(0, TALL, merge, 0)

    left_lanes = lax.broadcasted_iota(jnp.int32, (8, 128), 1) < PROBES
    for group, (out, buffer) in enumerate(((own, got0), (far, got1), (near, got2))):

        def pick(at, carry):
            rows = buffer.at[pl.ds(pl.multiple_of(at * 128, 128), 128)]
            for k in range(128):
                rows[k : k + 1] = full[pl.ds(codes[group * 8 + at, k], 1)]
            return carry

        lax.fori_loop(0, SLOTS // 128, pick, 0)

        def join(at, carry):
            for k in range(16):
                at8 = pl.multiple_of(at * 128 + k * 8, 8)
                one, two = buffer[pl.ds(at8, 8)], buffer[pl.ds(at8 + SLOTS // 2, 8)]
                straight = jnp.where(left_lanes, one, two)
                crossed = pltpu.roll(jnp.where(left_lanes, two, one), PROBES, 1)
                out[pl.ds(at8, 8)] = jnp.where(turned[group, pl.ds(at8, 8)] > 0.5, crossed, straight)
            return carry

        lax.fori_loop(0, SLOTS // 256, join, 0)


def strips(odd, codes, turned, far, near, split, field):
    strip = pltpu.VMEM((TALL, 2 * HALO, LEVP, 128), F32)
    line = pltpu.VMEM((2 * HALO, LEVP, 128), F32)
    buffer = pltpu.VMEM((SLOTS, 128), F32)
    return pl.pallas_call(
        strips_kernel,
        in_specs=[whole(pltpu.SMEM), whole(pltpu.SMEM), whole(), whole(), whole(), whole(), whole(pl.ANY)],
        out_specs=[whole()] * 3,
        out_shape=[jax.ShapeDtypeStruct((SLOTS // 2, 128), F32)] * 3,
        scratch_shapes=[
            strip,
            strip,
            strip,
            strip,
            line,
            line,
            line,
            pltpu.VMEM((BANDS, HALO, 8, 128), F32),
            pltpu.VMEM((FIELD_ROWS + 8, 128), F32),
            buffer,
            buffer,
            buffer,
            pltpu.SemaphoreType.DMA,
        ],
        compiler_params=params(56),
        name="strips",
    )(odd, codes, turned, far, near, split, field)


def gram_kernel(own, far, near, weight, images, gram):
    rows = (own[...] + far[...] + near[...]) * weight[...]
    images[...] = rows
    both = lax.dot_general(
        rows, rows, (((0,), (0,)), ((), ())), precision=HIGHEST, preferred_element_type=F32
    )
    total = both[:PROBES, :PROBES] + both[PROBES:, PROBES:]
    gram[:, 0:PROBES] = total[: PROBES // 2]
    gram[:, PROBES:] = total[PROBES // 2 :]


def gram_of(own, far, near, weight):
    return pl.pallas_call(
        gram_kernel,
        in_specs=[whole()] * 4,
        out_specs=[whole()] * 2,
        out_shape=[
            jax.ShapeDtypeStruct((SLOTS // 2, 128), F32),
            jax.ShapeDtypeStruct((PROBES // 2, 128), F32),
        ],
        compiler_params=params(),
        name="gram",
    )(own, far, near, weight)


def factor_kernel(root, gram, images, basis_t, factor, work, pivots):
    sublane = lax.broadcasted_iota(jnp.int32, (8, 128), 0)
    half = PROBES // 2
    work[0:half, 0:PROBES] = gram[:, 0:PROBES]
    work[half:, 0:PROBES] = gram[:, PROBES:]
    diagonal = (
        lax.broadcasted_iota(jnp.int32, (PROBES, PROBES), 0)
        == lax.broadcasted_iota(jnp.int32, (PROBES, PROBES), 1)
    )
    work[:, PROBES:] = diagonal.astype(F32)
    tiles = [work[8 * t : 8 * t + 8] for t in range(PROBES // 8)]
    for first in range(0, PROBES, BLOCK):
        top = first // 8
        live = range(top, PROBES // 8)
        column = {
            (j, t): jnp.broadcast_to(tiles[t][:, first + j : first + j + 1], (8, 128))
            for j in range(BLOCK)
            for t in live
        }
        for j in range(BLOCK):
            at = first + j
            pick = lambda tile, n: jnp.broadcast_to(tile[n % 8 : n % 8 + 1], (8, 128))
            inverse = 1.0 / pick(column[j, top], at)
            pivots[at : at + 1] = column[j, top][at % 8 : at % 8 + 1]
            pivot = pick(tiles[top], at) * inverse
            later = [pick(column[j, top], first + i) * inverse for i in range(j + 1, BLOCK)]
            for t in live:
                share = column[j, t]
                if t == top:
                    share = jnp.where(sublane > at % 8, share, 0.0)
                tiles[t] = tiles[t] - share * pivot
                for i in range(j + 1, BLOCK):
                    column[i, t] = column[i, t] - share * later[i - j - 1]
    for t in range(PROBES // 8):
        rows = slice(8 * t, 8 * t + 8)
        work[rows] = tiles[t] * (1.0 / jnp.sqrt(pivots[rows]))
    both = work[...]
    row = lax.broadcasted_iota(jnp.int32, (PROBES, PROBES), 0)
    col = lax.broadcasted_iota(jnp.int32, (PROBES, PROBES), 1)
    factor[...] = jnp.where(col >= row, both[:, :PROBES], 0.0) * (1.0 / root)
    inverse_t = jnp.where(col <= row, both[:, PROBES:], 0.0) * root
    zero = jnp.zeros((PROBES, PROBES), F32)
    twice = jnp.concatenate(
        [
            jnp.concatenate([inverse_t, zero], axis=1),
            jnp.concatenate([zero, inverse_t], axis=1),
        ],
        axis=0,
    )
    basis = lax.dot_general(
        twice, images[...], (((1,), (1,)), ((), ())), precision=HIGHEST, preferred_element_type=F32
    )
    basis_t[:, 0 : SLOTS // 2] = basis[:PROBES]
    basis_t[:, SLOTS // 2 :] = basis[PROBES:]


def factor_of(gram, images, root):
    return pl.pallas_call(
        lambda *refs: factor_kernel(root, *refs),
        in_specs=[whole()] * 2,
        out_specs=[whole()] * 2,
        out_shape=[
            jax.ShapeDtypeStruct((PROBES, SLOTS), F32),
            jax.ShapeDtypeStruct((PROBES, PROBES), F32),
        ],
        scratch_shapes=[pltpu.VMEM((PROBES, 128), F32)] * 2,
        compiler_params=params(),
        name="factor",
    )(gram, images)


def on_device(
    flux_probes, conc_start, u_courant, v_courant, vert_mix, obs_cell, obs_weight, obs_count
):
    odd = (lax.axis_index("lat") % 2 + 2 * (lax.axis_index("lon") % 2)).astype(jnp.int32).reshape(1)
    to_far, to_near, own_west, own_east = pack_lat(odd, u_courant, v_courant, vert_mix, obs_cell)
    from_far = swap(to_far, "lat", True)
    from_near = swap(to_near, "lat", False)
    edges = pack_edges(odd, conc_start, flux_probes)
    own_west, own_east, *edges = lax.optimization_barrier((own_west, own_east, *edges))
    lon_far, lon_near = pack_lon(odd, own_west, own_east, from_far, from_near)
    lon_far = swap(lon_far, "lon", True, wrap=True)
    lon_near = swap(lon_near, "lon", False)
    gains, coef, codes, turned = prepare(
        odd, flux_probes, u_courant, v_courant, vert_mix, from_far, from_near, obs_cell
    )
    edge_far, edge_near, coef, lon_far, lon_near = lax.optimization_barrier(
        (*edges, coef, lon_far, lon_near)
    )
    edge_far = swap(edge_far, "lon", True, wrap=True)
    edge_near = swap(edge_near, "lon", False)
    field, split = transport(odd, conc_start, gains, coef, lon_far, lon_near)
    rows, for_far, for_near = strips(
        odd, codes, turned, edge_far, edge_near, split, field.reshape(FIELD_ROWS, 128)
    )
    far_rows = swap(for_far, "lat", True)
    near_rows = swap(for_near, "lat", False)
    live = jnp.arange(SLOTS, dtype=jnp.int32) < obs_count[0]
    scale = jnp.where(live, obs_weight, 0.0)
    lanes = (SLOTS // 2, PROBES)
    weight = jnp.concatenate(
        [
            jnp.broadcast_to(scale[: SLOTS // 2, None], lanes),
            jnp.broadcast_to(scale[SLOTS // 2 :, None], lanes),
        ],
        axis=1,
    )
    images, gram = gram_of(rows, far_rows, near_rows, weight)
    gram = all_sum(gram)
    total_rows = SLOTS * lax.axis_size("lon") * lax.axis_size("lat")
    basis_t, factor = factor_of(gram, images, float(total_rows) ** 0.5)
    return basis_t.T, factor


def solution(mesh):
    in_specs = (
        P("lat", "lon", None),
        P("lat", "lon", None, None),
        P("lat", "lon", None),
        P("lat", "lon", None),
        P("lat", "lon", None),
        P(("lon", "lat")),
        P(("lon", "lat")),
        P(("lon", "lat")),
    )
    out_specs = (P(("lon", "lat"), None), P())
    return jax.shard_map(
        on_device, mesh=mesh, in_specs=in_specs, out_specs=out_specs, check_vma=False
    )
```

```python
import jax
import jax.numpy as jnp
from jax import lax
from jax.experimental import pallas as pl
from jax.experimental.pallas import tpu as pltpu
from jax.sharding import PartitionSpec as P

STEPS = 4
BANDS, COLS, LEVS, PROBES = 12, 36, 47, 64
HALO = STEPS
TALL = BANDS + 2 * HALO
WIDE = COLS + 2 * HALO
LEVP = 48
TILES = LEVP // 8
COLP = 40
RING = 6
BLOCK = 8
LAT_ROWS = 3 * (HALO // 2) * COLP
LON_BANDS = TALL // 2
HALF = COLS // 2
PAIRS = HALF + 2 * HALO
SLOTS = 1024
FIELD_ROWS = TALL * HALF * LEVP
ZERO_ROW = FIELD_ROWS
F32 = jnp.float32
HIGHEST = lax.Precision.HIGHEST
MIB = 1024 * 1024


def params(mib=12):
    return pltpu.CompilerParams(vmem_limit_bytes=mib * MIB)


def whole(space=pltpu.VMEM):
    return pl.BlockSpec(memory_space=space)


def swap(x, axis, apart, wrap=False):
    size = lax.axis_size(axis)
    partner = [((i + 1) ^ 1) - 1 if apart else i ^ 1 for i in range(size)]
    if wrap:
        partner = [j % size for j in partner]
    return lax.ppermute(x, axis, [(i, j) for i, j in enumerate(partner) if 0 <= j < size])


def all_sum(x):
    lats = lax.axis_size("lat")
    size = lats * lax.axis_size("lon")
    for bits in ((1,), (2, 4), (2 * lats, 4 * lats), (lats, 8)):
        masks = [bits[0]] if len(bits) == 1 else [bits[0], bits[1], bits[0] | bits[1]]
        terms = [lax.ppermute(x, ("lon", "lat"), [(i, i ^ m) for i in range(size)]) for m in masks]
        for term in terms:
            x = x + term
    return x


def north_far(odd):
    return odd[0] & 1


def near_west(odd):
    return odd[0] >> 1


def lat_at(which, band):
    return (which * (HALO // 2) + band % (HALO // 2)) * COLP, 64 * (band // (HALO // 2))


def lon_at(band):
    place = band % LON_BANDS
    return place // 2, HALO * (place % 2), 64 * (band // LON_BANDS)


def pack_lat_kernel(odd, u, v, mix, cells, to_far, to_near, to_west, to_east):
    far = north_far(odd) * (BANDS - HALO)
    near = BANDS - HALO - far
    for which, ref in enumerate((u, v, mix)):
        for band in range(HALO):
            row, lane = lat_at(which, band)
            to_far[row : row + COLS, lane : lane + LEVS] = ref[far + band]
            to_near[row : row + COLS, lane : lane + LEVS] = ref[near + band]
        for band in range(BANDS):
            tile, row, lane = lon_at(band + HALO)
            for dst, col in ((to_west, 0), (to_east, COLS - HALO)):
                dst[which, tile, row : row + HALO, lane : lane + LEVS] = ref[band, col : col + HALO]
    for dst in (to_far, to_near):
        dst[LAT_ROWS:] = cells[...].astype(F32)


def pack_lat(odd, u, v, mix, cells):
    lat = jax.ShapeDtypeStruct((LAT_ROWS + 8, 128), F32)
    lon = jax.ShapeDtypeStruct((3, LON_BANDS // 2, 8, 128), F32)
    return pl.pallas_call(
        pack_lat_kernel,
        in_specs=[whole(pltpu.SMEM)] + [whole()] * 4,
        out_specs=[whole()] * 4,
        out_shape=[lat, lat, lon, lon],
        compiler_params=params(62),
        name="pack_lat",
    )(odd, u, v, mix, cells.reshape(8, 128))


def pack_lon_kernel(odd, west, east, far, near, to_far, to_near, edge_west, edge_east):
    far_north, west_near = north_far(odd) == 1, near_west(odd) == 1
    for src, dst, col in ((west, edge_west, 0), (east, edge_east, COLS - HALO)):
        dst[...] = src[...]
        for which in range(3):
            for edge in range(HALO):
                row, lane = lat_at(which, edge)
                ours = (slice(row + col, row + col + HALO), slice(lane, lane + LEVS))
                one, two = far[ours], near[ours]
                for rows, band in (
                    (jnp.where(far_north, two, one), edge),
                    (jnp.where(far_north, one, two), HALO + BANDS + edge),
                ):
                    tile, at, first = lon_at(band)
                    dst[which, tile, at : at + HALO, first : first + LEVS] = rows
    one, two = edge_west[...], edge_east[...]
    to_near[...] = jnp.where(west_near, one, two)
    to_far[...] = jnp.where(west_near, two, one)


def pack_lon(odd, west, east, far, near):
    out = jax.ShapeDtypeStruct(west.shape, F32)
    return pl.pallas_call(
        pack_lon_kernel,
        in_specs=[whole(pltpu.SMEM)] + [whole()] * 4,
        out_specs=[whole()] * 2,
        out_shape=[out, out],
        scratch_shapes=[pltpu.VMEM(west.shape, F32)] * 2,
        compiler_params=params(),
        name="pack_lon",
    )(odd, west, east, far, near)


def turn(dst, at, rows, flat, last_level):
    flat[0:LEVS, HALO : HALO + COLS] = rows.T
    if last_level:
        flat[LEVS - 1 : LEVS] = jnp.zeros((1, 128), F32)
    for tile in range(TILES):
        dst[at + (slice(8 * tile, 8 * tile + 8),)] = flat[pl.ds(tile, 8, stride=TILES)]


def two_terms(x, lane):
    high = x.astype(jnp.bfloat16).astype(F32)
    return jnp.where(lane < 64, high, x - high)


def level_tile(ref, at, tile):
    if tile < TILES - 1:
        return ref[at + (pl.ds(tile, 8, stride=TILES),)]
    part = ref[at + (pl.ds(tile, 7, stride=TILES),)]
    return jnp.concatenate([part, jnp.zeros((1, PROBES), F32)], axis=0)


def edges_kernel(odd, far, near, flux, u, v, mix, to_far, to_near, gains, coef, *flats):
    for dst, src, west in ((to_far, far, 1 - near_west(odd)), (to_near, near, near_west(odd))):
        first = (1 - west) * (COLS - HALO)

        def pack(at, carry):
            for band in (2 * at, 2 * at + 1):
                for k in range(2):
                    pair = jnp.concatenate([src[band, k], src[band, k + 2]], axis=1)
                    dst[band, k, 0:LEVS] = pair
                    col = first + k
                    gain = [flux[band, pl.ds(col, 1)], flux[band, pl.ds(col + 2, 1)]]
                    dst[band, k, LEVS:LEVP] = jnp.concatenate(gain, axis=1)
            return carry

        lax.fori_loop(0, BANDS // 2, pack, 0)
    high = HALF - HALO
    none = jnp.zeros((BANDS, HALO, PROBES), F32)
    gains[:, 0:HALO, 0:PROBES] = none
    gains[:, HALO:, 0:PROBES] = flux[:, 0 : HALF + HALO]
    gains[:, 0 : HALF + HALO, PROBES:] = flux[:, high:]
    gains[:, HALF + HALO :, PROBES:] = none
    for flat in flats:
        flat[...] = jnp.zeros((LEVP, 128), F32)
    for which, ref in enumerate((u, v, mix)):
        for band in range(BANDS):
            turn(coef, (which, band), ref[band], flats[band % 4], which == 2)
    split_all(coef, BANDS)


def split_all(coef, bands):
    lane = lax.broadcasted_iota(jnp.int32, (LEVP, 128), 1)

    def split(at, carry):
        for which in range(3):
            for k in range(4):
                x = coef[which, at * 4 + k]
                coef[which, at * 4 + k] = two_terms(x + pltpu.roll(x, 64, 1), lane)
        return carry

    lax.fori_loop(0, bands // 4, split, 0)


def pack_edges(odd, conc, flux, u, v, mix):
    out = jax.ShapeDtypeStruct((BANDS, 2, LEVP, 128), F32)
    last = COLS // HALO - 1
    shape = (BANDS, HALO, LEVS, PROBES)
    return pl.pallas_call(
        edges_kernel,
        grid_spec=pltpu.PrefetchScalarGridSpec(
            num_scalar_prefetch=1,
            grid=(1,),
            in_specs=[
                pl.BlockSpec(shape, lambda i, odd: (0, last * near_west(odd), 0, 0)),
                pl.BlockSpec(shape, lambda i, odd: (0, last * (1 - near_west(odd)), 0, 0)),
            ]
            + [whole()] * 4,
            out_specs=[whole()] * 4,
            scratch_shapes=[pltpu.VMEM((LEVP, 128), F32)] * 4,
        ),
        out_shape=[
            out,
            out,
            jax.ShapeDtypeStruct((BANDS, PAIRS, 128), F32),
            jax.ShapeDtypeStruct((3, BANDS, LEVP, 128), F32),
        ],
        compiler_params=params(62),
        name="pack_edges",
    )(odd, conc, conc, flux, u, v, mix)


def row_code(cells, shift):
    rest = ((cells.astype(F32) + 0.5) * (1.0 / LEVS)).astype(jnp.int32)
    level = cells - rest * LEVS
    line = ((rest.astype(F32) + 0.5) * (1.0 / COLS)).astype(jnp.int32)
    col = rest - line * COLS
    group = ((level.astype(F32) + 0.5) * (1.0 / TILES)).astype(jnp.int32)
    band = line + HALO + shift
    held = (band >= 0) & (band < TALL)
    upper = (col >= HALF).astype(jnp.int32)
    row = (band * HALF + col - HALF * upper) * LEVP + (level - group * TILES) * 8 + group
    later = lax.broadcasted_iota(jnp.int32, cells.shape, 0) * 128 >= SLOTS // 2
    cross = (upper == 1) != later
    return jnp.where(held, row, ZERO_ROW), cross.astype(F32)


def margins_kernel(odd, far, near, cells, coef, codes, turned, *flats):
    north = north_far(odd) * 2 - 1
    places = (
        (cells[...], 0),
        (far[LAT_ROWS:].astype(jnp.int32), BANDS * north),
        (near[LAT_ROWS:].astype(jnp.int32), -BANDS * north),
    )
    lower = lax.broadcasted_iota(jnp.int32, (128, 128), 1) < PROBES
    for group, (at, shift) in enumerate(places):
        row, cross = row_code(at, shift)
        codes[8 * group : 8 * group + 8] = row
        column = jnp.concatenate([cross, jnp.zeros((120, 128), F32)], axis=0).T
        for k in range(4):
            low = jnp.broadcast_to(column[:, k : k + 1], (128, 128))
            up = jnp.broadcast_to(column[:, k + 4 : k + 5], (128, 128))
            turned[group, 128 * k : 128 * k + 128] = jnp.where(lower, low, up)
    for flat in flats:
        flat[...] = jnp.zeros((LEVP, 128), F32)
    far_at = north_far(odd) * HALO
    near_at = HALO - far_at
    for which in range(3):
        for band in range(HALO):
            row, lane = lat_at(which, band)
            for k, (first, src) in enumerate(((far_at, far), (near_at, near))):
                rows = src[row : row + COLS, lane : lane + LEVS]
                turn(coef, (which, first + band), rows, flats[band % 2 * 2 + k], which == 2)
    split_all(coef, 2 * HALO)


def margins(odd, far, near, cells):
    return pl.pallas_call(
        margins_kernel,
        in_specs=[whole(pltpu.SMEM)] + [whole()] * 3,
        out_specs=[whole()] * 3,
        out_shape=[
            jax.ShapeDtypeStruct((3, 2 * HALO, LEVP, 128), F32),
            jax.ShapeDtypeStruct((24, 128), jnp.int32),
            jax.ShapeDtypeStruct((3, SLOTS // 2, 128), F32),
        ],
        scratch_shapes=[pltpu.VMEM((LEVP, 128), F32)] * 4,
        compiler_params=params(62),
        name="margins",
    )(odd, far, near, cells.reshape(8, 128))


def join_coef(odd, split, own, beyond, far, near, sides, flat):
    span = 5 * HALO
    lane = lax.broadcasted_iota(jnp.int32, (8, 128), 1)
    west_near = near_west(odd) == 1
    flat[...] = jnp.zeros((LEVP, 128), F32)
    for which in range(3):
        one, two = far[which].reshape(-1, 128), near[which].reshape(-1, 128)
        west = jnp.where(west_near, two, one).T
        east = jnp.where(west_near, one, two).T
        for group in range(4):
            levels = slice(64 * (group // 2), 64 * (group // 2) + LEVS)
            cols = slice(span * (group % 2), span * (group % 2) + span)
            for at, src in ((0, west), (HALO + COLS, east)):
                flat[0:LEVS, at : at + span] = src[levels, cols]
            if which == 2:
                flat[LEVS - 1 : LEVS] = jnp.zeros((1, 128), F32)
            for tile in range(TILES):
                x = flat[pl.ds(tile, 8, stride=TILES)]
                x = x + pltpu.roll(x, 64, 1)
                sides[which, group, 8 * tile : 8 * tile + 8] = two_terms(x, lane)
    column = lax.broadcasted_iota(jnp.int32, (LEVP, 128), 1) & 63
    margin = (column < HALO) | ((column >= HALO + COLS) & (column < WIDE))

    def join(band, ref, at):
        group = lax.div(band, 5)
        rows = pl.ds(pl.multiple_of(band * LEVP, LEVP), LEVP)
        for which in range(3):
            shift = lax.rem(128 - HALO * lax.rem(band, 5), 128)
            beside = pltpu.roll(sides[which, group], shift, 1)
            x = jnp.where(margin, beside, ref[which, at])
            split[which, rows] = x.astype(jnp.bfloat16)

    def inner(at, carry):
        for k in range(4):
            join(HALO + 4 * at + k, own, 4 * at + k)
        return carry

    def outer(at, carry):
        for k in range(HALO):
            join(at * (HALO + BANDS) + k, beyond, at * HALO + k)
        return carry

    lax.fori_loop(0, BANDS // 4, inner, 0)
    lax.fori_loop(0, 2, outer, 0)


def selector(tile, low, high, high_sign=1.0):
    shape = (128, 256)
    row = lax.broadcasted_iota(jnp.int32, shape, 0) & 63
    col = lax.broadcasted_iota(jnp.int32, shape, 1)
    pair = 2 * tile + (col >> 7)
    upper = ((col >> 6) & 1) == 1
    weight = jnp.where(upper, high_sign, 1.0)
    return jnp.where(row == jnp.where(upper, high(pair), low(pair)), weight, 0.0).astype(jnp.bfloat16)


def spread(ref, split, chosen, tile, first=0, count=TALL):
    out = jnp.dot(
        split[first * LEVP : (first + count) * LEVP], chosen, preferred_element_type=F32
    )
    out = out.reshape(count, 1, LEVP, 256)
    ref[first : first + count, pl.ds(2 * tile, 1)] = out[..., :128]
    ref[first : first + count, pl.ds(2 * tile + 1, 1)] = out[..., 128:]


def face_flux(speed, behind, ahead):
    return speed * jnp.where(speed > 0.0, behind, ahead)


def mix_levels(dst, line, mixing, at, pair):
    here = [line[pair, 8 * t : 8 * t + 8] for t in range(TILES)]
    above = here[1:] + [pltpu.roll(here[0], 7, 0)]
    moved = [
        mixing[at, pair, 8 * t : 8 * t + 8] * (above[t] - here[t]) for t in range(TILES)
    ]
    below = [pltpu.roll(moved[-1], 1, 0)] + moved[:-1]
    for t in range(TILES):
        dst[at, pair, 8 * t : 8 * t + 8] = here[t] + (moved[t] - below[t])


def two_rows(band, pairs, c, u, v, m, fs, line0, line1, closed=False):
    first, north = pairs[0], jnp.minimum(band + 2, TALL - 1)
    here0, here1 = c[band, first], c[band + 1, first]
    west0 = face_flux(u[band, first], c[band, first - 1], here0)
    west1 = face_flux(u[band + 1, first], c[band + 1, first - 1], here1)
    for pair in pairs:
        middle = face_flux(v[band + 1, pair], here0, here1)
        top = face_flux(v[north, pair], here1, c[north, pair])
        net0, net1 = here0 + west0, here1 + west1
        if not (closed and pair == pairs[-1]):
            ahead0, ahead1 = c[band, pair + 1], c[band + 1, pair + 1]
            west0 = face_flux(u[band, pair + 1], here0, ahead0)
            west1 = face_flux(u[band + 1, pair + 1], here1, ahead1)
            net0, net1 = net0 - west0, net1 - west1
            here0, here1 = ahead0, ahead1
        line0[pair] = net0 + (fs[pair] - middle)
        line1[pair] = net1 + (middle - top)
        fs[pair] = top
    for pair in pairs:
        mix_levels(c, line0, m, band, pair)
        mix_levels(c, line1, m, band + 1, pair)


def transport_kernel(
    odd, conc, flux, own, beyond, far, near, out, split,
    c, u, v, m, fs, line0, line1, sides, flat, stage, in_sem, out_sem,
):
    def fetch(band):
        slot = lax.rem(band, RING)
        return pltpu.make_async_copy(conc.at[band], stage.at[slot], in_sem.at[slot])

    for band in range(RING):
        fetch(band).start()
    join_coef(odd, split, own, beyond, far, near, sides, flat)

    def expand(tile):
        chosen = selector(tile, lambda pair: pair, lambda pair: pair + HALF)
        half = TALL // 2
        for which, ref in enumerate((u, v, m)):
            for first in (0, half):
                yield lambda: spread(ref, split.at[which], chosen, tile, first, half)

    zero = jnp.zeros((8, PROBES), F32)

    def load(band, carry):
        slot = lax.rem(band, RING)
        fetch(band).wait()
        pieces = expand(band)
        for pair in range(PAIRS):
            low, high = pair - HALO, pair - HALO + HALF
            for t in range(TILES):
                left = level_tile(stage, (slot, low), t) if low >= 0 else zero
                right = level_tile(stage, (slot, high), t) if high < COLS else zero
                both = jnp.concatenate([left, right], axis=1)
                c[band + HALO, pair, 8 * t : 8 * t + 8] = both
            if pair % 4 == 3:
                next(pieces)()

        @pl.when(band + RING < BANDS)
        def _():
            fetch(band + RING).start()

        return carry

    lax.fori_loop(0, BANDS, load, 0)
    for piece in expand(BANDS):
        piece()

    def clear(band, carry):
        c[band] = jnp.zeros((PAIRS, LEVP, 128), F32)
        c[band + HALO + BANDS] = jnp.zeros((PAIRS, LEVP, 128), F32)
        return carry

    lax.fori_loop(0, HALO, clear, 0)

    def save(band):
        return pltpu.make_async_copy(c.at[band, pl.ds(HALO, HALF)], out.at[band], out_sem.at[band])

    for step in range(1, STEPS + 1):
        first, last = step, PAIRS - step
        count = last - first

        def gain(band, carry):
            for pair in range(PAIRS):
                c[band + HALO, pair, 0:1] = c[band + HALO, pair, 0:1] + flux[band, pair : pair + 1]
            return carry

        lax.fori_loop(0, BANDS, gain, 0)
        fs[first:last] = jnp.zeros((count, LEVP, 128), F32)

        def rows(at, carry):
            band = HALO - step + 2 * at
            two_rows(band, range(first, last), c, u, v, m, fs, line0, line1)
            if step == STEPS:
                save(band).start()
                save(band + 1).start()
            return carry

        lax.fori_loop(0, (BANDS + 2 * step) // 2, rows, 0)

    def drain(band, carry):
        save(band).wait()
        return carry

    lax.fori_loop(0, TALL, drain, 0)


def transport(odd, conc, flux, own, beyond, far, near):
    field = pltpu.VMEM((TALL, PAIRS, LEVP, 128), F32)
    line = pltpu.VMEM((PAIRS, LEVP, 128), F32)
    return pl.pallas_call(
        transport_kernel,
        in_specs=[whole(pltpu.SMEM), whole(pl.ANY)] + [whole()] * 5,
        out_specs=[whole(pl.ANY), whole()],
        out_shape=[
            jax.ShapeDtypeStruct((TALL, HALF, LEVP, 128), F32),
            jax.ShapeDtypeStruct((3, TALL * LEVP, 128), jnp.bfloat16),
        ],
        scratch_shapes=[
            field,
            field,
            field,
            field,
            line,
            line,
            line,
            pltpu.VMEM((3, 4, LEVP, 128), F32),
            pltpu.VMEM((LEVP, 128), F32),
            pltpu.VMEM((RING, COLS, LEVS, PROBES), F32),
            pltpu.SemaphoreType.DMA((RING,)),
            pltpu.SemaphoreType.DMA((TALL,)),
        ],
        compiler_params=params(62),
        name="transport",
    )(odd, conc, flux, own, beyond, far, near)


def strips_kernel(
    odd, codes, turned, edge_far, edge_near, split, field, own, far, near,
    c, u, v, m, fs, line0, line1, gain, full, got0, got1, got2, sem,
):
    fetch = pltpu.make_async_copy(field, full.at[pl.ds(0, FIELD_ROWS)], sem)
    fetch.start()

    def expand(tile, carry):
        faces = selector(tile, lambda k: k, lambda k: WIDE - k, -1.0)
        cells = selector(tile, lambda k: k, lambda k: WIDE - 1 - k)
        for which, ref in enumerate((u, v, m)):
            spread(ref, split.at[which], cells if which else faces, tile)
        return carry

    lax.fori_loop(0, HALO, expand, 0)

    def clear(band, carry):
        c[band] = jnp.zeros((2 * HALO, LEVP, 128), F32)
        return carry

    lax.fori_loop(0, TALL, clear, 0)
    lower = lax.broadcasted_iota(jnp.int32, (LEVP, 128), 1) < PROBES
    inside = lax.broadcasted_iota(jnp.int32, (8, 128), 0) < 7
    low_lanes = lax.broadcasted_iota(jnp.int32, (8, 128), 1) < PROBES
    west_near = near_west(odd) == 1

    def place(band, carry):
        for k in range(2):
            for tile in range(TILES):
                rows = pl.ds(tile, 8, stride=TILES)
                one, two = edge_far[band, k, rows], edge_near[band, k, rows]
                three, four = edge_far[band, 1 - k, rows], edge_near[band, 1 - k, rows]
                left, right = jnp.where(west_near, two, one), jnp.where(west_near, three, four)
                outer = jnp.where(low_lanes, left, right)
                inner = pltpu.roll(jnp.where(low_lanes, right, left), PROBES, 1)
                for at, value in ((k, outer), (k + 2, inner)):
                    if tile == TILES - 1:
                        gain[band, at, 0:1] = value[7:8]
                        value = jnp.where(inside, value, 0.0)
                    c[band + HALO, at, 8 * tile : 8 * tile + 8] = value
        return carry

    lax.fori_loop(0, BANDS, place, 0)

    full[ZERO_ROW : ZERO_ROW + 8] = jnp.zeros((8, 128), F32)

    for step in range(1, STEPS + 1):
        region = range(step, step + HALO)

        def add(band, carry):
            for k in range(step - 1, HALO):
                c[band + HALO, k, 0:1] = c[band + HALO, k, 0:1] + gain[band, k, 0:1]
            return carry

        lax.fori_loop(0, BANDS, add, 0)
        for k in region:
            fs[k] = jnp.zeros((LEVP, 128), F32)

        def rows(at, carry):
            two_rows(HALO - step + 2 * at, region, c, u, v, m, fs, line0, line1, closed=True)
            return carry

        lax.fori_loop(0, (BANDS + 2 * step) // 2, rows, 0)

    fetch.wait()

    def merge(band, carry):
        base = band * (HALF * LEVP)
        spots, sums = [], []
        for k in range(HALO):
            share = c[band, HALO + k]
            for pair, keep in ((k, lower), (HALF - 1 - k, ~lower)):
                rows = pl.ds(pl.multiple_of(base + pair * LEVP, LEVP), LEVP)
                spots.append(rows)
                sums.append(full[rows] + jnp.where(keep, share, 0.0))
        for rows, value in zip(spots, sums):
            full[rows] = value
        return carry

    lax.fori_loop(0, TALL, merge, 0)

    half = SLOTS // 2
    left_lanes = lax.broadcasted_iota(jnp.int32, (8, 128), 1) < PROBES
    for group, (out, buffer) in enumerate(((own, got0), (far, got1), (near, got2))):

        def pick(at, carry):
            first = pl.multiple_of(at * 128, 128)
            rows = buffer.at[pl.ds(first, 128)], buffer.at[pl.ds(first + half, 128)]
            done = out.at[pl.ds(first, 128)]
            cross = turned.at[group, pl.ds(first, 128)]
            for tile in range(16):
                tiles = slice(8 * tile, 8 * tile + 8)
                for part in range(2):
                    for k in range(8 * tile, 8 * tile + 8):
                        place = codes[group * 8 + at + 4 * part, k]
                        rows[part][k : k + 1] = full[pl.ds(place, 1)]
                one, two = rows[0][tiles], rows[1][tiles]
                straight = jnp.where(left_lanes, one, two)
                crossed = pltpu.roll(jnp.where(left_lanes, two, one), PROBES, 1)
                done[tiles] = jnp.where(cross[tiles] > 0.5, crossed, straight)
            return carry

        lax.fori_loop(0, half // 128, pick, 0)


def strips(odd, codes, turned, far, near, split, field):
    strip = pltpu.VMEM((TALL, 2 * HALO, LEVP, 128), F32)
    line = pltpu.VMEM((2 * HALO, LEVP, 128), F32)
    buffer = pltpu.VMEM((SLOTS, 128), F32)
    return pl.pallas_call(
        strips_kernel,
        in_specs=[whole(pltpu.SMEM), whole(pltpu.SMEM), whole(), whole(), whole(), whole(), whole(pl.ANY)],
        out_specs=[whole()] * 3,
        out_shape=[jax.ShapeDtypeStruct((SLOTS // 2, 128), F32)] * 3,
        scratch_shapes=[
            strip,
            strip,
            strip,
            strip,
            line,
            line,
            line,
            pltpu.VMEM((BANDS, HALO, 8, 128), F32),
            pltpu.VMEM((FIELD_ROWS + 8, 128), F32),
            buffer,
            buffer,
            buffer,
            pltpu.SemaphoreType.DMA,
        ],
        compiler_params=params(56),
        name="strips",
    )(odd, codes, turned, far, near, split, field)


def gram_kernel(own, far, near, weight, images, gram):
    rows = own[...] + (far[...] + near[...]) * weight[...]
    images[...] = rows
    both = lax.dot_general(
        rows, rows, (((0,), (0,)), ((), ())), precision=HIGHEST, preferred_element_type=F32
    )
    total = both[:PROBES, :PROBES] + both[PROBES:, PROBES:]
    gram[:, 0:PROBES] = total[: PROBES // 2]
    gram[:, PROBES:] = total[PROBES // 2 :]


def gram_of(own, far, near, weight):
    return pl.pallas_call(
        gram_kernel,
        in_specs=[whole()] * 4,
        out_specs=[whole()] * 2,
        out_shape=[
            jax.ShapeDtypeStruct((SLOTS // 2, 128), F32),
            jax.ShapeDtypeStruct((PROBES // 2, 128), F32),
        ],
        compiler_params=params(),
        name="gram",
    )(own, far, near, weight)


def factor_kernel(root, gram, images, basis_t, factor, work, pivots):
    sublane = lax.broadcasted_iota(jnp.int32, (8, 128), 0)
    half = PROBES // 2
    work[0:half, 0:PROBES] = gram[:, 0:PROBES]
    work[half:, 0:PROBES] = gram[:, PROBES:]
    diagonal = (
        lax.broadcasted_iota(jnp.int32, (PROBES, PROBES), 0)
        == lax.broadcasted_iota(jnp.int32, (PROBES, PROBES), 1)
    )
    work[:, PROBES:] = diagonal.astype(F32)
    tiles = [work[8 * t : 8 * t + 8] for t in range(PROBES // 8)]
    for first in range(0, PROBES, BLOCK):
        top = first // 8
        live = range(top, PROBES // 8)
        column = {
            (j, t): jnp.broadcast_to(tiles[t][:, first + j : first + j + 1], (8, 128))
            for j in range(BLOCK)
            for t in live
        }
        for j in range(BLOCK):
            at = first + j
            pick = lambda tile, n: jnp.broadcast_to(tile[n % 8 : n % 8 + 1], (8, 128))
            inverse = 1.0 / pick(column[j, top], at)
            pivots[at : at + 1] = column[j, top][at % 8 : at % 8 + 1]
            pivot = pick(tiles[top], at) * inverse
            later = [pick(column[j, top], first + i) * inverse for i in range(j + 1, BLOCK)]
            for t in live:
                share = column[j, t]
                if t == top:
                    share = jnp.where(sublane > at % 8, share, 0.0)
                tiles[t] = tiles[t] - share * pivot
                for i in range(j + 1, BLOCK):
                    column[i, t] = column[i, t] - share * later[i - j - 1]
    for t in range(PROBES // 8):
        rows = slice(8 * t, 8 * t + 8)
        work[rows] = tiles[t] * (1.0 / jnp.sqrt(pivots[rows]))
    both = work[...]
    row = lax.broadcasted_iota(jnp.int32, (PROBES, PROBES), 0)
    col = lax.broadcasted_iota(jnp.int32, (PROBES, PROBES), 1)
    factor[...] = jnp.where(col >= row, both[:, :PROBES], 0.0) * (1.0 / root)
    inverse_t = jnp.where(col <= row, both[:, PROBES:], 0.0) * root
    zero = jnp.zeros((PROBES, PROBES), F32)
    twice = jnp.concatenate(
        [
            jnp.concatenate([inverse_t, zero], axis=1),
            jnp.concatenate([zero, inverse_t], axis=1),
        ],
        axis=0,
    )
    basis = lax.dot_general(
        twice, images[...], (((1,), (1,)), ((), ())), precision=HIGHEST, preferred_element_type=F32
    )
    basis_t[:, 0 : SLOTS // 2] = basis[:PROBES]
    basis_t[:, SLOTS // 2 :] = basis[PROBES:]


def factor_of(gram, images, root):
    return pl.pallas_call(
        lambda *refs: factor_kernel(root, *refs),
        in_specs=[whole()] * 2,
        out_specs=[whole()] * 2,
        out_shape=[
            jax.ShapeDtypeStruct((PROBES, SLOTS), F32),
            jax.ShapeDtypeStruct((PROBES, PROBES), F32),
        ],
        scratch_shapes=[pltpu.VMEM((PROBES, 128), F32)] * 2,
        compiler_params=params(),
        name="factor",
    )(gram, images)


def on_device(
    flux_probes, conc_start, u_courant, v_courant, vert_mix, obs_cell, obs_weight, obs_count
):
    odd = (lax.axis_index("lat") % 2 + 2 * (lax.axis_index("lon") % 2)).astype(jnp.int32).reshape(1)
    to_far, to_near, own_west, own_east = pack_lat(odd, u_courant, v_courant, vert_mix, obs_cell)
    from_far = swap(to_far, "lat", True)
    from_near = swap(to_near, "lat", False)
    *edges, gains, own = pack_edges(
        odd, conc_start, flux_probes, u_courant, v_courant, vert_mix
    )
    own_west, own_east, *edges = lax.optimization_barrier((own_west, own_east, *edges))
    lon_far, lon_near = pack_lon(odd, own_west, own_east, from_far, from_near)
    lon_far = swap(lon_far, "lon", True, wrap=True)
    lon_near = swap(lon_near, "lon", False)
    beyond, codes, turned = margins(odd, from_far, from_near, obs_cell)
    edge_far, edge_near, beyond, lon_far, lon_near = lax.optimization_barrier(
        (*edges, beyond, lon_far, lon_near)
    )
    edge_far = swap(edge_far, "lon", True, wrap=True)
    edge_near = swap(edge_near, "lon", False)
    field, split = transport(odd, conc_start, gains, own, beyond, lon_far, lon_near)
    rows, for_far, for_near = strips(
        odd, codes, turned, edge_far, edge_near, split, field.reshape(FIELD_ROWS, 128)
    )
    far_rows = swap(for_far, "lat", True)
    near_rows = swap(for_near, "lat", False)
    live = jnp.arange(SLOTS, dtype=jnp.int32) < obs_count[0]
    scale = jnp.where(live, obs_weight, 0.0)
    lanes = (SLOTS // 2, PROBES)
    weight = jnp.concatenate(
        [
            jnp.broadcast_to(scale[: SLOTS // 2, None], lanes),
            jnp.broadcast_to(scale[SLOTS // 2 :, None], lanes),
        ],
        axis=1,
    )
    images, gram = gram_of(rows * weight, far_rows, near_rows, weight)
    gram = all_sum(gram)
    total_rows = SLOTS * lax.axis_size("lon") * lax.axis_size("lat")
    basis_t, factor = factor_of(gram, images, float(total_rows) ** 0.5)
    return basis_t.T, factor


def solution(mesh):
    in_specs = (
        P("lat", "lon", None),
        P("lat", "lon", None, None),
        P("lat", "lon", None),
        P("lat", "lon", None),
        P("lat", "lon", None),
        P(("lon", "lat")),
        P(("lon", "lat")),
        P(("lon", "lat")),
    )
    out_specs = (P(("lon", "lat"), None), P())
    return jax.shard_map(
        on_device, mesh=mesh, in_specs=in_specs, out_specs=out_specs, check_vma=False
    )
```

```python
import jax
import jax.numpy as jnp
from jax import lax
from jax.experimental import pallas as pl
from jax.experimental.pallas import tpu as pltpu
from jax.sharding import PartitionSpec as P

STEPS = 4
BANDS, COLS, LEVS, PROBES = 12, 36, 47, 64
HALO = STEPS
TALL = BANDS + 2 * HALO
WIDE = COLS + 2 * HALO
LEVP = 48
TILES = LEVP // 8
COLP = 40
BLOCK = 8
LAT_ROWS = 3 * (HALO // 2) * COLP
LON_BANDS = TALL // 2
HALF = COLS // 2
SPILL = 2
PAIRS = SPILL + HALF
SLOTS = 1024
FIELD_ROWS = TALL * HALF * LEVP
ZERO_ROW = FIELD_ROWS
F32 = jnp.float32
HIGHEST = lax.Precision.HIGHEST
MIB = 1024 * 1024


def params(mib=12):
    return pltpu.CompilerParams(vmem_limit_bytes=mib * MIB)


def whole(space=pltpu.VMEM):
    return pl.BlockSpec(memory_space=space)


def swap(x, axis, apart, wrap=False):
    size = lax.axis_size(axis)
    partner = [((i + 1) ^ 1) - 1 if apart else i ^ 1 for i in range(size)]
    if wrap:
        partner = [j % size for j in partner]
    return lax.ppermute(x, axis, [(i, j) for i, j in enumerate(partner) if 0 <= j < size])


def all_sum(x):
    lats = lax.axis_size("lat")
    size = lats * lax.axis_size("lon")
    for bits in ((1,), (2, 4), (2 * lats, 4 * lats), (lats, 8)):
        masks = [bits[0]] if len(bits) == 1 else [bits[0], bits[1], bits[0] | bits[1]]
        terms = [lax.ppermute(x, ("lon", "lat"), [(i, i ^ m) for i in range(size)]) for m in masks]
        for term in terms:
            x = x + term
    return x


def north_far(odd):
    return odd[0] & 1


def near_west(odd):
    return odd[0] >> 1


def lat_at(which, band):
    return (which * (HALO // 2) + band % (HALO // 2)) * COLP, 64 * (band // (HALO // 2))


def lon_at(band):
    place = band % LON_BANDS
    return place // 2, HALO * (place % 2), 64 * (band // LON_BANDS)


def pack_lat_kernel(odd, u, v, mix, cells, to_far, to_near, to_west, to_east):
    far = north_far(odd) * (BANDS - HALO)
    near = BANDS - HALO - far
    for which, ref in enumerate((u, v, mix)):
        for band in range(HALO):
            row, lane = lat_at(which, band)
            to_far[row : row + COLS, lane : lane + LEVS] = ref[far + band]
            to_near[row : row + COLS, lane : lane + LEVS] = ref[near + band]
        for band in range(BANDS):
            tile, row, lane = lon_at(band + HALO)
            for dst, col in ((to_west, 0), (to_east, COLS - HALO)):
                dst[which, tile, row : row + HALO, lane : lane + LEVS] = ref[band, col : col + HALO]
    for dst in (to_far, to_near):
        dst[LAT_ROWS:] = cells[...].astype(F32)


def pack_lat(odd, u, v, mix, cells):
    lat = jax.ShapeDtypeStruct((LAT_ROWS + 8, 128), F32)
    lon = jax.ShapeDtypeStruct((3, LON_BANDS // 2, 8, 128), F32)
    return pl.pallas_call(
        pack_lat_kernel,
        in_specs=[whole(pltpu.SMEM)] + [whole()] * 4,
        out_specs=[whole()] * 4,
        out_shape=[lat, lat, lon, lon],
        compiler_params=params(62),
        name="pack_lat",
    )(odd, u, v, mix, cells.reshape(8, 128))


def pack_lon_kernel(odd, west, east, far, near, to_far, to_near, edge_west, edge_east):
    far_north, west_near = north_far(odd) == 1, near_west(odd) == 1
    for src, dst, col in ((west, edge_west, 0), (east, edge_east, COLS - HALO)):
        dst[...] = src[...]
        for which in range(3):
            for edge in range(HALO):
                row, lane = lat_at(which, edge)
                ours = (slice(row + col, row + col + HALO), slice(lane, lane + LEVS))
                one, two = far[ours], near[ours]
                for rows, band in (
                    (jnp.where(far_north, two, one), edge),
                    (jnp.where(far_north, one, two), HALO + BANDS + edge),
                ):
                    tile, at, first = lon_at(band)
                    dst[which, tile, at : at + HALO, first : first + LEVS] = rows
    one, two = edge_west[...], edge_east[...]
    to_near[...] = jnp.where(west_near, one, two)
    to_far[...] = jnp.where(west_near, two, one)


def pack_lon(odd, west, east, far, near):
    out = jax.ShapeDtypeStruct(west.shape, F32)
    return pl.pallas_call(
        pack_lon_kernel,
        in_specs=[whole(pltpu.SMEM)] + [whole()] * 4,
        out_specs=[whole()] * 2,
        out_shape=[out, out],
        scratch_shapes=[pltpu.VMEM(west.shape, F32)] * 2,
        compiler_params=params(),
        name="pack_lon",
    )(odd, west, east, far, near)


def turn(dst, at, rows, flat, last_level):
    flat[0:LEVS, HALO : HALO + COLS] = rows.T
    if last_level:
        flat[LEVS - 1 : LEVS] = jnp.zeros((1, 128), F32)
    for tile in range(TILES):
        dst[at + (slice(8 * tile, 8 * tile + 8),)] = flat[pl.ds(tile, 8, stride=TILES)]


def two_terms(x, lane):
    high = x.astype(jnp.bfloat16).astype(F32)
    return jnp.where(lane < 64, high, x - high)


def level_tile(ref, at, tile):
    if tile < TILES - 1:
        return ref[at + (pl.ds(tile, 8, stride=TILES),)]
    part = ref[at + (pl.ds(tile, 7, stride=TILES),)]
    return jnp.concatenate([part, jnp.zeros((1, PROBES), F32)], axis=0)


def edges_kernel(odd, far, near, flux, u, v, mix, to_far, to_near, gains, coef, *flats):
    for dst, src, west in ((to_far, far, 1 - near_west(odd)), (to_near, near, near_west(odd))):
        first = (1 - west) * (COLS - HALO)

        def pack(at, carry):
            for band in (2 * at, 2 * at + 1):
                for k in range(2):
                    pair = jnp.concatenate([src[band, k], src[band, k + 2]], axis=1)
                    dst[band, k, 0:LEVS] = pair
                    col = first + k
                    gain = [flux[band, pl.ds(col, 1)], flux[band, pl.ds(col + 2, 1)]]
                    dst[band, k, LEVS:LEVP] = jnp.concatenate(gain, axis=1)
            return carry

        lax.fori_loop(0, BANDS // 2, pack, 0)
    gains[:, :, 0:PROBES] = flux[:, :HALF]
    gains[:, :, PROBES:] = flux[:, HALF:]
    for flat in flats:
        flat[...] = jnp.zeros((LEVP, 128), F32)
    for which, ref in enumerate((u, v, mix)):
        for band in range(BANDS):
            turn(coef, (which, band), ref[band], flats[band % 4], which == 2)
    split_all(coef, BANDS)


def split_all(coef, bands):
    lane = lax.broadcasted_iota(jnp.int32, (LEVP, 128), 1)

    def split(at, carry):
        for which in range(3):
            for k in range(4):
                x = coef[which, at * 4 + k]
                coef[which, at * 4 + k] = two_terms(x + pltpu.roll(x, 64, 1), lane)
        return carry

    lax.fori_loop(0, bands // 4, split, 0)


def pack_edges(odd, conc, flux, u, v, mix):
    out = jax.ShapeDtypeStruct((BANDS, 2, LEVP, 128), F32)
    last = COLS // HALO - 1
    shape = (BANDS, HALO, LEVS, PROBES)
    return pl.pallas_call(
        edges_kernel,
        grid_spec=pltpu.PrefetchScalarGridSpec(
            num_scalar_prefetch=1,
            grid=(1,),
            in_specs=[
                pl.BlockSpec(shape, lambda i, odd: (0, last * near_west(odd), 0, 0)),
                pl.BlockSpec(shape, lambda i, odd: (0, last * (1 - near_west(odd)), 0, 0)),
            ]
            + [whole()] * 4,
            out_specs=[whole()] * 4,
            scratch_shapes=[pltpu.VMEM((LEVP, 128), F32)] * 4,
        ),
        out_shape=[
            out,
            out,
            jax.ShapeDtypeStruct((BANDS, HALF, 128), F32),
            jax.ShapeDtypeStruct((3, BANDS, LEVP, 128), F32),
        ],
        compiler_params=params(62),
        name="pack_edges",
    )(odd, conc, conc, flux, u, v, mix)


def row_code(cells, shift):
    rest = ((cells.astype(F32) + 0.5) * (1.0 / LEVS)).astype(jnp.int32)
    level = cells - rest * LEVS
    line = ((rest.astype(F32) + 0.5) * (1.0 / COLS)).astype(jnp.int32)
    col = rest - line * COLS
    group = ((level.astype(F32) + 0.5) * (1.0 / TILES)).astype(jnp.int32)
    band = line + HALO + shift
    held = (band >= 0) & (band < TALL)
    upper = (col >= HALF).astype(jnp.int32)
    row = (band * HALF + col - HALF * upper) * LEVP + (level - group * TILES) * 8 + group
    later = lax.broadcasted_iota(jnp.int32, cells.shape, 0) * 128 >= SLOTS // 2
    cross = (upper == 1) != later
    return jnp.where(held, row, ZERO_ROW), cross.astype(F32)


def margins_kernel(odd, far, near, cells, coef, codes, turned, *flats):
    north = north_far(odd) * 2 - 1
    places = (
        (cells[...], 0),
        (far[LAT_ROWS:].astype(jnp.int32), BANDS * north),
        (near[LAT_ROWS:].astype(jnp.int32), -BANDS * north),
    )
    lower = lax.broadcasted_iota(jnp.int32, (128, 128), 1) < PROBES
    for group, (at, shift) in enumerate(places):
        row, cross = row_code(at, shift)
        codes[8 * group : 8 * group + 8] = row
        column = jnp.concatenate([cross, jnp.zeros((120, 128), F32)], axis=0).T
        for k in range(4):
            low = jnp.broadcast_to(column[:, k : k + 1], (128, 128))
            up = jnp.broadcast_to(column[:, k + 4 : k + 5], (128, 128))
            turned[group, 128 * k : 128 * k + 128] = jnp.where(lower, low, up)
    for flat in flats:
        flat[...] = jnp.zeros((LEVP, 128), F32)
    far_at = north_far(odd) * HALO
    near_at = HALO - far_at
    for which in range(3):
        for band in range(HALO):
            row, lane = lat_at(which, band)
            for k, (first, src) in enumerate(((far_at, far), (near_at, near))):
                rows = src[row : row + COLS, lane : lane + LEVS]
                turn(coef, (which, first + band), rows, flats[band % 2 * 2 + k], which == 2)
    split_all(coef, 2 * HALO)


def margins(odd, far, near, cells):
    return pl.pallas_call(
        margins_kernel,
        in_specs=[whole(pltpu.SMEM)] + [whole()] * 3,
        out_specs=[whole()] * 3,
        out_shape=[
            jax.ShapeDtypeStruct((3, 2 * HALO, LEVP, 128), F32),
            jax.ShapeDtypeStruct((24, 128), jnp.int32),
            jax.ShapeDtypeStruct((3, SLOTS // 2, 128), F32),
        ],
        scratch_shapes=[pltpu.VMEM((LEVP, 128), F32)] * 4,
        compiler_params=params(62),
        name="margins",
    )(odd, far, near, cells.reshape(8, 128))


def join_coef(odd, split, own, beyond, far, near, sides, flat):
    span = 5 * HALO
    lane = lax.broadcasted_iota(jnp.int32, (8, 128), 1)
    west_near = near_west(odd) == 1
    flat[...] = jnp.zeros((LEVP, 128), F32)
    for which in range(3):
        one, two = far[which].reshape(-1, 128), near[which].reshape(-1, 128)
        west = jnp.where(west_near, two, one).T
        east = jnp.where(west_near, one, two).T
        for group in range(4):
            levels = slice(64 * (group // 2), 64 * (group // 2) + LEVS)
            cols = slice(span * (group % 2), span * (group % 2) + span)
            for at, src in ((0, west), (HALO + COLS, east)):
                flat[0:LEVS, at : at + span] = src[levels, cols]
            if which == 2:
                flat[LEVS - 1 : LEVS] = jnp.zeros((1, 128), F32)
            for tile in range(TILES):
                x = flat[pl.ds(tile, 8, stride=TILES)]
                x = x + pltpu.roll(x, 64, 1)
                sides[which, group, 8 * tile : 8 * tile + 8] = two_terms(x, lane)
    column = lax.broadcasted_iota(jnp.int32, (LEVP, 128), 1) & 63
    margin = (column < HALO) | ((column >= HALO + COLS) & (column < WIDE))

    def join(band, ref, at):
        group = lax.div(band, 5)
        rows = pl.ds(pl.multiple_of(band * LEVP, LEVP), LEVP)
        for which in range(3):
            shift = lax.rem(128 - HALO * lax.rem(band, 5), 128)
            beside = pltpu.roll(sides[which, group], shift, 1)
            x = jnp.where(margin, beside, ref[which, at])
            split[which, rows] = x.astype(jnp.bfloat16)

    def inner(at, carry):
        for k in range(4):
            join(HALO + 4 * at + k, own, 4 * at + k)
        return carry

    def outer(at, carry):
        for k in range(HALO):
            join(at * (HALO + BANDS) + k, beyond, at * HALO + k)
        return carry

    lax.fori_loop(0, BANDS // 4, inner, 0)
    lax.fori_loop(0, 2, outer, 0)


def selector(tile, low, high, high_sign=1.0):
    shape = (128, 256)
    row = lax.broadcasted_iota(jnp.int32, shape, 0) & 63
    col = lax.broadcasted_iota(jnp.int32, shape, 1)
    pair = 2 * tile + (col >> 7)
    upper = ((col >> 6) & 1) == 1
    weight = jnp.where(upper, high_sign, 1.0)
    return jnp.where(row == jnp.where(upper, high(pair), low(pair)), weight, 0.0).astype(jnp.bfloat16)


def spread(ref, split, chosen, tile, first=0, count=TALL):
    out = jnp.dot(
        split[first * LEVP : (first + count) * LEVP], chosen, preferred_element_type=F32
    )
    out = out.reshape(count, 1, LEVP, 256)
    ref[first : first + count, pl.ds(2 * tile, 1)] = out[..., :128]
    ref[first : first + count, pl.ds(2 * tile + 1, 1)] = out[..., 128:]


def face_flux(speed, behind, ahead):
    return speed * jnp.where(speed > 0.0, behind, ahead)


def mix_levels(dst, line, mixing, at, pair):
    here = [line[pair, 8 * t : 8 * t + 8] for t in range(TILES)]
    above = here[1:] + [pltpu.roll(here[0], 7, 0)]
    moved = [
        mixing[at, pair, 8 * t : 8 * t + 8] * (above[t] - here[t]) for t in range(TILES)
    ]
    below = [pltpu.roll(moved[-1], 1, 0)] + moved[:-1]
    for t in range(TILES):
        dst[at, pair, 8 * t : 8 * t + 8] = here[t] + (moved[t] - below[t])


def two_rows(band, pairs, c, u, v, m, fs, line0, line1, closed=False):
    first, north = pairs[0], jnp.minimum(band + 2, TALL - 1)
    here0, here1 = c[band, first], c[band + 1, first]
    west0 = face_flux(u[band, first], c[band, first - 1], here0)
    west1 = face_flux(u[band + 1, first], c[band + 1, first - 1], here1)
    for pair in pairs:
        middle = face_flux(v[band + 1, pair], here0, here1)
        top = face_flux(v[north, pair], here1, c[north, pair])
        net0, net1 = here0 + west0, here1 + west1
        if not (closed and pair == pairs[-1]):
            ahead0, ahead1 = c[band, pair + 1], c[band + 1, pair + 1]
            west0 = face_flux(u[band, pair + 1], here0, ahead0)
            west1 = face_flux(u[band + 1, pair + 1], here1, ahead1)
            net0, net1 = net0 - west0, net1 - west1
            here0, here1 = ahead0, ahead1
        line0[pair] = net0 + (fs[pair] - middle)
        line1[pair] = net1 + (middle - top)
        fs[pair] = top
    for pair in pairs:
        mix_levels(c, line0, m, band, pair)
        mix_levels(c, line1, m, band + 1, pair)


def block_rows(step, band, c, u, v, m, fs, line0, line1, last):
    north = jnp.minimum(band + 2, TALL - 1)
    lower = lax.broadcasted_iota(jnp.int32, (LEVP, 128), 1) < PROBES
    begin, end = SPILL, PAIRS - 1
    fluxes, spills = [], []
    for k in range(2):
        at = band + k
        far, near, head, tail = (c[at, place] for place in (0, 1, begin, end))
        into = face_flux(u[at, begin], jnp.where(lower, near, pltpu.roll(tail, PROBES, 1)), head)
        out = face_flux(u[at, 1], tail, jnp.where(lower, pltpu.roll(head, PROBES, 1), near))
        last[k] = out
        fluxes.append(into)
        if step < STEPS:
            outer = face_flux(
                u[at, 0], jnp.where(lower, far, near), jnp.where(lower, near, far)
            )
            net = {1: jnp.where(lower, outer - into, out - outer)}
            if step == 2:
                net[0] = jnp.where(lower, -outer, outer)
            spills.append(net)

    def advance(place, here0, here1, net0, net1):
        middle = face_flux(v[band + 1, place], here0, here1)
        top = face_flux(v[north, place], here1, c[north, place])
        line0[place] = net0 + (fs[place] - middle)
        line1[place] = net1 + (middle - top)
        fs[place] = top

    places = list(range(begin, PAIRS))
    if step < STEPS:
        for place in spills[0]:
            here0, here1 = c[band, place], c[band + 1, place]
            advance(place, here0, here1, here0 + spills[0][place], here1 + spills[1][place])
            places.append(place)
    here0, here1 = c[band, begin], c[band + 1, begin]
    west0, west1 = fluxes
    for place in range(begin, PAIRS):
        net0, net1 = here0 + west0, here1 + west1
        old0, old1 = here0, here1
        if place < end:
            here0, here1 = c[band, place + 1], c[band + 1, place + 1]
            west0 = face_flux(u[band, place + 1], old0, here0)
            west1 = face_flux(u[band + 1, place + 1], old1, here1)
        else:
            west0, west1 = last[0], last[1]
        advance(place, old0, old1, net0 - west0, net1 - west1)
    for place in places:
        mix_levels(c, line0, m, band, place)
        mix_levels(c, line1, m, band + 1, place)


def transport_kernel(
    odd, conc, flux, own, beyond, far, near, out, split,
    c, u, v, m, fs, line0, line1, last, sides, flat, stage, in_sem, out_sem,
):
    def fetch(band):
        return pltpu.make_async_copy(conc.at[band], stage.at[band], in_sem.at[band])

    for band in range(BANDS):
        fetch(band).start()
    join_coef(odd, split, own, beyond, far, near, sides, flat)

    def expand(tile):
        def cells(low, shift):
            outside = jnp.where(low == 1, HALO - 1 if not shift else HALO + COLS, HALO - 2 if not shift else HALO + COLS + 1)
            return jnp.where(low >= SPILL, low + HALO - SPILL + shift, outside)

        def faces(low, shift):
            outside = jnp.where(low == 1, HALO + HALF + shift, HALO - 1 if not shift else HALO + COLS + 1)
            return jnp.where(low >= SPILL, low + HALO - SPILL + shift, outside)

        at_faces = selector(tile, lambda p: faces(p, 0), lambda p: faces(p, HALF))
        at_cells = selector(tile, lambda p: cells(p, 0), lambda p: cells(p, HALF))
        half = TALL // 2
        for which, (ref, chosen) in enumerate(((u, at_faces), (v, at_cells), (m, at_cells))):
            for first in (0, half):
                yield lambda: spread(ref, split.at[which], chosen, tile, first, half)

    def load(band, pieces):
        fetch(band).wait()
        for pair in range(HALF):
            for t in range(TILES):
                both = [level_tile(stage, (band, col), t) for col in (pair, pair + HALF)]
                both = jnp.concatenate(both, axis=1)
                c[band + HALO, SPILL + pair, 8 * t : 8 * t + 8] = both
            if pieces is not None and pair % 3 == 2:
                next(pieces)()
        c[band + HALO, 0:SPILL] = jnp.zeros((SPILL, LEVP, 128), F32)

    def load_and_expand(band, carry):
        load(band, expand(band))
        return carry

    def load_only(band, carry):
        load(band, None)
        return carry

    lax.fori_loop(0, PAIRS // 2, load_and_expand, 0)
    lax.fori_loop(PAIRS // 2, BANDS, load_only, 0)

    def clear(band, carry):
        c[band] = jnp.zeros((PAIRS, LEVP, 128), F32)
        c[band + HALO + BANDS] = jnp.zeros((PAIRS, LEVP, 128), F32)
        return carry

    lax.fori_loop(0, HALO, clear, 0)

    def save(band):
        return pltpu.make_async_copy(c.at[band, pl.ds(SPILL, HALF)], out.at[band], out_sem.at[band])

    for step in range(1, STEPS + 1):

        def gain(band, carry):
            for pair in range(HALF):
                at = SPILL + pair
                c[band + HALO, at, 0:1] = c[band + HALO, at, 0:1] + flux[band, pair : pair + 1]
            return carry

        lax.fori_loop(0, BANDS, gain, 0)
        fs[...] = jnp.zeros((PAIRS, LEVP, 128), F32)

        def rows(at, carry):
            band = HALO - step + 2 * at
            block_rows(step, band, c, u, v, m, fs, line0, line1, last)
            if step == STEPS:
                save(band).start()
                save(band + 1).start()
            return carry

        lax.fori_loop(0, (BANDS + 2 * step) // 2, rows, 0)

    def drain(band, carry):
        save(band).wait()
        return carry

    lax.fori_loop(0, TALL, drain, 0)


def transport(odd, conc, flux, own, beyond, far, near):
    field = pltpu.VMEM((TALL, PAIRS, LEVP, 128), F32)
    line = pltpu.VMEM((PAIRS, LEVP, 128), F32)
    return pl.pallas_call(
        transport_kernel,
        in_specs=[whole(pltpu.SMEM), whole(pl.ANY)] + [whole()] * 5,
        out_specs=[whole(pl.ANY), whole()],
        out_shape=[
            jax.ShapeDtypeStruct((TALL, HALF, LEVP, 128), F32),
            jax.ShapeDtypeStruct((3, TALL * LEVP, 128), jnp.bfloat16),
        ],
        scratch_shapes=[
            field,
            field,
            field,
            field,
            line,
            line,
            line,
            pltpu.VMEM((2, LEVP, 128), F32),
            pltpu.VMEM((3, 4, LEVP, 128), F32),
            pltpu.VMEM((LEVP, 128), F32),
            pltpu.VMEM((BANDS, COLS, LEVS, PROBES), F32),
            pltpu.SemaphoreType.DMA((BANDS,)),
            pltpu.SemaphoreType.DMA((TALL,)),
        ],
        compiler_params=params(62),
        name="transport",
    )(odd, conc, flux, own, beyond, far, near)


def strips_kernel(
    odd, codes, turned, edge_far, edge_near, split, field, own, far, near,
    c, u, v, m, fs, line0, line1, gain, full, got0, got1, got2, sem,
):
    fetch = pltpu.make_async_copy(field, full.at[pl.ds(0, FIELD_ROWS)], sem)
    fetch.start()

    def expand(tile, carry):
        faces = selector(tile, lambda k: k, lambda k: WIDE - k, -1.0)
        cells = selector(tile, lambda k: k, lambda k: WIDE - 1 - k)
        for which, ref in enumerate((u, v, m)):
            spread(ref, split.at[which], cells if which else faces, tile)
        return carry

    lax.fori_loop(0, HALO, expand, 0)

    def clear(band, carry):
        c[band] = jnp.zeros((2 * HALO, LEVP, 128), F32)
        return carry

    lax.fori_loop(0, TALL, clear, 0)
    lower = lax.broadcasted_iota(jnp.int32, (LEVP, 128), 1) < PROBES
    inside = lax.broadcasted_iota(jnp.int32, (8, 128), 0) < 7
    low_lanes = lax.broadcasted_iota(jnp.int32, (8, 128), 1) < PROBES
    west_near = near_west(odd) == 1

    def place(band, carry):
        for k in range(2):
            for tile in range(TILES):
                rows = pl.ds(tile, 8, stride=TILES)
                one, two = edge_far[band, k, rows], edge_near[band, k, rows]
                three, four = edge_far[band, 1 - k, rows], edge_near[band, 1 - k, rows]
                left, right = jnp.where(west_near, two, one), jnp.where(west_near, three, four)
                outer = jnp.where(low_lanes, left, right)
                inner = pltpu.roll(jnp.where(low_lanes, right, left), PROBES, 1)
                for at, value in ((k, outer), (k + 2, inner)):
                    if tile == TILES - 1:
                        gain[band, at, 0:1] = value[7:8]
                        value = jnp.where(inside, value, 0.0)
                    c[band + HALO, at, 8 * tile : 8 * tile + 8] = value
        return carry

    lax.fori_loop(0, BANDS, place, 0)

    full[ZERO_ROW : ZERO_ROW + 8] = jnp.zeros((8, 128), F32)

    for step in range(1, STEPS + 1):
        region = range(step, step + HALO)

        def add(band, carry):
            for k in range(step - 1, HALO):
                c[band + HALO, k, 0:1] = c[band + HALO, k, 0:1] + gain[band, k, 0:1]
            return carry

        lax.fori_loop(0, BANDS, add, 0)
        for k in region:
            fs[k] = jnp.zeros((LEVP, 128), F32)

        def rows(at, carry):
            two_rows(HALO - step + 2 * at, region, c, u, v, m, fs, line0, line1, closed=True)
            return carry

        lax.fori_loop(0, (BANDS + 2 * step) // 2, rows, 0)

    fetch.wait()

    def merge(band, carry):
        base = band * (HALF * LEVP)
        spots, sums = [], []
        for k in range(HALO):
            share = c[band, HALO + k]
            for pair, keep in ((k, lower), (HALF - 1 - k, ~lower)):
                rows = pl.ds(pl.multiple_of(base + pair * LEVP, LEVP), LEVP)
                spots.append(rows)
                sums.append(full[rows] + jnp.where(keep, share, 0.0))
        for rows, value in zip(spots, sums):
            full[rows] = value
        return carry

    lax.fori_loop(0, TALL, merge, 0)

    half = SLOTS // 2
    left_lanes = lax.broadcasted_iota(jnp.int32, (8, 128), 1) < PROBES
    for group, (out, buffer) in enumerate(((own, got0), (far, got1), (near, got2))):

        def pick(at, carry):
            first = pl.multiple_of(at * 128, 128)
            rows = buffer.at[pl.ds(first, 128)], buffer.at[pl.ds(first + half, 128)]
            done = out.at[pl.ds(first, 128)]
            cross = turned.at[group, pl.ds(first, 128)]
            for tile in range(16):
                tiles = slice(8 * tile, 8 * tile + 8)
                for part in range(2):
                    for k in range(8 * tile, 8 * tile + 8):
                        place = codes[group * 8 + at + 4 * part, k]
                        rows[part][k : k + 1] = full[pl.ds(place, 1)]
                one, two = rows[0][tiles], rows[1][tiles]
                straight = jnp.where(left_lanes, one, two)
                crossed = pltpu.roll(jnp.where(left_lanes, two, one), PROBES, 1)
                done[tiles] = jnp.where(cross[tiles] > 0.5, crossed, straight)
            return carry

        lax.fori_loop(0, half // 128, pick, 0)


def strips(odd, codes, turned, far, near, split, field):
    strip = pltpu.VMEM((TALL, 2 * HALO, LEVP, 128), F32)
    line = pltpu.VMEM((2 * HALO, LEVP, 128), F32)
    buffer = pltpu.VMEM((SLOTS, 128), F32)
    return pl.pallas_call(
        strips_kernel,
        in_specs=[whole(pltpu.SMEM), whole(pltpu.SMEM), whole(), whole(), whole(), whole(), whole(pl.ANY)],
        out_specs=[whole()] * 3,
        out_shape=[jax.ShapeDtypeStruct((SLOTS // 2, 128), F32)] * 3,
        scratch_shapes=[
            strip,
            strip,
            strip,
            strip,
            line,
            line,
            line,
            pltpu.VMEM((BANDS, HALO, 8, 128), F32),
            pltpu.VMEM((FIELD_ROWS + 8, 128), F32),
            buffer,
            buffer,
            buffer,
            pltpu.SemaphoreType.DMA,
        ],
        compiler_params=params(56),
        name="strips",
    )(odd, codes, turned, far, near, split, field)


def gram_kernel(own, far, near, weight, images, gram):
    rows = own[...] + (far[...] + near[...]) * weight[...]
    images[...] = rows
    both = lax.dot_general(
        rows, rows, (((0,), (0,)), ((), ())), precision=HIGHEST, preferred_element_type=F32
    )
    total = both[:PROBES, :PROBES] + both[PROBES:, PROBES:]
    gram[:, 0:PROBES] = total[: PROBES // 2]
    gram[:, PROBES:] = total[PROBES // 2 :]


def gram_of(own, far, near, weight):
    return pl.pallas_call(
        gram_kernel,
        in_specs=[whole()] * 4,
        out_specs=[whole()] * 2,
        out_shape=[
            jax.ShapeDtypeStruct((SLOTS // 2, 128), F32),
            jax.ShapeDtypeStruct((PROBES // 2, 128), F32),
        ],
        compiler_params=params(),
        name="gram",
    )(own, far, near, weight)


def factor_kernel(root, gram, images, basis_t, factor, work, pivots):
    sublane = lax.broadcasted_iota(jnp.int32, (8, 128), 0)
    half = PROBES // 2
    work[0:half, 0:PROBES] = gram[:, 0:PROBES]
    work[half:, 0:PROBES] = gram[:, PROBES:]
    diagonal = (
        lax.broadcasted_iota(jnp.int32, (PROBES, PROBES), 0)
        == lax.broadcasted_iota(jnp.int32, (PROBES, PROBES), 1)
    )
    work[:, PROBES:] = diagonal.astype(F32)
    tiles = [work[8 * t : 8 * t + 8] for t in range(PROBES // 8)]
    for first in range(0, PROBES, BLOCK):
        top = first // 8
        live = range(top, PROBES // 8)
        column = {
            (j, t): jnp.broadcast_to(tiles[t][:, first + j : first + j + 1], (8, 128))
            for j in range(BLOCK)
            for t in live
        }
        for j in range(BLOCK):
            at = first + j
            pick = lambda tile, n: jnp.broadcast_to(tile[n % 8 : n % 8 + 1], (8, 128))
            inverse = 1.0 / pick(column[j, top], at)
            pivots[at : at + 1] = column[j, top][at % 8 : at % 8 + 1]
            pivot = pick(tiles[top], at) * inverse
            later = [pick(column[j, top], first + i) * inverse for i in range(j + 1, BLOCK)]
            for t in live:
                share = column[j, t]
                if t == top:
                    share = jnp.where(sublane > at % 8, share, 0.0)
                tiles[t] = tiles[t] - share * pivot
                for i in range(j + 1, BLOCK):
                    column[i, t] = column[i, t] - share * later[i - j - 1]
    for t in range(PROBES // 8):
        rows = slice(8 * t, 8 * t + 8)
        work[rows] = tiles[t] * (1.0 / jnp.sqrt(pivots[rows]))
    both = work[...]
    row = lax.broadcasted_iota(jnp.int32, (PROBES, PROBES), 0)
    col = lax.broadcasted_iota(jnp.int32, (PROBES, PROBES), 1)
    factor[...] = jnp.where(col >= row, both[:, :PROBES], 0.0) * (1.0 / root)
    inverse_t = jnp.where(col <= row, both[:, PROBES:], 0.0) * root
    zero = jnp.zeros((PROBES, PROBES), F32)
    twice = jnp.concatenate(
        [
            jnp.concatenate([inverse_t, zero], axis=1),
            jnp.concatenate([zero, inverse_t], axis=1),
        ],
        axis=0,
    )
    basis = lax.dot_general(
        twice, images[...], (((1,), (1,)), ((), ())), precision=HIGHEST, preferred_element_type=F32
    )
    basis_t[:, 0 : SLOTS // 2] = basis[:PROBES]
    basis_t[:, SLOTS // 2 :] = basis[PROBES:]


def factor_of(gram, images, root):
    return pl.pallas_call(
        lambda *refs: factor_kernel(root, *refs),
        in_specs=[whole()] * 2,
        out_specs=[whole()] * 2,
        out_shape=[
            jax.ShapeDtypeStruct((PROBES, SLOTS), F32),
            jax.ShapeDtypeStruct((PROBES, PROBES), F32),
        ],
        scratch_shapes=[pltpu.VMEM((PROBES, 128), F32)] * 2,
        compiler_params=params(),
        name="factor",
    )(gram, images)


def on_device(
    flux_probes, conc_start, u_courant, v_courant, vert_mix, obs_cell, obs_weight, obs_count
):
    odd = (lax.axis_index("lat") % 2 + 2 * (lax.axis_index("lon") % 2)).astype(jnp.int32).reshape(1)
    to_far, to_near, own_west, own_east = pack_lat(odd, u_courant, v_courant, vert_mix, obs_cell)
    from_far = swap(to_far, "lat", True)
    from_near = swap(to_near, "lat", False)
    *edges, gains, own = pack_edges(
        odd, conc_start, flux_probes, u_courant, v_courant, vert_mix
    )
    own_west, own_east, *edges = lax.optimization_barrier((own_west, own_east, *edges))
    lon_far, lon_near = pack_lon(odd, own_west, own_east, from_far, from_near)
    lon_far = swap(lon_far, "lon", True, wrap=True)
    lon_near = swap(lon_near, "lon", False)
    beyond, codes, turned = margins(odd, from_far, from_near, obs_cell)
    edge_far, edge_near, beyond, lon_far, lon_near = lax.optimization_barrier(
        (*edges, beyond, lon_far, lon_near)
    )
    edge_far = swap(edge_far, "lon", True, wrap=True)
    edge_near = swap(edge_near, "lon", False)
    field, split = transport(odd, conc_start, gains, own, beyond, lon_far, lon_near)
    rows, for_far, for_near = strips(
        odd, codes, turned, edge_far, edge_near, split, field.reshape(FIELD_ROWS, 128)
    )
    far_rows = swap(for_far, "lat", True)
    near_rows = swap(for_near, "lat", False)
    live = jnp.arange(SLOTS, dtype=jnp.int32) < obs_count[0]
    scale = jnp.where(live, obs_weight, 0.0)
    lanes = (SLOTS // 2, PROBES)
    weight = jnp.concatenate(
        [
            jnp.broadcast_to(scale[: SLOTS // 2, None], lanes),
            jnp.broadcast_to(scale[SLOTS // 2 :, None], lanes),
        ],
        axis=1,
    )
    images, gram = gram_of(rows * weight, far_rows, near_rows, weight)
    gram = all_sum(gram)
    total_rows = SLOTS * lax.axis_size("lon") * lax.axis_size("lat")
    basis_t, factor = factor_of(gram, images, float(total_rows) ** 0.5)
    return basis_t.T, factor


def solution(mesh):
    in_specs = (
        P("lat", "lon", None),
        P("lat", "lon", None, None),
        P("lat", "lon", None),
        P("lat", "lon", None),
        P("lat", "lon", None),
        P(("lon", "lat")),
        P(("lon", "lat")),
        P(("lon", "lat")),
    )
    out_specs = (P(("lon", "lat"), None), P())
    return jax.shard_map(
        on_device, mesh=mesh, in_specs=in_specs, out_specs=out_specs, check_vma=False
    )
```

```python
import jax
import jax.numpy as jnp
from jax import lax
from jax.experimental import pallas as pl
from jax.experimental.pallas import tpu as pltpu
from jax.sharding import PartitionSpec as P

STEPS = 4
BANDS, COLS, LEVS, PROBES = 12, 36, 47, 64
HALO = STEPS
TALL = BANDS + 2 * HALO
WIDE = COLS + 2 * HALO
LEVP = 48
TILES = LEVP // 8
COLP = 40
BLOCK = 8
LAT_ROWS = 3 * (HALO // 2) * COLP
LON_BANDS = TALL // 2
HALF = COLS // 2
SPILL = 2
PAIRS = SPILL + HALF
SLOTS = 1024
FIELD_ROWS = TALL * HALF * LEVP
ZERO_ROW = FIELD_ROWS
F32 = jnp.float32
HIGHEST = lax.Precision.HIGHEST
MIB = 1024 * 1024


def params(mib=12):
    return pltpu.CompilerParams(vmem_limit_bytes=mib * MIB)


def whole(space=pltpu.VMEM):
    return pl.BlockSpec(memory_space=space)


def swap(x, axis, apart, wrap=False):
    size = lax.axis_size(axis)
    partner = [((i + 1) ^ 1) - 1 if apart else i ^ 1 for i in range(size)]
    if wrap:
        partner = [j % size for j in partner]
    return lax.ppermute(x, axis, [(i, j) for i, j in enumerate(partner) if 0 <= j < size])


def all_sum(x):
    lats = lax.axis_size("lat")
    size = lats * lax.axis_size("lon")
    for bits in ((1,), (2, 4), (2 * lats, 4 * lats), (lats, 8)):
        masks = [bits[0]] if len(bits) == 1 else [bits[0], bits[1], bits[0] | bits[1]]
        terms = [lax.ppermute(x, ("lon", "lat"), [(i, i ^ m) for i in range(size)]) for m in masks]
        for term in terms:
            x = x + term
    return x


def north_far(odd):
    return odd[0] & 1


def near_west(odd):
    return odd[0] >> 1


def lat_at(which, band):
    return (which * (HALO // 2) + band % (HALO // 2)) * COLP, 64 * (band // (HALO // 2))


def lon_at(band):
    place = band % LON_BANDS
    return place // 2, HALO * (place % 2), 64 * (band // LON_BANDS)


def pack_lat_kernel(odd, u, v, mix, cells, to_far, to_near, to_west, to_east):
    far = north_far(odd) * (BANDS - HALO)
    near = BANDS - HALO - far
    for which, ref in enumerate((u, v, mix)):
        for band in range(HALO):
            row, lane = lat_at(which, band)
            to_far[row : row + COLS, lane : lane + LEVS] = ref[far + band]
            to_near[row : row + COLS, lane : lane + LEVS] = ref[near + band]
        for band in range(BANDS):
            tile, row, lane = lon_at(band + HALO)
            for dst, col in ((to_west, 0), (to_east, COLS - HALO)):
                dst[which, tile, row : row + HALO, lane : lane + LEVS] = ref[band, col : col + HALO]
    for dst in (to_far, to_near):
        dst[LAT_ROWS:] = cells[...].astype(F32)


def pack_lat(odd, u, v, mix, cells):
    lat = jax.ShapeDtypeStruct((LAT_ROWS + 8, 128), F32)
    lon = jax.ShapeDtypeStruct((3, LON_BANDS // 2, 8, 128), F32)
    return pl.pallas_call(
        pack_lat_kernel,
        in_specs=[whole(pltpu.SMEM)] + [whole()] * 4,
        out_specs=[whole()] * 4,
        out_shape=[lat, lat, lon, lon],
        compiler_params=params(62),
        name="pack_lat",
    )(odd, u, v, mix, cells.reshape(8, 128))


def pack_lon_kernel(odd, west, east, far, near, to_far, to_near, edge_west, edge_east):
    far_north, west_near = north_far(odd) == 1, near_west(odd) == 1
    for src, dst, col in ((west, edge_west, 0), (east, edge_east, COLS - HALO)):
        dst[...] = src[...]
        for which in range(3):
            for edge in range(HALO):
                row, lane = lat_at(which, edge)
                ours = (slice(row + col, row + col + HALO), slice(lane, lane + LEVS))
                one, two = far[ours], near[ours]
                for rows, band in (
                    (jnp.where(far_north, two, one), edge),
                    (jnp.where(far_north, one, two), HALO + BANDS + edge),
                ):
                    tile, at, first = lon_at(band)
                    dst[which, tile, at : at + HALO, first : first + LEVS] = rows
    one, two = edge_west[...], edge_east[...]
    to_near[...] = jnp.where(west_near, one, two)
    to_far[...] = jnp.where(west_near, two, one)


def pack_lon(odd, west, east, far, near):
    out = jax.ShapeDtypeStruct(west.shape, F32)
    return pl.pallas_call(
        pack_lon_kernel,
        in_specs=[whole(pltpu.SMEM)] + [whole()] * 4,
        out_specs=[whole()] * 2,
        out_shape=[out, out],
        scratch_shapes=[pltpu.VMEM(west.shape, F32)] * 2,
        compiler_params=params(),
        name="pack_lon",
    )(odd, west, east, far, near)


def turn(dst, at, rows, flat, last_level):
    flat[0:LEVS, HALO : HALO + COLS] = rows.T
    if last_level:
        flat[LEVS - 1 : LEVS] = jnp.zeros((1, 128), F32)
    for tile in range(TILES):
        dst[at + (slice(8 * tile, 8 * tile + 8),)] = flat[pl.ds(tile, 8, stride=TILES)]


def two_terms(x, lane):
    high = x.astype(jnp.bfloat16).astype(F32)
    return jnp.where(lane < 64, high, x - high)


def level_tile(ref, at, tile):
    if tile < TILES - 1:
        return ref[at + (pl.ds(tile, 8, stride=TILES),)]
    part = ref[at + (pl.ds(tile, 7, stride=TILES),)]
    return jnp.concatenate([part, jnp.zeros((1, PROBES), F32)], axis=0)


def edges_kernel(odd, far, near, flux, u, v, mix, to_far, to_near, gains, coef, *flats):
    for dst, src, west in ((to_far, far, 1 - near_west(odd)), (to_near, near, near_west(odd))):
        first = (1 - west) * (COLS - HALO)

        def pack(at, carry):
            for band in (2 * at, 2 * at + 1):
                for k in range(2):
                    pair = jnp.concatenate([src[band, k], src[band, k + 2]], axis=1)
                    dst[band, k, 0:LEVS] = pair
                    col = first + k
                    gain = [flux[band, pl.ds(col, 1)], flux[band, pl.ds(col + 2, 1)]]
                    dst[band, k, LEVS:LEVP] = jnp.concatenate(gain, axis=1)
            return carry

        lax.fori_loop(0, BANDS // 2, pack, 0)
    gains[:, :, 0:PROBES] = flux[:, :HALF]
    gains[:, :, PROBES:] = flux[:, HALF:]
    for flat in flats:
        flat[...] = jnp.zeros((LEVP, 128), F32)
    for which, ref in enumerate((u, v, mix)):
        for band in range(BANDS):
            turn(coef, (which, band), ref[band], flats[band % 4], which == 2)
    split_all(coef, BANDS)


def split_all(coef, bands):
    lane = lax.broadcasted_iota(jnp.int32, (LEVP, 128), 1)

    def split(at, carry):
        for which in range(3):
            for k in range(4):
                x = coef[which, at * 4 + k]
                coef[which, at * 4 + k] = two_terms(x + pltpu.roll(x, 64, 1), lane)
        return carry

    lax.fori_loop(0, bands // 4, split, 0)


def pack_edges(odd, conc, flux, u, v, mix):
    out = jax.ShapeDtypeStruct((BANDS, 2, LEVP, 128), F32)
    last = COLS // HALO - 1
    shape = (BANDS, HALO, LEVS, PROBES)
    return pl.pallas_call(
        edges_kernel,
        grid_spec=pltpu.PrefetchScalarGridSpec(
            num_scalar_prefetch=1,
            grid=(1,),
            in_specs=[
                pl.BlockSpec(shape, lambda i, odd: (0, last * near_west(odd), 0, 0)),
                pl.BlockSpec(shape, lambda i, odd: (0, last * (1 - near_west(odd)), 0, 0)),
            ]
            + [whole()] * 4,
            out_specs=[whole()] * 4,
            scratch_shapes=[pltpu.VMEM((LEVP, 128), F32)] * 4,
        ),
        out_shape=[
            out,
            out,
            jax.ShapeDtypeStruct((BANDS, HALF, 128), F32),
            jax.ShapeDtypeStruct((3, BANDS, LEVP, 128), F32),
        ],
        compiler_params=params(62),
        name="pack_edges",
    )(odd, conc, conc, flux, u, v, mix)


def row_code(cells, shift):
    rest = ((cells.astype(F32) + 0.5) * (1.0 / LEVS)).astype(jnp.int32)
    level = cells - rest * LEVS
    line = ((rest.astype(F32) + 0.5) * (1.0 / COLS)).astype(jnp.int32)
    col = rest - line * COLS
    group = ((level.astype(F32) + 0.5) * (1.0 / TILES)).astype(jnp.int32)
    band = line + HALO + shift
    held = (band >= 0) & (band < TALL)
    upper = (col >= HALF).astype(jnp.int32)
    row = (band * HALF + col - HALF * upper) * LEVP + (level - group * TILES) * 8 + group
    later = lax.broadcasted_iota(jnp.int32, cells.shape, 0) * 128 >= SLOTS // 2
    cross = (upper == 1) != later
    return jnp.where(held, row, ZERO_ROW), cross.astype(F32)


def margins_kernel(odd, far, near, cells, coef, codes, turned, *flats):
    north = north_far(odd) * 2 - 1
    places = (
        (cells[...], 0),
        (far[LAT_ROWS:].astype(jnp.int32), BANDS * north),
        (near[LAT_ROWS:].astype(jnp.int32), -BANDS * north),
    )
    lower = lax.broadcasted_iota(jnp.int32, (128, 128), 1) < PROBES
    for group, (at, shift) in enumerate(places):
        row, cross = row_code(at, shift)
        codes[8 * group : 8 * group + 8] = row
        column = jnp.concatenate([cross, jnp.zeros((120, 128), F32)], axis=0).T
        for k in range(4):
            low = jnp.broadcast_to(column[:, k : k + 1], (128, 128))
            up = jnp.broadcast_to(column[:, k + 4 : k + 5], (128, 128))
            turned[group, 128 * k : 128 * k + 128] = jnp.where(lower, low, up)
    for flat in flats:
        flat[...] = jnp.zeros((LEVP, 128), F32)
    far_at = north_far(odd) * HALO
    near_at = HALO - far_at
    for which in range(3):
        for band in range(HALO):
            row, lane = lat_at(which, band)
            for k, (first, src) in enumerate(((far_at, far), (near_at, near))):
                rows = src[row : row + COLS, lane : lane + LEVS]
                turn(coef, (which, first + band), rows, flats[band % 2 * 2 + k], which == 2)
    split_all(coef, 2 * HALO)


def margins(odd, far, near, cells):
    return pl.pallas_call(
        margins_kernel,
        in_specs=[whole(pltpu.SMEM)] + [whole()] * 3,
        out_specs=[whole()] * 3,
        out_shape=[
            jax.ShapeDtypeStruct((3, 2 * HALO, LEVP, 128), F32),
            jax.ShapeDtypeStruct((24, 128), jnp.int32),
            jax.ShapeDtypeStruct((3, SLOTS // 2, 128), F32),
        ],
        scratch_shapes=[pltpu.VMEM((LEVP, 128), F32)] * 4,
        compiler_params=params(62),
        name="margins",
    )(odd, far, near, cells.reshape(8, 128))


def join_coef(odd, split, own, beyond, far, near, sides, flat):
    span = 5 * HALO
    lane = lax.broadcasted_iota(jnp.int32, (8, 128), 1)
    west_near = near_west(odd) == 1
    flat[...] = jnp.zeros((LEVP, 128), F32)
    for which in range(3):
        one, two = far[which].reshape(-1, 128), near[which].reshape(-1, 128)
        west = jnp.where(west_near, two, one).T
        east = jnp.where(west_near, one, two).T
        for group in range(4):
            levels = slice(64 * (group // 2), 64 * (group // 2) + LEVS)
            cols = slice(span * (group % 2), span * (group % 2) + span)
            for at, src in ((0, west), (HALO + COLS, east)):
                flat[0:LEVS, at : at + span] = src[levels, cols]
            if which == 2:
                flat[LEVS - 1 : LEVS] = jnp.zeros((1, 128), F32)
            for tile in range(TILES):
                x = flat[pl.ds(tile, 8, stride=TILES)]
                x = x + pltpu.roll(x, 64, 1)
                sides[which, group, 8 * tile : 8 * tile + 8] = two_terms(x, lane)
    column = lax.broadcasted_iota(jnp.int32, (LEVP, 128), 1) & 63
    margin = (column < HALO) | ((column >= HALO + COLS) & (column < WIDE))

    def join(band, ref, at):
        group = lax.div(band, 5)
        rows = pl.ds(pl.multiple_of(band * LEVP, LEVP), LEVP)
        for which in range(3):
            shift = lax.rem(128 - HALO * lax.rem(band, 5), 128)
            beside = pltpu.roll(sides[which, group], shift, 1)
            x = jnp.where(margin, beside, ref[which, at])
            split[which, rows] = x.astype(jnp.bfloat16)

    def inner(at, carry):
        for k in range(4):
            join(HALO + 4 * at + k, own, 4 * at + k)
        return carry

    def outer(at, carry):
        for k in range(HALO):
            join(at * (HALO + BANDS) + k, beyond, at * HALO + k)
        return carry

    lax.fori_loop(0, BANDS // 4, inner, 0)
    lax.fori_loop(0, 2, outer, 0)


def selector(tile, low, high, high_sign=1.0):
    shape = (128, 256)
    row = lax.broadcasted_iota(jnp.int32, shape, 0) & 63
    col = lax.broadcasted_iota(jnp.int32, shape, 1)
    pair = 2 * tile + (col >> 7)
    upper = ((col >> 6) & 1) == 1
    weight = jnp.where(upper, high_sign, 1.0)
    return jnp.where(row == jnp.where(upper, high(pair), low(pair)), weight, 0.0).astype(jnp.bfloat16)


def spread(ref, split, chosen, tile, first=0, count=TALL):
    out = jnp.dot(
        split[first * LEVP : (first + count) * LEVP], chosen, preferred_element_type=F32
    )
    out = out.reshape(count, 1, LEVP, 256)
    ref[first : first + count, pl.ds(2 * tile, 1)] = out[..., :128]
    ref[first : first + count, pl.ds(2 * tile + 1, 1)] = out[..., 128:]


def face_flux(speed, behind, ahead):
    return speed * jnp.where(speed > 0.0, behind, ahead)


def mix_levels(dst, line, mixing, at, pair):
    here = [line[pair, 8 * t : 8 * t + 8] for t in range(TILES)]
    above = here[1:] + [pltpu.roll(here[0], 7, 0)]
    moved = [
        mixing[at, pair, 8 * t : 8 * t + 8] * (above[t] - here[t]) for t in range(TILES)
    ]
    below = [pltpu.roll(moved[-1], 1, 0)] + moved[:-1]
    for t in range(TILES):
        dst[at, pair, 8 * t : 8 * t + 8] = here[t] + (moved[t] - below[t])


def two_rows(band, pairs, c, u, v, m, fs, line0, line1, closed=False):
    first, north = pairs[0], jnp.minimum(band + 2, TALL - 1)
    here0, here1 = c[band, first], c[band + 1, first]
    west0 = face_flux(u[band, first], c[band, first - 1], here0)
    west1 = face_flux(u[band + 1, first], c[band + 1, first - 1], here1)
    for pair in pairs:
        middle = face_flux(v[band + 1, pair], here0, here1)
        top = face_flux(v[north, pair], here1, c[north, pair])
        net0, net1 = here0 + west0, here1 + west1
        if not (closed and pair == pairs[-1]):
            ahead0, ahead1 = c[band, pair + 1], c[band + 1, pair + 1]
            west0 = face_flux(u[band, pair + 1], here0, ahead0)
            west1 = face_flux(u[band + 1, pair + 1], here1, ahead1)
            net0, net1 = net0 - west0, net1 - west1
            here0, here1 = ahead0, ahead1
        line0[pair] = net0 + (fs[pair] - middle)
        line1[pair] = net1 + (middle - top)
        fs[pair] = top
    for pair in pairs:
        mix_levels(c, line0, m, band, pair)
        mix_levels(c, line1, m, band + 1, pair)


def block_rows(step, band, c, u, v, m, fs, line0, line1, last):
    north = jnp.minimum(band + 2, TALL - 1)
    lower = lax.broadcasted_iota(jnp.int32, (LEVP, 128), 1) < PROBES
    begin, end = SPILL, PAIRS - 1
    fluxes, spills = [], []
    for k in range(2):
        at = band + k
        far, near, head, tail = (c[at, place] for place in (0, 1, begin, end))
        into = face_flux(u[at, begin], jnp.where(lower, near, pltpu.roll(tail, PROBES, 1)), head)
        out = face_flux(u[at, 1], tail, jnp.where(lower, pltpu.roll(head, PROBES, 1), near))
        last[k] = out
        fluxes.append(into)
        if step < STEPS:
            outer = face_flux(
                u[at, 0], jnp.where(lower, far, near), jnp.where(lower, near, far)
            )
            net = {1: jnp.where(lower, outer - into, out - outer)}
            if step == 2:
                net[0] = jnp.where(lower, -outer, outer)
            spills.append(net)

    def advance(place, here0, here1, net0, net1):
        middle = face_flux(v[band + 1, place], here0, here1)
        top = face_flux(v[north, place], here1, c[north, place])
        line0[place] = net0 + (fs[place] - middle)
        line1[place] = net1 + (middle - top)
        fs[place] = top

    places = list(range(begin, PAIRS))
    if step < STEPS:
        for place in spills[0]:
            here0, here1 = c[band, place], c[band + 1, place]
            advance(place, here0, here1, here0 + spills[0][place], here1 + spills[1][place])
            places.append(place)
    here0, here1 = c[band, begin], c[band + 1, begin]
    west0, west1 = fluxes
    for place in range(begin, PAIRS):
        net0, net1 = here0 + west0, here1 + west1
        old0, old1 = here0, here1
        if place < end:
            here0, here1 = c[band, place + 1], c[band + 1, place + 1]
            west0 = face_flux(u[band, place + 1], old0, here0)
            west1 = face_flux(u[band + 1, place + 1], old1, here1)
        else:
            west0, west1 = last[0], last[1]
        advance(place, old0, old1, net0 - west0, net1 - west1)
    for place in places:
        mix_levels(c, line0, m, band, place)
        mix_levels(c, line1, m, band + 1, place)


def transport_kernel(
    odd, conc, flux, own, beyond, far, near, out, split,
    c, u, v, m, fs, line0, line1, last, sides, flat, stage, in_sem, out_sem,
):
    def fetch(band):
        return pltpu.make_async_copy(conc.at[band], stage.at[band], in_sem.at[band])

    for band in range(BANDS):
        fetch(band).start()
    join_coef(odd, split, own, beyond, far, near, sides, flat)

    def expand(tile):
        def cells(low, shift):
            outside = jnp.where(low == 1, HALO - 1 if not shift else HALO + COLS, HALO - 2 if not shift else HALO + COLS + 1)
            return jnp.where(low >= SPILL, low + HALO - SPILL + shift, outside)

        def faces(low, shift):
            outside = jnp.where(low == 1, HALO + HALF + shift, HALO - 1 if not shift else HALO + COLS + 1)
            return jnp.where(low >= SPILL, low + HALO - SPILL + shift, outside)

        at_faces = selector(tile, lambda p: faces(p, 0), lambda p: faces(p, HALF))
        at_cells = selector(tile, lambda p: cells(p, 0), lambda p: cells(p, HALF))
        half = TALL // 2
        for which, (ref, chosen) in enumerate(((u, at_faces), (v, at_cells), (m, at_cells))):
            for first in (0, half):
                yield lambda: spread(ref, split.at[which], chosen, tile, first, half)

    def load(band, pieces):
        fetch(band).wait()
        for pair in range(HALF):
            for t in range(TILES):
                both = [level_tile(stage, (band, col), t) for col in (pair, pair + HALF)]
                both = jnp.concatenate(both, axis=1)
                c[band + HALO, SPILL + pair, 8 * t : 8 * t + 8] = both
            if pieces is not None and pair % 3 == 2:
                next(pieces)()
        c[band + HALO, 0:SPILL] = jnp.zeros((SPILL, LEVP, 128), F32)

    def load_and_expand(band, carry):
        load(band, expand(band))
        return carry

    def load_only(band, carry):
        load(band, None)
        return carry

    lax.fori_loop(0, PAIRS // 2, load_and_expand, 0)
    lax.fori_loop(PAIRS // 2, BANDS, load_only, 0)

    def clear(band, carry):
        c[band] = jnp.zeros((PAIRS, LEVP, 128), F32)
        c[band + HALO + BANDS] = jnp.zeros((PAIRS, LEVP, 128), F32)
        return carry

    lax.fori_loop(0, HALO, clear, 0)

    def save(band):
        return pltpu.make_async_copy(c.at[band, pl.ds(SPILL, HALF)], out.at[band], out_sem.at[band])

    for step in range(1, STEPS + 1):

        def gain(at, carry):
            for band in range(3):
                for pair in range(HALF):
                    spot = 3 * at + band + HALO, SPILL + pair, slice(0, 1)
                    c[spot] = c[spot] + flux[3 * at + band, pair : pair + 1]
            return carry

        lax.fori_loop(0, BANDS // 3, gain, 0)
        fs[...] = jnp.zeros((PAIRS, LEVP, 128), F32)

        def rows(at, carry):
            band = HALO - step + 2 * at
            block_rows(step, band, c, u, v, m, fs, line0, line1, last)
            if step == STEPS:
                save(band).start()
                save(band + 1).start()
            return carry

        lax.fori_loop(0, (BANDS + 2 * step) // 2, rows, 0)

    def drain(band, carry):
        save(band).wait()
        return carry

    lax.fori_loop(0, TALL, drain, 0)


def transport(odd, conc, flux, own, beyond, far, near):
    field = pltpu.VMEM((TALL, PAIRS, LEVP, 128), F32)
    line = pltpu.VMEM((PAIRS, LEVP, 128), F32)
    return pl.pallas_call(
        transport_kernel,
        in_specs=[whole(pltpu.SMEM), whole(pl.ANY)] + [whole()] * 5,
        out_specs=[whole(pl.ANY), whole()],
        out_shape=[
            jax.ShapeDtypeStruct((TALL, HALF, LEVP, 128), F32),
            jax.ShapeDtypeStruct((3, TALL * LEVP, 128), jnp.bfloat16),
        ],
        scratch_shapes=[
            field,
            field,
            field,
            field,
            line,
            line,
            line,
            pltpu.VMEM((2, LEVP, 128), F32),
            pltpu.VMEM((3, 4, LEVP, 128), F32),
            pltpu.VMEM((LEVP, 128), F32),
            pltpu.VMEM((BANDS, COLS, LEVS, PROBES), F32),
            pltpu.SemaphoreType.DMA((BANDS,)),
            pltpu.SemaphoreType.DMA((TALL,)),
        ],
        compiler_params=params(62),
        name="transport",
    )(odd, conc, flux, own, beyond, far, near)


def strips_kernel(
    odd, codes, turned, edge_far, edge_near, split, field, own, far, near,
    c, u, v, m, fs, line0, line1, gain, full, got0, got1, got2, sem,
):
    fetch = pltpu.make_async_copy(field, full.at[pl.ds(0, FIELD_ROWS)], sem)
    fetch.start()

    lower = lax.broadcasted_iota(jnp.int32, (LEVP, 128), 1) < PROBES
    inside = lax.broadcasted_iota(jnp.int32, (8, 128), 0) < 7
    low_lanes = lax.broadcasted_iota(jnp.int32, (8, 128), 1) < PROBES
    west_near = near_west(odd) == 1

    def place(band):
        for k in range(2):
            for tile in range(TILES):
                rows = pl.ds(tile, 8, stride=TILES)
                one, two = edge_far[band, k, rows], edge_near[band, k, rows]
                three, four = edge_far[band, 1 - k, rows], edge_near[band, 1 - k, rows]
                left, right = jnp.where(west_near, two, one), jnp.where(west_near, three, four)
                outer = jnp.where(low_lanes, left, right)
                inner = pltpu.roll(jnp.where(low_lanes, right, left), PROBES, 1)
                for at, value in ((k, outer), (k + 2, inner)):
                    if tile == TILES - 1:
                        gain[band, at, 0:1] = value[7:8]
                        value = jnp.where(inside, value, 0.0)
                    c[band + HALO, at, 8 * tile : 8 * tile + 8] = value

    def expand(tile, carry):
        faces = selector(tile, lambda k: k, lambda k: WIDE - k, -1.0)
        cells = selector(tile, lambda k: k, lambda k: WIDE - 1 - k)
        none = jnp.zeros((HALO, LEVP, 128), F32)
        for which, ref in enumerate((u, v, m)):
            spread(ref, split.at[which], cells if which else faces, tile)
            place(3 * tile + which)
        for k in range(TALL // 4):
            c[tile * (TALL // 4) + k, HALO:] = none
        c[tile, 0:HALO] = none
        c[tile + HALO + BANDS, 0:HALO] = none
        return carry

    lax.fori_loop(0, HALO, expand, 0)

    full[ZERO_ROW : ZERO_ROW + 8] = jnp.zeros((8, 128), F32)

    for step in range(1, STEPS + 1):
        region = range(step, step + HALO)

        def add(band, carry):
            for k in range(step - 1, HALO):
                c[band + HALO, k, 0:1] = c[band + HALO, k, 0:1] + gain[band, k, 0:1]
            return carry

        lax.fori_loop(0, BANDS, add, 0)
        for k in region:
            fs[k] = jnp.zeros((LEVP, 128), F32)

        def rows(at, carry):
            two_rows(HALO - step + 2 * at, region, c, u, v, m, fs, line0, line1, closed=True)
            return carry

        lax.fori_loop(0, (BANDS + 2 * step) // 2, rows, 0)

    fetch.wait()

    def merge(band, carry):
        base = band * (HALF * LEVP)
        spots, sums = [], []
        for k in range(HALO):
            share = c[band, HALO + k]
            for pair, keep in ((k, lower), (HALF - 1 - k, ~lower)):
                rows = pl.ds(pl.multiple_of(base + pair * LEVP, LEVP), LEVP)
                spots.append(rows)
                sums.append(full[rows] + jnp.where(keep, share, 0.0))
        for rows, value in zip(spots, sums):
            full[rows] = value
        return carry

    lax.fori_loop(0, TALL, merge, 0)

    half = SLOTS // 2
    left_lanes = lax.broadcasted_iota(jnp.int32, (8, 128), 1) < PROBES
    for group, (out, buffer) in enumerate(((own, got0), (far, got1), (near, got2))):

        def pick(at, carry):
            first = pl.multiple_of(at * 128, 128)
            rows = buffer.at[pl.ds(first, 128)], buffer.at[pl.ds(first + half, 128)]
            done = out.at[pl.ds(first, 128)]
            cross = turned.at[group, pl.ds(first, 128)]
            for tile in range(16):
                tiles = slice(8 * tile, 8 * tile + 8)
                for part in range(2):
                    for k in range(8 * tile, 8 * tile + 8):
                        place = codes[group * 8 + at + 4 * part, k]
                        rows[part][k : k + 1] = full[pl.ds(place, 1)]
                one, two = rows[0][tiles], rows[1][tiles]
                straight = jnp.where(left_lanes, one, two)
                crossed = pltpu.roll(jnp.where(left_lanes, two, one), PROBES, 1)
                done[tiles] = jnp.where(cross[tiles] > 0.5, crossed, straight)
            return carry

        lax.fori_loop(0, half // 128, pick, 0)


def strips(odd, codes, turned, far, near, split, field):
    strip = pltpu.VMEM((TALL, 2 * HALO, LEVP, 128), F32)
    line = pltpu.VMEM((2 * HALO, LEVP, 128), F32)
    buffer = pltpu.VMEM((SLOTS, 128), F32)
    return pl.pallas_call(
        strips_kernel,
        in_specs=[whole(pltpu.SMEM), whole(pltpu.SMEM), whole(), whole(), whole(), whole(), whole(pl.ANY)],
        out_specs=[whole()] * 3,
        out_shape=[jax.ShapeDtypeStruct((SLOTS // 2, 128), F32)] * 3,
        scratch_shapes=[
            strip,
            strip,
            strip,
            strip,
            line,
            line,
            line,
            pltpu.VMEM((BANDS, HALO, 8, 128), F32),
            pltpu.VMEM((FIELD_ROWS + 8, 128), F32),
            buffer,
            buffer,
            buffer,
            pltpu.SemaphoreType.DMA,
        ],
        compiler_params=params(56),
        name="strips",
    )(odd, codes, turned, far, near, split, field)


def gram_kernel(own, far, near, weight, images, gram):
    rows = own[...] + (far[...] + near[...]) * weight[...]
    images[...] = rows
    both = lax.dot_general(
        rows, rows, (((0,), (0,)), ((), ())), precision=HIGHEST, preferred_element_type=F32
    )
    total = both[:PROBES, :PROBES] + both[PROBES:, PROBES:]
    gram[:, 0:PROBES] = total[: PROBES // 2]
    gram[:, PROBES:] = total[PROBES // 2 :]


def gram_of(own, far, near, weight):
    return pl.pallas_call(
        gram_kernel,
        in_specs=[whole()] * 4,
        out_specs=[whole()] * 2,
        out_shape=[
            jax.ShapeDtypeStruct((SLOTS // 2, 128), F32),
            jax.ShapeDtypeStruct((PROBES // 2, 128), F32),
        ],
        compiler_params=params(),
        name="gram",
    )(own, far, near, weight)


def factor_kernel(root, gram, images, basis_t, factor, work, pivots):
    sublane = lax.broadcasted_iota(jnp.int32, (8, 128), 0)
    half = PROBES // 2
    work[0:half, 0:PROBES] = gram[:, 0:PROBES]
    work[half:, 0:PROBES] = gram[:, PROBES:]
    diagonal = (
        lax.broadcasted_iota(jnp.int32, (PROBES, PROBES), 0)
        == lax.broadcasted_iota(jnp.int32, (PROBES, PROBES), 1)
    )
    work[:, PROBES:] = diagonal.astype(F32)
    tiles = [work[8 * t : 8 * t + 8] for t in range(PROBES // 8)]
    for first in range(0, PROBES, BLOCK):
        top = first // 8
        live = range(top, PROBES // 8)
        column = {
            (j, t): jnp.broadcast_to(tiles[t][:, first + j : first + j + 1], (8, 128))
            for j in range(BLOCK)
            for t in live
        }
        for j in range(BLOCK):
            at = first + j
            pick = lambda tile, n: jnp.broadcast_to(tile[n % 8 : n % 8 + 1], (8, 128))
            inverse = 1.0 / pick(column[j, top], at)
            pivots[at : at + 1] = column[j, top][at % 8 : at % 8 + 1]
            pivot = pick(tiles[top], at) * inverse
            later = [pick(column[j, top], first + i) * inverse for i in range(j + 1, BLOCK)]
            for t in live:
                share = column[j, t]
                if t == top:
                    share = jnp.where(sublane > at % 8, share, 0.0)
                tiles[t] = tiles[t] - share * pivot
                for i in range(j + 1, BLOCK):
                    column[i, t] = column[i, t] - share * later[i - j - 1]
    for t in range(PROBES // 8):
        rows = slice(8 * t, 8 * t + 8)
        work[rows] = tiles[t] * (1.0 / jnp.sqrt(pivots[rows]))
    both = work[...]
    row = lax.broadcasted_iota(jnp.int32, (PROBES, PROBES), 0)
    col = lax.broadcasted_iota(jnp.int32, (PROBES, PROBES), 1)
    factor[...] = jnp.where(col >= row, both[:, :PROBES], 0.0) * (1.0 / root)
    inverse_t = jnp.where(col <= row, both[:, PROBES:], 0.0) * root
    zero = jnp.zeros((PROBES, PROBES), F32)
    twice = jnp.concatenate(
        [
            jnp.concatenate([inverse_t, zero], axis=1),
            jnp.concatenate([zero, inverse_t], axis=1),
        ],
        axis=0,
    )
    basis = lax.dot_general(
        twice, images[...], (((1,), (1,)), ((), ())), precision=HIGHEST, preferred_element_type=F32
    )
    basis_t[:, 0 : SLOTS // 2] = basis[:PROBES]
    basis_t[:, SLOTS // 2 :] = basis[PROBES:]


def factor_of(gram, images, root):
    return pl.pallas_call(
        lambda *refs: factor_kernel(root, *refs),
        in_specs=[whole()] * 2,
        out_specs=[whole()] * 2,
        out_shape=[
            jax.ShapeDtypeStruct((PROBES, SLOTS), F32),
            jax.ShapeDtypeStruct((PROBES, PROBES), F32),
        ],
        scratch_shapes=[pltpu.VMEM((PROBES, 128), F32)] * 2,
        compiler_params=params(),
        name="factor",
    )(gram, images)


def on_device(
    flux_probes, conc_start, u_courant, v_courant, vert_mix, obs_cell, obs_weight, obs_count
):
    odd = (lax.axis_index("lat") % 2 + 2 * (lax.axis_index("lon") % 2)).astype(jnp.int32).reshape(1)
    to_far, to_near, own_west, own_east = pack_lat(odd, u_courant, v_courant, vert_mix, obs_cell)
    from_far = swap(to_far, "lat", True)
    from_near = swap(to_near, "lat", False)
    *edges, gains, own = pack_edges(
        odd, conc_start, flux_probes, u_courant, v_courant, vert_mix
    )
    own_west, own_east, *edges = lax.optimization_barrier((own_west, own_east, *edges))
    lon_far, lon_near = pack_lon(odd, own_west, own_east, from_far, from_near)
    lon_far = swap(lon_far, "lon", True, wrap=True)
    lon_near = swap(lon_near, "lon", False)
    beyond, codes, turned = margins(odd, from_far, from_near, obs_cell)
    edge_far, edge_near, beyond, lon_far, lon_near = lax.optimization_barrier(
        (*edges, beyond, lon_far, lon_near)
    )
    edge_far = swap(edge_far, "lon", True, wrap=True)
    edge_near = swap(edge_near, "lon", False)
    field, split = transport(odd, conc_start, gains, own, beyond, lon_far, lon_near)
    rows, for_far, for_near = strips(
        odd, codes, turned, edge_far, edge_near, split, field.reshape(FIELD_ROWS, 128)
    )
    far_rows = swap(for_far, "lat", True)
    near_rows = swap(for_near, "lat", False)
    live = jnp.arange(SLOTS, dtype=jnp.int32) < obs_count[0]
    scale = jnp.where(live, obs_weight, 0.0)
    lanes = (SLOTS // 2, PROBES)
    weight = jnp.concatenate(
        [
            jnp.broadcast_to(scale[: SLOTS // 2, None], lanes),
            jnp.broadcast_to(scale[SLOTS // 2 :, None], lanes),
        ],
        axis=1,
    )
    images, gram = gram_of(rows * weight, far_rows, near_rows, weight)
    gram = all_sum(gram)
    total_rows = SLOTS * lax.axis_size("lon") * lax.axis_size("lat")
    basis_t, factor = factor_of(gram, images, float(total_rows) ** 0.5)
    return basis_t.T, factor


def solution(mesh):
    in_specs = (
        P("lat", "lon", None),
        P("lat", "lon", None, None),
        P("lat", "lon", None),
        P("lat", "lon", None),
        P("lat", "lon", None),
        P(("lon", "lat")),
        P(("lon", "lat")),
        P(("lon", "lat")),
    )
    out_specs = (P(("lon", "lat"), None), P())
    return jax.shard_map(
        on_device, mesh=mesh, in_specs=in_specs, out_specs=out_specs, check_vma=False
    )
```

```python
import jax
import jax.numpy as jnp
from jax import lax
from jax.experimental import pallas as pl
from jax.experimental.pallas import tpu as pltpu
from jax.sharding import PartitionSpec as P

STEPS = 4
BANDS, COLS, LEVS, PROBES = 12, 36, 47, 64
HALO = STEPS
TALL = BANDS + 2 * HALO
WIDE = COLS + 2 * HALO
LEVP = 48
TILES = LEVP // 8
COLP = 40
BLOCK = 8
LAT_ROWS = 3 * (HALO // 2) * COLP
LON_BANDS = TALL // 2
HALF = COLS // 2
SPILL = 2
PAIRS = SPILL + HALF
SLOTS = 1024
FIELD_ROWS = TALL * HALF * LEVP
ZERO_ROW = FIELD_ROWS
F32 = jnp.float32
HIGHEST = lax.Precision.HIGHEST
MIB = 1024 * 1024


def params(mib=12):
    return pltpu.CompilerParams(vmem_limit_bytes=mib * MIB)


def whole(space=pltpu.VMEM):
    return pl.BlockSpec(memory_space=space)


def swap(x, axis, apart, wrap=False):
    size = lax.axis_size(axis)
    partner = [((i + 1) ^ 1) - 1 if apart else i ^ 1 for i in range(size)]
    if wrap:
        partner = [j % size for j in partner]
    return lax.ppermute(x, axis, [(i, j) for i, j in enumerate(partner) if 0 <= j < size])


def all_sum(x):
    lats = lax.axis_size("lat")
    size = lats * lax.axis_size("lon")
    for bits in ((2, 4), (2 * lats, 4 * lats), (lats, 8), (1,)):
        masks = [bits[0]] if len(bits) == 1 else [bits[0], bits[1], bits[0] | bits[1]]
        terms = [lax.ppermute(x, ("lon", "lat"), [(i, i ^ m) for i in range(size)]) for m in masks]
        for term in terms:
            x = x + term
    return x


def north_far(odd):
    return odd[0] & 1


def near_west(odd):
    return odd[0] >> 1


def lat_at(which, band):
    return (which * (HALO // 2) + band % (HALO // 2)) * COLP, 64 * (band // (HALO // 2))


def lon_at(band):
    place = band % LON_BANDS
    return place // 2, HALO * (place % 2), 64 * (band // LON_BANDS)


def pack_lat_kernel(odd, u, v, mix, cells, to_far, to_near, to_west, to_east):
    far = north_far(odd) * (BANDS - HALO)
    near = BANDS - HALO - far
    for which, ref in enumerate((u, v, mix)):
        for band in range(HALO):
            row, lane = lat_at(which, band)
            to_far[row : row + COLS, lane : lane + LEVS] = ref[far + band]
            to_near[row : row + COLS, lane : lane + LEVS] = ref[near + band]
        for band in range(BANDS):
            tile, row, lane = lon_at(band + HALO)
            for dst, col in ((to_west, 0), (to_east, COLS - HALO)):
                dst[which, tile, row : row + HALO, lane : lane + LEVS] = ref[band, col : col + HALO]
    for dst in (to_far, to_near):
        dst[LAT_ROWS:] = cells[...].astype(F32)


def pack_lat(odd, u, v, mix, cells):
    lat = jax.ShapeDtypeStruct((LAT_ROWS + 8, 128), F32)
    lon = jax.ShapeDtypeStruct((3, LON_BANDS // 2, 8, 128), F32)
    return pl.pallas_call(
        pack_lat_kernel,
        in_specs=[whole(pltpu.SMEM)] + [whole()] * 4,
        out_specs=[whole()] * 4,
        out_shape=[lat, lat, lon, lon],
        compiler_params=params(62),
        name="pack_lat",
    )(odd, u, v, mix, cells.reshape(8, 128))


def pack_lon_kernel(odd, west, east, far, near, to_far, to_near, edge_west, edge_east):
    far_north, west_near = north_far(odd) == 1, near_west(odd) == 1
    for src, dst, col in ((west, edge_west, 0), (east, edge_east, COLS - HALO)):
        dst[...] = src[...]
        for which in range(3):
            for edge in range(HALO):
                row, lane = lat_at(which, edge)
                ours = (slice(row + col, row + col + HALO), slice(lane, lane + LEVS))
                one, two = far[ours], near[ours]
                for rows, band in (
                    (jnp.where(far_north, two, one), edge),
                    (jnp.where(far_north, one, two), HALO + BANDS + edge),
                ):
                    tile, at, first = lon_at(band)
                    dst[which, tile, at : at + HALO, first : first + LEVS] = rows
    one, two = edge_west[...], edge_east[...]
    to_near[...] = jnp.where(west_near, one, two)
    to_far[...] = jnp.where(west_near, two, one)


def pack_lon(odd, west, east, far, near):
    out = jax.ShapeDtypeStruct(west.shape, F32)
    return pl.pallas_call(
        pack_lon_kernel,
        in_specs=[whole(pltpu.SMEM)] + [whole()] * 4,
        out_specs=[whole()] * 2,
        out_shape=[out, out],
        scratch_shapes=[pltpu.VMEM(west.shape, F32)] * 2,
        compiler_params=params(),
        name="pack_lon",
    )(odd, west, east, far, near)


def turn(dst, at, rows, flat, last_level):
    flat[0:LEVS, HALO : HALO + COLS] = rows.T
    if last_level:
        flat[LEVS - 1 : LEVS] = jnp.zeros((1, 128), F32)
    for tile in range(TILES):
        dst[at + (slice(8 * tile, 8 * tile + 8),)] = flat[pl.ds(tile, 8, stride=TILES)]


def two_terms(x, lane):
    high = x.astype(jnp.bfloat16).astype(F32)
    return jnp.where(lane < 64, high, x - high)


def level_tile(ref, at, tile):
    if tile < TILES - 1:
        return ref[at + (pl.ds(tile, 8, stride=TILES),)]
    part = ref[at + (pl.ds(tile, 7, stride=TILES),)]
    return jnp.concatenate([part, jnp.zeros((1, PROBES), F32)], axis=0)


def edges_kernel(odd, far, near, flux, u, v, mix, to_far, to_near, gains, coef, *flats):
    for dst, src, west in ((to_far, far, 1 - near_west(odd)), (to_near, near, near_west(odd))):
        first = (1 - west) * (COLS - HALO)

        def pack(at, carry):
            for band in (2 * at, 2 * at + 1):
                for k in range(2):
                    pair = jnp.concatenate([src[band, k], src[band, k + 2]], axis=1)
                    dst[band, k, 0:LEVS] = pair
                    col = first + k
                    gain = [flux[band, pl.ds(col, 1)], flux[band, pl.ds(col + 2, 1)]]
                    dst[band, k, LEVS:LEVP] = jnp.concatenate(gain, axis=1)
            return carry

        lax.fori_loop(0, BANDS // 2, pack, 0)
    gains[:, :, 0:PROBES] = flux[:, :HALF]
    gains[:, :, PROBES:] = flux[:, HALF:]
    for flat in flats:
        flat[...] = jnp.zeros((LEVP, 128), F32)
    for which, ref in enumerate((u, v, mix)):
        for band in range(BANDS):
            turn(coef, (which, band), ref[band], flats[band % 4], which == 2)
    split_all(coef, BANDS)


def split_all(coef, bands):
    lane = lax.broadcasted_iota(jnp.int32, (LEVP, 128), 1)

    def split(at, carry):
        for which in range(3):
            for k in range(4):
                x = coef[which, at * 4 + k]
                coef[which, at * 4 + k] = two_terms(x + pltpu.roll(x, 64, 1), lane)
        return carry

    lax.fori_loop(0, bands // 4, split, 0)


def pack_edges(odd, conc, flux, u, v, mix):
    out = jax.ShapeDtypeStruct((BANDS, 2, LEVP, 128), F32)
    last = COLS // HALO - 1
    shape = (BANDS, HALO, LEVS, PROBES)
    return pl.pallas_call(
        edges_kernel,
        grid_spec=pltpu.PrefetchScalarGridSpec(
            num_scalar_prefetch=1,
            grid=(1,),
            in_specs=[
                pl.BlockSpec(shape, lambda i, odd: (0, last * near_west(odd), 0, 0)),
                pl.BlockSpec(shape, lambda i, odd: (0, last * (1 - near_west(odd)), 0, 0)),
            ]
            + [whole()] * 4,
            out_specs=[whole()] * 4,
            scratch_shapes=[pltpu.VMEM((LEVP, 128), F32)] * 4,
        ),
        out_shape=[
            out,
            out,
            jax.ShapeDtypeStruct((BANDS, HALF, 128), F32),
            jax.ShapeDtypeStruct((3, BANDS, LEVP, 128), F32),
        ],
        compiler_params=params(62),
        name="pack_edges",
    )(odd, conc, conc, flux, u, v, mix)


def row_code(cells, shift):
    rest = ((cells.astype(F32) + 0.5) * (1.0 / LEVS)).astype(jnp.int32)
    level = cells - rest * LEVS
    line = ((rest.astype(F32) + 0.5) * (1.0 / COLS)).astype(jnp.int32)
    col = rest - line * COLS
    group = ((level.astype(F32) + 0.5) * (1.0 / TILES)).astype(jnp.int32)
    band = line + HALO + shift
    held = (band >= 0) & (band < TALL)
    upper = (col >= HALF).astype(jnp.int32)
    row = (band * HALF + col - HALF * upper) * LEVP + (level - group * TILES) * 8 + group
    later = lax.broadcasted_iota(jnp.int32, cells.shape, 0) * 128 >= SLOTS // 2
    cross = (upper == 1) != later
    return jnp.where(held, row, ZERO_ROW), cross.astype(F32)


def margins_kernel(odd, far, near, cells, coef, codes, turned, *flats):
    north = north_far(odd) * 2 - 1
    places = (
        (cells[...], 0),
        (far[LAT_ROWS:].astype(jnp.int32), BANDS * north),
        (near[LAT_ROWS:].astype(jnp.int32), -BANDS * north),
    )
    lower = lax.broadcasted_iota(jnp.int32, (128, 128), 1) < PROBES
    for group, (at, shift) in enumerate(places):
        row, cross = row_code(at, shift)
        codes[8 * group : 8 * group + 8] = row
        column = jnp.concatenate([cross, jnp.zeros((120, 128), F32)], axis=0).T
        for k in range(4):
            low = jnp.broadcast_to(column[:, k : k + 1], (128, 128))
            up = jnp.broadcast_to(column[:, k + 4 : k + 5], (128, 128))
            turned[group, 128 * k : 128 * k + 128] = jnp.where(lower, low, up)
    for flat in flats:
        flat[...] = jnp.zeros((LEVP, 128), F32)
    far_at = north_far(odd) * HALO
    near_at = HALO - far_at
    for which in range(3):
        for band in range(HALO):
            row, lane = lat_at(which, band)
            for k, (first, src) in enumerate(((far_at, far), (near_at, near))):
                rows = src[row : row + COLS, lane : lane + LEVS]
                turn(coef, (which, first + band), rows, flats[band % 2 * 2 + k], which == 2)
    split_all(coef, 2 * HALO)


def margins(odd, far, near, cells):
    return pl.pallas_call(
        margins_kernel,
        in_specs=[whole(pltpu.SMEM)] + [whole()] * 3,
        out_specs=[whole()] * 3,
        out_shape=[
            jax.ShapeDtypeStruct((3, 2 * HALO, LEVP, 128), F32),
            jax.ShapeDtypeStruct((24, 128), jnp.int32),
            jax.ShapeDtypeStruct((3, SLOTS // 2, 128), F32),
        ],
        scratch_shapes=[pltpu.VMEM((LEVP, 128), F32)] * 4,
        compiler_params=params(62),
        name="margins",
    )(odd, far, near, cells.reshape(8, 128))


def join_coef(odd, split, own, beyond, far, near, sides, flat):
    span = 5 * HALO
    lane = lax.broadcasted_iota(jnp.int32, (8, 128), 1)
    west_near = near_west(odd) == 1
    flat[...] = jnp.zeros((LEVP, 128), F32)
    for which in range(3):
        one, two = far[which].reshape(-1, 128), near[which].reshape(-1, 128)
        west = jnp.where(west_near, two, one).T
        east = jnp.where(west_near, one, two).T
        for group in range(4):
            levels = slice(64 * (group // 2), 64 * (group // 2) + LEVS)
            cols = slice(span * (group % 2), span * (group % 2) + span)
            for at, src in ((0, west), (HALO + COLS, east)):
                flat[0:LEVS, at : at + span] = src[levels, cols]
            if which == 2:
                flat[LEVS - 1 : LEVS] = jnp.zeros((1, 128), F32)
            for tile in range(TILES):
                x = flat[pl.ds(tile, 8, stride=TILES)]
                x = x + pltpu.roll(x, 64, 1)
                sides[which, group, 8 * tile : 8 * tile + 8] = two_terms(x, lane)
    column = lax.broadcasted_iota(jnp.int32, (LEVP, 128), 1) & 63
    margin = (column < HALO) | ((column >= HALO + COLS) & (column < WIDE))

    def join(band, ref, at):
        group = lax.div(band, 5)
        rows = pl.ds(pl.multiple_of(band * LEVP, LEVP), LEVP)
        for which in range(3):
            shift = lax.rem(128 - HALO * lax.rem(band, 5), 128)
            beside = pltpu.roll(sides[which, group], shift, 1)
            x = jnp.where(margin, beside, ref[which, at])
            split[which, rows] = x.astype(jnp.bfloat16)

    def inner(at, carry):
        for k in range(4):
            join(HALO + 4 * at + k, own, 4 * at + k)
        return carry

    def outer(at, carry):
        for k in range(HALO):
            join(at * (HALO + BANDS) + k, beyond, at * HALO + k)
        return carry

    lax.fori_loop(0, BANDS // 4, inner, 0)
    lax.fori_loop(0, 2, outer, 0)


def selector(tile, low, high, high_sign=1.0):
    shape = (128, 256)
    row = lax.broadcasted_iota(jnp.int32, shape, 0) & 63
    col = lax.broadcasted_iota(jnp.int32, shape, 1)
    pair = 2 * tile + (col >> 7)
    upper = ((col >> 6) & 1) == 1
    weight = jnp.where(upper, high_sign, 1.0)
    return jnp.where(row == jnp.where(upper, high(pair), low(pair)), weight, 0.0).astype(jnp.bfloat16)


def spread(ref, split, chosen, tile, first=0, count=TALL):
    out = jnp.dot(
        split[first * LEVP : (first + count) * LEVP], chosen, preferred_element_type=F32
    )
    out = out.reshape(count, 1, LEVP, 256)
    ref[first : first + count, pl.ds(2 * tile, 1)] = out[..., :128]
    ref[first : first + count, pl.ds(2 * tile + 1, 1)] = out[..., 128:]


def face_flux(speed, behind, ahead):
    return speed * jnp.where(speed > 0.0, behind, ahead)


def mix_levels(dst, line, mixing, at, pair):
    here = [line[pair, 8 * t : 8 * t + 8] for t in range(TILES)]
    above = here[1:] + [pltpu.roll(here[0], 7, 0)]
    moved = [
        mixing[at, pair, 8 * t : 8 * t + 8] * (above[t] - here[t]) for t in range(TILES)
    ]
    below = [pltpu.roll(moved[-1], 1, 0)] + moved[:-1]
    for t in range(TILES):
        dst[at, pair, 8 * t : 8 * t + 8] = here[t] + (moved[t] - below[t])


def two_rows(band, pairs, c, u, v, m, fs, line0, line1, closed=False):
    first, north = pairs[0], jnp.minimum(band + 2, TALL - 1)
    here0, here1 = c[band, first], c[band + 1, first]
    west0 = face_flux(u[band, first], c[band, first - 1], here0)
    west1 = face_flux(u[band + 1, first], c[band + 1, first - 1], here1)
    for pair in pairs:
        middle = face_flux(v[band + 1, pair], here0, here1)
        top = face_flux(v[north, pair], here1, c[north, pair])
        net0, net1 = here0 + west0, here1 + west1
        if not (closed and pair == pairs[-1]):
            ahead0, ahead1 = c[band, pair + 1], c[band + 1, pair + 1]
            west0 = face_flux(u[band, pair + 1], here0, ahead0)
            west1 = face_flux(u[band + 1, pair + 1], here1, ahead1)
            net0, net1 = net0 - west0, net1 - west1
            here0, here1 = ahead0, ahead1
        line0[pair] = net0 + (fs[pair] - middle)
        line1[pair] = net1 + (middle - top)
        fs[pair] = top
    for pair in pairs:
        mix_levels(c, line0, m, band, pair)
        mix_levels(c, line1, m, band + 1, pair)


def block_rows(step, band, c, u, v, m, fs, line0, line1, last):
    north = jnp.minimum(band + 2, TALL - 1)
    lower = lax.broadcasted_iota(jnp.int32, (LEVP, 128), 1) < PROBES
    begin, end = SPILL, PAIRS - 1
    fluxes, spills = [], []
    for k in range(2):
        at = band + k
        far, near, head, tail = (c[at, place] for place in (0, 1, begin, end))
        into = face_flux(u[at, begin], jnp.where(lower, near, pltpu.roll(tail, PROBES, 1)), head)
        out = face_flux(u[at, 1], tail, jnp.where(lower, pltpu.roll(head, PROBES, 1), near))
        last[k] = out
        fluxes.append(into)
        if step < STEPS:
            outer = face_flux(
                u[at, 0], jnp.where(lower, far, near), jnp.where(lower, near, far)
            )
            net = {1: jnp.where(lower, outer - into, out - outer)}
            if step == 2:
                net[0] = jnp.where(lower, -outer, outer)
            spills.append(net)

    def advance(place, here0, here1, net0, net1):
        middle = face_flux(v[band + 1, place], here0, here1)
        top = face_flux(v[north, place], here1, c[north, place])
        line0[place] = net0 + (fs[place] - middle)
        line1[place] = net1 + (middle - top)
        fs[place] = top

    places = list(range(begin, PAIRS))
    if step < STEPS:
        for place in spills[0]:
            here0, here1 = c[band, place], c[band + 1, place]
            advance(place, here0, here1, here0 + spills[0][place], here1 + spills[1][place])
            places.append(place)
    here0, here1 = c[band, begin], c[band + 1, begin]
    west0, west1 = fluxes
    for place in range(begin, PAIRS):
        net0, net1 = here0 + west0, here1 + west1
        old0, old1 = here0, here1
        if place < end:
            here0, here1 = c[band, place + 1], c[band + 1, place + 1]
            west0 = face_flux(u[band, place + 1], old0, here0)
            west1 = face_flux(u[band + 1, place + 1], old1, here1)
        else:
            west0, west1 = last[0], last[1]
        advance(place, old0, old1, net0 - west0, net1 - west1)
    for place in places:
        mix_levels(c, line0, m, band, place)
        mix_levels(c, line1, m, band + 1, place)


def transport_kernel(
    odd, conc, flux, own, beyond, far, near, out, split,
    c, u, v, m, fs, line0, line1, last, sides, flat, stage, in_sem, out_sem,
):
    def fetch(band):
        return pltpu.make_async_copy(conc.at[band], stage.at[band], in_sem.at[band])

    for band in range(BANDS):
        fetch(band).start()
    join_coef(odd, split, own, beyond, far, near, sides, flat)

    def expand(tile):
        def cells(low, shift):
            outside = jnp.where(low == 1, HALO - 1 if not shift else HALO + COLS, HALO - 2 if not shift else HALO + COLS + 1)
            return jnp.where(low >= SPILL, low + HALO - SPILL + shift, outside)

        def faces(low, shift):
            outside = jnp.where(low == 1, HALO + HALF + shift, HALO - 1 if not shift else HALO + COLS + 1)
            return jnp.where(low >= SPILL, low + HALO - SPILL + shift, outside)

        at_faces = selector(tile, lambda p: faces(p, 0), lambda p: faces(p, HALF))
        at_cells = selector(tile, lambda p: cells(p, 0), lambda p: cells(p, HALF))
        half = TALL // 2
        for which, (ref, chosen) in enumerate(((u, at_faces), (v, at_cells), (m, at_cells))):
            for first in (0, half):
                yield lambda: spread(ref, split.at[which], chosen, tile, first, half)

    def load(band, pieces):
        fetch(band).wait()
        for pair in range(HALF):
            for t in range(TILES):
                both = [level_tile(stage, (band, col), t) for col in (pair, pair + HALF)]
                both = jnp.concatenate(both, axis=1)
                c[band + HALO, SPILL + pair, 8 * t : 8 * t + 8] = both
            if pieces is not None and pair % 3 == 2:
                next(pieces)()
        c[band + HALO, 0:SPILL] = jnp.zeros((SPILL, LEVP, 128), F32)

    def load_and_expand(band, carry):
        load(band, expand(band))
        return carry

    def load_only(band, carry):
        load(band, None)
        return carry

    lax.fori_loop(0, PAIRS // 2, load_and_expand, 0)
    lax.fori_loop(PAIRS // 2, BANDS, load_only, 0)

    def clear(band, carry):
        c[band] = jnp.zeros((PAIRS, LEVP, 128), F32)
        c[band + HALO + BANDS] = jnp.zeros((PAIRS, LEVP, 128), F32)
        return carry

    lax.fori_loop(0, HALO, clear, 0)

    def save(band):
        return pltpu.make_async_copy(c.at[band, pl.ds(SPILL, HALF)], out.at[band], out_sem.at[band])

    for step in range(1, STEPS + 1):

        def gain(at, carry):
            for band in range(3):
                for pair in range(HALF):
                    spot = 3 * at + band + HALO, SPILL + pair, slice(0, 1)
                    c[spot] = c[spot] + flux[3 * at + band, pair : pair + 1]
            return carry

        lax.fori_loop(0, BANDS // 3, gain, 0)
        fs[...] = jnp.zeros((PAIRS, LEVP, 128), F32)

        def rows(at, carry):
            band = HALO - step + 2 * at
            block_rows(step, band, c, u, v, m, fs, line0, line1, last)
            if step == STEPS:
                save(band).start()
                save(band + 1).start()
            return carry

        lax.fori_loop(0, (BANDS + 2 * step) // 2, rows, 0)

    def drain(band, carry):
        save(band).wait()
        return carry

    lax.fori_loop(0, TALL, drain, 0)


def transport(odd, conc, flux, own, beyond, far, near):
    field = pltpu.VMEM((TALL, PAIRS, LEVP, 128), F32)
    line = pltpu.VMEM((PAIRS, LEVP, 128), F32)
    return pl.pallas_call(
        transport_kernel,
        in_specs=[whole(pltpu.SMEM), whole(pl.ANY)] + [whole()] * 5,
        out_specs=[whole(pl.ANY), whole()],
        out_shape=[
            jax.ShapeDtypeStruct((TALL, HALF, LEVP, 128), F32),
            jax.ShapeDtypeStruct((3, TALL * LEVP, 128), jnp.bfloat16),
        ],
        scratch_shapes=[
            field,
            field,
            field,
            field,
            line,
            line,
            line,
            pltpu.VMEM((2, LEVP, 128), F32),
            pltpu.VMEM((3, 4, LEVP, 128), F32),
            pltpu.VMEM((LEVP, 128), F32),
            pltpu.VMEM((BANDS, COLS, LEVS, PROBES), F32),
            pltpu.SemaphoreType.DMA((BANDS,)),
            pltpu.SemaphoreType.DMA((TALL,)),
        ],
        compiler_params=params(62),
        name="transport",
    )(odd, conc, flux, own, beyond, far, near)


def strips_kernel(
    odd, codes, turned, edge_far, edge_near, split, field, own, far, near,
    c, u, v, m, fs, line0, line1, gain, full, got0, got1, got2, sem,
):
    fetch = pltpu.make_async_copy(field, full.at[pl.ds(0, FIELD_ROWS)], sem)
    fetch.start()

    lower = lax.broadcasted_iota(jnp.int32, (LEVP, 128), 1) < PROBES
    inside = lax.broadcasted_iota(jnp.int32, (8, 128), 0) < 7
    low_lanes = lax.broadcasted_iota(jnp.int32, (8, 128), 1) < PROBES
    west_near = near_west(odd) == 1

    def place(band):
        for k in range(2):
            for tile in range(TILES):
                rows = pl.ds(tile, 8, stride=TILES)
                one, two = edge_far[band, k, rows], edge_near[band, k, rows]
                three, four = edge_far[band, 1 - k, rows], edge_near[band, 1 - k, rows]
                left, right = jnp.where(west_near, two, one), jnp.where(west_near, three, four)
                outer = jnp.where(low_lanes, left, right)
                inner = pltpu.roll(jnp.where(low_lanes, right, left), PROBES, 1)
                for at, value in ((k, outer), (k + 2, inner)):
                    if tile == TILES - 1:
                        gain[band, at, 0:1] = value[7:8]
                        value = jnp.where(inside, value, 0.0)
                    c[band + HALO, at, 8 * tile : 8 * tile + 8] = value

    def expand(tile, carry):
        faces = selector(tile, lambda k: k, lambda k: WIDE - k, -1.0)
        cells = selector(tile, lambda k: k, lambda k: WIDE - 1 - k)
        none = jnp.zeros((HALO, LEVP, 128), F32)
        for which, ref in enumerate((u, v, m)):
            spread(ref, split.at[which], cells if which else faces, tile)
            place(3 * tile + which)
        for k in range(TALL // 4):
            c[tile * (TALL // 4) + k, HALO:] = none
        c[tile, 0:HALO] = none
        c[tile + HALO + BANDS, 0:HALO] = none
        return carry

    lax.fori_loop(0, HALO, expand, 0)

    full[ZERO_ROW : ZERO_ROW + 8] = jnp.zeros((8, 128), F32)

    for step in range(1, STEPS + 1):
        region = range(step, step + HALO)

        def add(band, carry):
            for k in range(step - 1, HALO):
                c[band + HALO, k, 0:1] = c[band + HALO, k, 0:1] + gain[band, k, 0:1]
            return carry

        lax.fori_loop(0, BANDS, add, 0)
        for k in region:
            fs[k] = jnp.zeros((LEVP, 128), F32)

        def rows(at, carry):
            two_rows(HALO - step + 2 * at, region, c, u, v, m, fs, line0, line1, closed=True)
            return carry

        lax.fori_loop(0, (BANDS + 2 * step) // 2, rows, 0)

    fetch.wait()

    def merge(band, carry):
        base = band * (HALF * LEVP)
        spots, sums = [], []
        for k in range(HALO):
            share = c[band, HALO + k]
            for pair, keep in ((k, lower), (HALF - 1 - k, ~lower)):
                rows = pl.ds(pl.multiple_of(base + pair * LEVP, LEVP), LEVP)
                spots.append(rows)
                sums.append(full[rows] + jnp.where(keep, share, 0.0))
        for rows, value in zip(spots, sums):
            full[rows] = value
        return carry

    lax.fori_loop(0, TALL, merge, 0)

    half = SLOTS // 2
    left_lanes = lax.broadcasted_iota(jnp.int32, (8, 128), 1) < PROBES
    for group, (out, buffer) in enumerate(((own, got0), (far, got1), (near, got2))):

        def pick(at, carry):
            first = pl.multiple_of(at * 128, 128)
            rows = buffer.at[pl.ds(first, 128)], buffer.at[pl.ds(first + half, 128)]
            done = out.at[pl.ds(first, 128)]
            cross = turned.at[group, pl.ds(first, 128)]
            for tile in range(16):
                tiles = slice(8 * tile, 8 * tile + 8)
                for part in range(2):
                    for k in range(8 * tile, 8 * tile + 8):
                        place = codes[group * 8 + at + 4 * part, k]
                        rows[part][k : k + 1] = full[pl.ds(place, 1)]
                one, two = rows[0][tiles], rows[1][tiles]
                straight = jnp.where(left_lanes, one, two)
                crossed = pltpu.roll(jnp.where(left_lanes, two, one), PROBES, 1)
                done[tiles] = jnp.where(cross[tiles] > 0.5, crossed, straight)
            return carry

        lax.fori_loop(0, half // 128, pick, 0)


def strips(odd, codes, turned, far, near, split, field):
    strip = pltpu.VMEM((TALL, 2 * HALO, LEVP, 128), F32)
    line = pltpu.VMEM((2 * HALO, LEVP, 128), F32)
    buffer = pltpu.VMEM((SLOTS, 128), F32)
    return pl.pallas_call(
        strips_kernel,
        in_specs=[whole(pltpu.SMEM), whole(pltpu.SMEM), whole(), whole(), whole(), whole(), whole(pl.ANY)],
        out_specs=[whole()] * 3,
        out_shape=[jax.ShapeDtypeStruct((SLOTS // 2, 128), F32)] * 3,
        scratch_shapes=[
            strip,
            strip,
            strip,
            strip,
            line,
            line,
            line,
            pltpu.VMEM((BANDS, HALO, 8, 128), F32),
            pltpu.VMEM((FIELD_ROWS + 8, 128), F32),
            buffer,
            buffer,
            buffer,
            pltpu.SemaphoreType.DMA,
        ],
        compiler_params=params(56),
        name="strips",
    )(odd, codes, turned, far, near, split, field)


def gram_kernel(own, far, near, weight, images, gram):
    rows = own[...] + (far[...] + near[...]) * weight[...]
    images[...] = rows
    both = lax.dot_general(
        rows, rows, (((0,), (0,)), ((), ())), precision=HIGHEST, preferred_element_type=F32
    )
    total = both[:PROBES, :PROBES] + both[PROBES:, PROBES:]
    gram[:, 0:PROBES] = total[: PROBES // 2]
    gram[:, PROBES:] = total[PROBES // 2 :]


def gram_of(own, far, near, weight):
    return pl.pallas_call(
        gram_kernel,
        in_specs=[whole()] * 4,
        out_specs=[whole()] * 2,
        out_shape=[
            jax.ShapeDtypeStruct((SLOTS // 2, 128), F32),
            jax.ShapeDtypeStruct((PROBES // 2, 128), F32),
        ],
        compiler_params=params(),
        name="gram",
    )(own, far, near, weight)


def factor_kernel(root, gram, images, basis_t, factor, work, pivots):
    sublane = lax.broadcasted_iota(jnp.int32, (8, 128), 0)
    half = PROBES // 2
    work[0:half, 0:PROBES] = gram[:, 0:PROBES]
    work[half:, 0:PROBES] = gram[:, PROBES:]
    diagonal = (
        lax.broadcasted_iota(jnp.int32, (PROBES, PROBES), 0)
        == lax.broadcasted_iota(jnp.int32, (PROBES, PROBES), 1)
    )
    work[:, PROBES:] = diagonal.astype(F32)
    tiles = [work[8 * t : 8 * t + 8] for t in range(PROBES // 8)]
    for first in range(0, PROBES, BLOCK):
        top = first // 8
        live = range(top, PROBES // 8)
        column = {
            (j, t): jnp.broadcast_to(tiles[t][:, first + j : first + j + 1], (8, 128))
            for j in range(BLOCK)
            for t in live
        }
        for j in range(BLOCK):
            at = first + j
            pick = lambda tile, n: jnp.broadcast_to(tile[n % 8 : n % 8 + 1], (8, 128))
            inverse = 1.0 / pick(column[j, top], at)
            pivots[at : at + 1] = column[j, top][at % 8 : at % 8 + 1]
            pivot = pick(tiles[top], at) * inverse
            later = [pick(column[j, top], first + i) * inverse for i in range(j + 1, BLOCK)]
            for t in live:
                share = column[j, t]
                if t == top:
                    share = jnp.where(sublane > at % 8, share, 0.0)
                tiles[t] = tiles[t] - share * pivot
                for i in range(j + 1, BLOCK):
                    column[i, t] = column[i, t] - share * later[i - j - 1]
    for t in range(PROBES // 8):
        rows = slice(8 * t, 8 * t + 8)
        work[rows] = tiles[t] * (1.0 / jnp.sqrt(pivots[rows]))
    both = work[...]
    row = lax.broadcasted_iota(jnp.int32, (PROBES, PROBES), 0)
    col = lax.broadcasted_iota(jnp.int32, (PROBES, PROBES), 1)
    factor[...] = jnp.where(col >= row, both[:, :PROBES], 0.0) * (1.0 / root)
    inverse_t = jnp.where(col <= row, both[:, PROBES:], 0.0) * root
    zero = jnp.zeros((PROBES, PROBES), F32)
    twice = jnp.concatenate(
        [
            jnp.concatenate([inverse_t, zero], axis=1),
            jnp.concatenate([zero, inverse_t], axis=1),
        ],
        axis=0,
    )
    basis = lax.dot_general(
        twice, images[...], (((1,), (1,)), ((), ())), precision=HIGHEST, preferred_element_type=F32
    )
    basis_t[:, 0 : SLOTS // 2] = basis[:PROBES]
    basis_t[:, SLOTS // 2 :] = basis[PROBES:]


def factor_of(gram, images, root):
    return pl.pallas_call(
        lambda *refs: factor_kernel(root, *refs),
        in_specs=[whole()] * 2,
        out_specs=[whole()] * 2,
        out_shape=[
            jax.ShapeDtypeStruct((PROBES, SLOTS), F32),
            jax.ShapeDtypeStruct((PROBES, PROBES), F32),
        ],
        scratch_shapes=[pltpu.VMEM((PROBES, 128), F32)] * 2,
        compiler_params=params(),
        name="factor",
    )(gram, images)


def on_device(
    flux_probes, conc_start, u_courant, v_courant, vert_mix, obs_cell, obs_weight, obs_count
):
    odd = (lax.axis_index("lat") % 2 + 2 * (lax.axis_index("lon") % 2)).astype(jnp.int32).reshape(1)
    to_far, to_near, own_west, own_east = pack_lat(odd, u_courant, v_courant, vert_mix, obs_cell)
    from_far = swap(to_far, "lat", True)
    from_near = swap(to_near, "lat", False)
    *edges, gains, own = pack_edges(
        odd, conc_start, flux_probes, u_courant, v_courant, vert_mix
    )
    own_west, own_east, *edges = lax.optimization_barrier((own_west, own_east, *edges))
    lon_far, lon_near = pack_lon(odd, own_west, own_east, from_far, from_near)
    lon_far = swap(lon_far, "lon", True, wrap=True)
    lon_near = swap(lon_near, "lon", False)
    beyond, codes, turned = margins(odd, from_far, from_near, obs_cell)
    edge_far, edge_near, beyond, lon_far, lon_near = lax.optimization_barrier(
        (*edges, beyond, lon_far, lon_near)
    )
    edge_far = swap(edge_far, "lon", True, wrap=True)
    edge_near = swap(edge_near, "lon", False)
    field, split = transport(odd, conc_start, gains, own, beyond, lon_far, lon_near)
    rows, for_far, for_near = strips(
        odd, codes, turned, edge_far, edge_near, split, field.reshape(FIELD_ROWS, 128)
    )
    far_rows = swap(for_far, "lat", True)
    near_rows = swap(for_near, "lat", False)
    live = jnp.arange(SLOTS, dtype=jnp.int32) < obs_count[0]
    scale = jnp.where(live, obs_weight, 0.0)
    lanes = (SLOTS // 2, PROBES)
    weight = jnp.concatenate(
        [
            jnp.broadcast_to(scale[: SLOTS // 2, None], lanes),
            jnp.broadcast_to(scale[SLOTS // 2 :, None], lanes),
        ],
        axis=1,
    )
    images, gram = gram_of(rows * weight, far_rows, near_rows, weight)
    gram = all_sum(gram)
    total_rows = SLOTS * lax.axis_size("lon") * lax.axis_size("lat")
    basis_t, factor = factor_of(gram, images, float(total_rows) ** 0.5)
    return basis_t.T, factor


def solution(mesh):
    in_specs = (
        P("lat", "lon", None),
        P("lat", "lon", None, None),
        P("lat", "lon", None),
        P("lat", "lon", None),
        P("lat", "lon", None),
        P(("lon", "lat")),
        P(("lon", "lat")),
        P(("lon", "lat")),
    )
    out_specs = (P(("lon", "lat"), None), P())
    return jax.shard_map(
        on_device, mesh=mesh, in_specs=in_specs, out_specs=out_specs, check_vma=False
    )
```
